32 devices in a mesh: dp: 4 (over z), ctx: 8 (over y, x, core).
Axes of the slice: x: 2, y: 2, z: 4, core: 2. Of those that a mesh axis runs over, the one named last changes fastest.
Arguments:
- inputs: bfloat16 [8, 1024, 2048], P('dp', 'ctx'), may hold values from -6 to 6
- lengths: int32 [8], P('dp'), may hold values from 64 to 1024, as said below
- attention_gain: bfloat16 [2048], replicated, may hold values from 0.25 to 1.75
- query_weight: bfloat16 [2048, 2048], P(('dp', 'ctx')), may hold values from -0.125 to 0.125
- key_matrix: bfloat16 [2048, 512], P(('dp', 'ctx')), may hold values from -0.125 to 0.125
- value_matrix: bfloat16 [2048, 512], P(('dp', 'ctx')), may hold values from -0.125 to 0.125
- out_weight: bfloat16 [2048, 2048], P(('dp', 'ctx')), may hold values from -0.75 to 0.75
- query_gain: bfloat16 [64], replicated, may hold values from 0.25 to 1.75
- key_gain: bfloat16 [64], replicated, may hold values from 0.25 to 1.75
- feedforward_gain: bfloat16 [2048], replicated, may hold values from 0.25 to 1.75
- gate_weight: bfloat16 [2048, 8192], P(('dp', 'ctx')), may hold values from -0.125 to 0.125
- up_weight: bfloat16 [2048, 8192], P(('dp', 'ctx')), may hold values from -0.125 to 0.125
- down_weight: bfloat16 [2048, 8192], P(('dp', 'ctx')), may hold values from -0.0625 to 0.0625
- cotangent: bfloat16 [8, 1024, 2048], P('dp', 'ctx'), may hold values from -6 to 6
Outputs:
- outputs: bfloat16 [8, 1024, 2048], P('dp', 'ctx')
- input_gradient: bfloat16 [8, 1024, 2048], P('dp', 'ctx')
- attention_gain_gradient: float32 [2048], replicated
- query_weight_gradient: float32 [2048, 2048], P(('dp', 'ctx'))
- key_weight_gradient: float32 [2048, 512], P(('dp', 'ctx'))
- value_weight_gradient: float32 [2048, 512], P(('dp', 'ctx'))
- out_weight_gradient: float32 [2048, 2048], P(('dp', 'ctx'))
- query_gain_gradient: float32 [64], replicated
- key_gain_gradient: float32 [64], replicated
- feedforward_gain_gradient: float32 [2048], replicated
- gate_weight_gradient: float32 [2048, 8192], P(('dp', 'ctx'))
- up_weight_gradient: float32 [2048, 8192], P(('dp', 'ctx'))
- down_weight_gradient: float32 [2048, 8192], P(('dp', 'ctx'))
The draws below stay inside these ranges and needn't reach their ends.
Inputs may be any that keep to these rules, and one draw needn't show every extreme that they name: `lengths`: in each aligned block of 2 rows one row has length 1024; some row has length 64.
All inputs are finite; a program needn't handle non-finite values.
Results may differ from the reference program's by a relative error of at most 0.02.
Values may be sent and summed in bfloat16 or wider, within the bound.
No kernel may reach another device: no remote copies, remote signals or barrier semaphores. Data moves between devices by JAX's collectives and lax.ppermute only.
A program may use at most 768 MiB of HBM per device.

```python
import jax
import jax.numpy as jnp
from jax import lax

MODEL_WIDTH = 2048
QUERY_HEADS_TOTAL = 32
KEY_VALUE_HEADS = 8
HEAD_SIZE = 64
FF = 8192
ROWS_DEV = 2
MIN_LEN = 64
ROWS = 8
ROW_SLOTS = 1024


def draw_lengths(key, part):
    key = jax.random.fold_in(key, 11)
    tail_key, offset_key, group_key = jax.random.split(key, 3)
    coarse_values = jax.random.randint(tail_key, (ROWS,), 0, 1024, dtype=jnp.int32)
    tail = coarse_values * coarse_values // 1024 * coarse_values // 1024
    drawn = MIN_LEN + (ROW_SLOTS - MIN_LEN) * tail // 1024
    offsets = jax.random.randint(offset_key, (ROWS // ROWS_DEV,), 0, ROWS_DEV, dtype=jnp.int32)
    chosen = jax.random.randint(group_key, (), 0, ROWS // ROWS_DEV, dtype=jnp.int32)
    position = jnp.arange(ROWS, dtype=jnp.int32)
    group_index = position // ROWS_DEV
    within = position % ROWS_DEV
    own_offset = jnp.take(offsets, group_index)
    full_row = within == own_offset
    short_row = (group_index == chosen) & (within == (own_offset + 1) % ROWS_DEV)
    return jnp.where(full_row, ROW_SLOTS, jnp.where(short_row, MIN_LEN, drawn)).astype(jnp.int32)


def with_spikes(entries, rng, source, target, blocks, factor):
    owner, partner = [(jnp.arange(entries.shape[dim]) // (entries.shape[dim] // blocks)).reshape([-1 if axis == dim else 1 for axis in range(entries.ndim)]) for dim in (source, target)]
    chosen = jax.random.permutation(rng, blocks)[partner]
    strong = (owner == chosen) | (owner == (partner + blocks // 2) % blocks)
    return jnp.where(strong, factor * entries, entries)


def block_levels(key, dims, cuts, least, largest):
    gain = 1.0
    for dim, parts in cuts:
        steps = jax.random.uniform(jax.random.fold_in(jax.random.fold_in(key, 6), dim), (parts,), jnp.float32, least / len(cuts), largest / len(cuts))
        gain = gain * jnp.repeat(jnp.exp(steps), dims[dim] // parts).reshape((-1,) + (1,) * (len(dims) - 1 - dim))
    return gain


def normal_values(stream_key, dims, scale, most, pieces=(), held_as=jnp.bfloat16):
    level = block_levels(stream_key, dims, pieces, -0.22, 0.18) if pieces else 1.0
    entries = jax.random.normal(stream_key, dims, jnp.float32) * scale * level
    return jnp.minimum(jnp.maximum(entries, -most), most).astype(held_as)


def gaussian_with(rng, dims, spread, bound, cuts, heavy, kind=jnp.bfloat16):
    values = spread * jax.random.normal(rng, dims, jnp.float32)
    if cuts:
        values = values * block_levels(rng, dims, cuts, -0.22, 0.18)
    return jnp.clip(with_spikes(values, jax.random.fold_in(rng, 3), *heavy), -bound, bound).astype(kind)


def setup_inputs(seed: int = 0) -> dict:
    arg_keys = jax.random.split(jax.random.key(seed), 15)
    return {
        "inputs": normal_values(arg_keys[0], (ROWS, ROW_SLOTS, MODEL_WIDTH), 1.0, 6.0, ((0, 4), (1, 8))),
        "lengths": draw_lengths(jax.random.fold_in(arg_keys[14], 71), 0),
        "attention_gain": jnp.clip(1.0 + 0.15 * jax.random.normal(arg_keys[2], (MODEL_WIDTH,), jnp.float32), 0.25, 1.75).astype(jnp.bfloat16),
        "query_weight": normal_values(arg_keys[3], (MODEL_WIDTH, QUERY_HEADS_TOTAL * HEAD_SIZE), MODEL_WIDTH ** -0.5, 0.125, ((0, 32),)),
        "key_matrix": normal_values(arg_keys[4], (MODEL_WIDTH, KEY_VALUE_HEADS * HEAD_SIZE), MODEL_WIDTH ** -0.5, 0.125, ((0, 32),)),
        "value_matrix": normal_values(arg_keys[5], (MODEL_WIDTH, KEY_VALUE_HEADS * HEAD_SIZE), MODEL_WIDTH ** -0.5, 0.125, ((0, 32),)),
        "out_weight": normal_values(arg_keys[6], (MODEL_WIDTH, QUERY_HEADS_TOTAL * HEAD_SIZE), (QUERY_HEADS_TOTAL * HEAD_SIZE // 32) ** -0.5, 0.75, ((0, 32),)),
        "query_gain": jnp.clip(1.0 + 0.15 * jax.random.normal(arg_keys[7], (HEAD_SIZE,), jnp.float32), 0.25, 1.75).astype(jnp.bfloat16),
        "key_gain": jnp.clip(1.0 + 0.15 * jax.random.normal(arg_keys[8], (HEAD_SIZE,), jnp.float32), 0.25, 1.75).astype(jnp.bfloat16),
        "feedforward_gain": jnp.clip(1.0 + 0.15 * jax.random.normal(arg_keys[9], (MODEL_WIDTH,), jnp.float32), 0.25, 1.75).astype(jnp.bfloat16),
        "gate_weight": normal_values(arg_keys[10], (MODEL_WIDTH, FF), MODEL_WIDTH ** -0.5, 0.125, ((0, 32),)),
        "up_weight": normal_values(arg_keys[11], (MODEL_WIDTH, FF), MODEL_WIDTH ** -0.5, 0.125, ((0, 32),)),
        "down_weight": normal_values(arg_keys[12], (MODEL_WIDTH, FF), FF ** -0.5, 0.0625, ((0, 32),)),
        "cotangent": gaussian_with(arg_keys[13], (ROWS, ROW_SLOTS, MODEL_WIDTH), 1.0, 6.0, ((0, 4), (1, 8)), (1, 2, 8, 2.0)),
    }


epsilon = 1e-06
highest = lax.Precision.HIGHEST

@jax.custom_vjp
def lower_precision(v):
    return lax.optimization_barrier(v.astype(jnp.bfloat16)).astype(jnp.float32)

@jax.custom_vjp
def lower_backward(v):
    return v

def low_keep(v):
    return (lower_precision(v), None)

def low_pass(kept, grad):
    return (grad,)

def back_keep(v):
    return (v, None)

def back_low(kept, grad):
    return (lower_precision(grad),)
lower_precision.defvjp(low_keep, low_pass)
lower_backward.defvjp(back_keep, back_low)

def rms_scale(value_rows):
    return lax.rsqrt(lax.optimization_barrier(jnp.mean(value_rows * value_rows, axis=-1, keepdims=True)) + epsilon)

def rotary_tables(positions, width):
    inverse = 10000.0 ** (-(jnp.arange(width // 2, dtype=jnp.float32) * 2.0) / width)
    angle_table = positions.astype(jnp.float32)[:, None] * inverse[None, :]
    return (jnp.cos(angle_table), jnp.sin(angle_table))

def rotate(value_rows, cosine, sine):
    half = value_rows.shape[-1] // 2
    first = value_rows[..., :half]
    second = value_rows[..., half:]
    return jnp.concatenate([first * cosine - second * sine, second * cosine + first * sine], axis=-1)

def matrix_product(left, right):
    return jnp.dot(left, right, precision=highest, preferred_element_type=jnp.float32)

def attend(query_rows, keys, value_rows, length):
    block_slice = min(512, ROW_SLOTS)
    item_count = ROW_SLOTS // block_slice
    group_count = QUERY_HEADS_TOTAL // KEY_VALUE_HEADS
    key_pos = jnp.arange(ROW_SLOTS, dtype=jnp.int32)
    grouped_heads = query_rows.reshape(item_count, block_slice, KEY_VALUE_HEADS, group_count, HEAD_SIZE)
    starts = jnp.arange(item_count, dtype=jnp.int32) * block_slice

    def one_block(pair):
        query_block, first = pair
        scores = lower_backward(jnp.einsum('qhgd,khd->hgqk', query_block, keys, precision=highest) * HEAD_SIZE ** (-0.5))
        query_pos = first + jnp.arange(block_slice, dtype=jnp.int32)
        allowed = (key_pos[None, :] <= query_pos[:, None]) & (key_pos[None, :] < length)
        scores = jnp.where(allowed[None, None], scores, -1e+30)
        top = lax.optimization_barrier(jnp.max(scores, axis=-1, keepdims=True))
        weights = jnp.exp(scores - top)
        probs = weights / lax.optimization_barrier(jnp.sum(weights, axis=-1, keepdims=True))
        blended = jnp.einsum('hgqk,khd->qhgd', lower_precision(probs), value_rows, precision=highest)
        return lower_precision(lower_backward(blended)).reshape(block_slice, QUERY_HEADS_TOTAL * HEAD_SIZE)
    return lax.map(jax.checkpoint(one_block), (grouped_heads, starts)).reshape(ROW_SLOTS, QUERY_HEADS_TOTAL * HEAD_SIZE)

def layer(inputs, length, attention_gain, query_weight, key_matrix, value_matrix, out_weight, query_gain, key_gain, feedforward_gain, gate_weight, up_weight, down_weight):
    normed = inputs * rms_scale(inputs)
    hidden_state = lower_precision(normed * attention_gain)
    raw_queries = lower_backward(matrix_product(hidden_state, query_weight)).reshape(ROW_SLOTS, QUERY_HEADS_TOTAL, HEAD_SIZE)
    unrotated_keys = lower_backward(matrix_product(hidden_state, key_matrix)).reshape(ROW_SLOTS, KEY_VALUE_HEADS, HEAD_SIZE)
    value_rows = lower_precision(lower_backward(matrix_product(hidden_state, value_matrix))).reshape(ROW_SLOTS, KEY_VALUE_HEADS, HEAD_SIZE)
    cosine, sine = rotary_tables(jnp.arange(ROW_SLOTS, dtype=jnp.int32), HEAD_SIZE)
    cosine = cosine[:, None, :]
    sine = sine[:, None, :]
    query_rows = lower_precision(rotate(raw_queries * rms_scale(raw_queries) * query_gain, cosine, sine))
    keys = lower_precision(rotate(unrotated_keys * rms_scale(unrotated_keys) * key_gain, cosine, sine))
    attended = attend(query_rows, keys, value_rows, length)
    mixed = inputs + lower_backward(matrix_product(attended, out_weight.T))
    normed_again = mixed * rms_scale(mixed)
    hidden_again = lower_precision(normed_again * feedforward_gain)
    gate = lower_backward(matrix_product(hidden_again, gate_weight))
    upward = lower_backward(matrix_product(hidden_again, up_weight))
    inner = lower_precision(jax.nn.silu(gate) * upward)
    return mixed + lower_backward(matrix_product(inner, down_weight.T))

def reference(inputs, lengths, attention_gain, query_weight, key_matrix, value_matrix, out_weight, query_gain, key_gain, feedforward_gain, gate_weight, up_weight, down_weight, cotangent):
    parameters = tuple((array.astype(jnp.float32) for array in (attention_gain, query_weight, key_matrix, value_matrix, out_weight, query_gain, key_gain, feedforward_gain, gate_weight, up_weight, down_weight)))

    def one_row(sums, row):
        row_inputs, row_length, row_cotangent = row

        def forward(value_rows, *weights):
            return layer(value_rows, row_length, *weights)
        result, pull = jax.vjp(forward, row_inputs.astype(jnp.float32), *parameters)
        gradients = pull(row_cotangent.astype(jnp.float32))
        sums = tuple((total + term for total, term in zip(sums, gradients[1:])))
        return (sums, (result.astype(jnp.bfloat16), gradients[0].astype(jnp.bfloat16)))
    initial = tuple((jnp.zeros_like(array) for array in parameters))
    sums, (outputs, input_gradient) = lax.scan(one_row, initial, (inputs, lengths, cotangent))
    return (outputs, input_gradient, sums[0], sums[1], sums[2], sums[3], sums[4], sums[5], sums[6], sums[7], sums[8], sums[9], sums[10])
```

```python
import functools

import jax
import jax.numpy as jnp
from jax import lax
from jax.experimental import pallas as pl
from jax.experimental.pallas import tpu as pltpu
from jax.sharding import PartitionSpec as P

QUERY_HEADS_TOTAL = 32
KEY_VALUE_HEADS = 8
HEAD_SIZE = 64
FACTOR = HEAD_SIZE ** (-0.5)

epsilon = 1e-06
f32 = jnp.float32
bf16 = jnp.bfloat16


def rms_scale(value_rows):
    return lax.rsqrt(jnp.mean(value_rows * value_rows, axis=-1, keepdims=True) + epsilon)


def rotary_tables(positions, width):
    inverse = 10000.0 ** (-(jnp.arange(width // 2, dtype=f32) * 2.0) / width)
    angle_table = positions.astype(f32)[:, None] * inverse[None, :]
    return (jnp.cos(angle_table), jnp.sin(angle_table))


def rotate(value_rows, cosine, sine):
    half = value_rows.shape[-1] // 2
    first = value_rows[..., :half]
    second = value_rows[..., half:]
    return jnp.concatenate(
        [first * cosine - second * sine, second * cosine + first * sine], axis=-1
    )


def dot_nn(left, right):
    return jnp.dot(left, right, preferred_element_type=f32)


def dot_tn(left, right):
    return lax.dot_general(left, right, (((0,), (0,)), ((), ())), preferred_element_type=f32)


def dot_nt(left, right):
    return lax.dot_general(left, right, (((1,), (1,)), ((), ())), preferred_element_type=f32)


def hop(value, bit):
    return lax.ppermute(value, "ctx", [(i, i ^ bit) for i in range(lax.axis_size("ctx"))])


def gather_tokens(value):
    if lax.axis_size("ctx") != 8:
        return lax.all_gather(value, "ctx", axis=0)
    half = value.shape[0] // 2
    by_x, by_y = hop(value, 2), hop(value, 4)
    far = jnp.concatenate([hop(by_x[:half], 4), hop(by_y[half:], 2)], axis=0)
    return jnp.stack(
        [value, hop(value, 1), by_x, hop(by_x, 1), by_y, hop(by_y, 1), far, hop(far, 1)], axis=0
    )


def scatter_tokens(parts):
    if lax.axis_size("ctx") != 8:
        whole = parts.astype(bf16).reshape(-1, parts.shape[-1])
        return lax.psum_scatter(whole, "ctx", scatter_dimension=0, tiled=True).astype(f32)
    half = parts.shape[1] // 2
    own = [parts[2 * k] + hop(parts[2 * k + 1], 1).astype(f32) for k in (3, 2, 1, 0)]
    far, y_sum, x_sum, total = own
    far = far.astype(bf16)
    from_x, from_y = hop(far[:half], 2), hop(far[half:], 4)
    y_sum = jnp.concatenate([y_sum[:half] + from_x.astype(f32), y_sum[half:]], axis=0)
    x_sum = jnp.concatenate([x_sum[:half], x_sum[half:] + from_y.astype(f32)], axis=0)
    return total + hop(x_sum.astype(bf16), 2).astype(f32) + hop(y_sum.astype(bf16), 4).astype(f32)


def spread_columns(packed):
    rows, parts, columns = packed.shape
    return lax.all_to_all(
        packed.reshape(rows, parts * columns), "ctx", split_axis=1, concat_axis=0, tiled=True
    )


def gather_rows(block):
    return lax.all_gather(block, "dp", axis=0, tiled=True)


def scatter_rows(gradient):
    return lax.psum_scatter(gradient.astype(bf16), "dp", scatter_dimension=0, tiled=True)


def collect_columns(block):
    parts = lax.axis_size("ctx")
    columns = block.shape[1]
    out = lax.all_to_all(block, "ctx", split_axis=0, concat_axis=1, tiled=True)
    return out.reshape(out.shape[0], parts, columns).astype(f32)


def heads_to_rows(block, heads):
    return jnp.concatenate(
        [block[:, h * HEAD_SIZE : (h + 1) * HEAD_SIZE] for h in range(heads)], axis=0
    )


def columns_to_heads(block, heads, slots):
    return jnp.concatenate(
        [block[:, h * slots : (h + 1) * slots].T for h in range(heads)], axis=1
    )


def masked_scores(key_block, query_rows, start, query_block, slots, length):
    scores = dot_nt(key_block, query_rows)
    key_pos = start + lax.broadcasted_iota(jnp.int32, scores.shape, 0)
    query_pos = query_block * slots + lax.rem(
        lax.broadcasted_iota(jnp.int32, scores.shape, 1), slots
    )
    return jnp.where((key_pos <= query_pos) & (key_pos < length), scores, -1e30)


def attend_kernel(
    blocks, slots, heads, chunk, base_ref, len_ref, q_ref, k_ref, v_ref, o_ref, lse_ref, k_all, v_t
):
    row, query_block = pl.program_id(0), pl.program_id(1)
    base, length = base_ref[0], len_ref[row]

    @pl.when(query_block == 0)
    def _():
        for j in range(blocks):
            at = lax.bitwise_xor(base, j)
            k_all[j * slots : (j + 1) * slots, :] = k_ref[at, 0]
            v_t[:, j * slots : (j + 1) * slots] = v_ref[at, 0].T

    count = lax.div(
        jnp.minimum((query_block + 1) * slots, length) + (chunk - 1), jnp.int32(chunk)
    )
    query_rows = heads_to_rows(q_ref[0, 0], heads) * FACTOR
    columns = heads * slots

    def step(j, carry):
        top, total, accum = carry
        start = pl.multiple_of(j * chunk, chunk)
        scores = masked_scores(
            k_all[pl.ds(start, chunk), :], query_rows, start, query_block, slots, length
        )
        new_top = jnp.maximum(top, jnp.max(scores, axis=0, keepdims=True))
        probs = jnp.exp(scores - new_top)
        alpha = jnp.exp(top - new_top)
        total = total * alpha + jnp.sum(probs, axis=0, keepdims=True)
        accum = accum * alpha + dot_nn(v_t[:, pl.ds(start, chunk)], probs.astype(bf16))
        return new_top, total, accum

    top, total, accum = lax.fori_loop(
        0,
        count,
        step,
        (
            jnp.full((1, columns), -1e30, f32),
            jnp.zeros((1, columns), f32),
            jnp.zeros((HEAD_SIZE, columns), f32),
        ),
    )
    o_ref[0, 0] = columns_to_heads(accum / total, heads, slots).astype(bf16)
    lse_ref[0, 0] = top + jnp.log(total)


def attend_back_kernel(
    blocks, slots, heads, chunk,
    base_ref, len_ref, q_ref, k_ref, v_ref, o_ref, do_ref, lse_ref,
    dq_ref, dk_ref, dv_ref, k_all, v_all, k_t, dk_all, dv_all,
):
    row, query_block = pl.program_id(0), pl.program_id(1)
    base, length = base_ref[0], len_ref[row]

    @pl.when(query_block == 0)
    def _():
        for j in range(blocks):
            at = lax.bitwise_xor(base, j)
            keys = k_ref[at, 0]
            k_all[j * slots : (j + 1) * slots, :] = keys
            k_t[:, j * slots : (j + 1) * slots] = keys.T
            v_all[j * slots : (j + 1) * slots, :] = v_ref[at, 0]
        dk_all[...] = jnp.zeros_like(dk_all)
        dv_all[...] = jnp.zeros_like(dv_all)

    count = lax.div(
        jnp.minimum((query_block + 1) * slots, length) + (chunk - 1), jnp.int32(chunk)
    )
    query_rows = heads_to_rows(q_ref[0, 0], heads) * FACTOR
    grad_rows = heads_to_rows(do_ref[0, 0], heads)
    products = do_ref[0, 0].astype(f32) * o_ref[0, 0].astype(f32)
    delta = jnp.concatenate(
        [
            jnp.sum(products[:, h * HEAD_SIZE : (h + 1) * HEAD_SIZE].T, axis=0, keepdims=True)
            for h in range(heads)
        ],
        axis=1,
    )
    log_total = lse_ref[0, 0]

    def step(j, dq_t):
        start = pl.multiple_of(j * chunk, chunk)
        at = pl.ds(start, chunk)
        scores = masked_scores(k_all[at, :], query_rows, start, query_block, slots, length)
        probs = jnp.exp(scores - log_total)
        grad_probs = dot_nt(v_all[at, :], grad_rows)
        grad_scores = (probs * (grad_probs - delta)).astype(bf16)
        dv_all[at, :] += dot_nn(probs.astype(bf16), grad_rows)
        dk_all[at, :] += dot_nn(grad_scores, query_rows)
        return dq_t + dot_nn(k_t[:, at], grad_scores)

    dq_t = lax.fori_loop(0, count, step, jnp.zeros((HEAD_SIZE, heads * slots), f32))
    dq_ref[0, 0] = columns_to_heads(dq_t * FACTOR, heads, slots)

    @pl.when(query_block == blocks - 1)
    def _():
        for j in range(blocks):
            at = lax.bitwise_xor(base, j)
            dk_ref[at, 0] = dk_all[j * slots : (j + 1) * slots, :]
            dv_ref[at, 0] = dv_all[j * slots : (j + 1) * slots, :]


def attention_specs(blocks, slots, width):
    own = lambda r, i, base, lens: (lax.bitwise_xor(base[0], i), r, 0, 0)
    whole = lambda r, i, base, lens: (0, r, 0, 0)
    return (
        pl.BlockSpec((1, 1, slots, width), own),
        pl.BlockSpec((blocks, 1, slots, HEAD_SIZE), whole),
        pl.BlockSpec((1, 1, 1, width // HEAD_SIZE * slots), own),
    )


def attend(base, lengths, queries, keys, values):
    blocks, rows, slots, width = queries.shape
    heads = width // HEAD_SIZE
    chunk = 2 * slots
    query_spec, key_spec, lse_spec = attention_specs(blocks, slots, width)
    total = blocks * slots
    work = rows * heads * total * total // 2
    return pl.pallas_call(
        functools.partial(attend_kernel, blocks, slots, heads, chunk),
        grid_spec=pltpu.PrefetchScalarGridSpec(
            num_scalar_prefetch=2,
            grid=(rows, blocks),
            in_specs=[query_spec, key_spec, key_spec],
            out_specs=[query_spec, lse_spec],
            scratch_shapes=[
                pltpu.VMEM((total, HEAD_SIZE), bf16),
                pltpu.VMEM((HEAD_SIZE, total), bf16),
            ],
        ),
        out_shape=[
            jax.ShapeDtypeStruct(queries.shape, bf16),
            jax.ShapeDtypeStruct((blocks, rows, 1, heads * slots), f32),
        ],
        compiler_params=pltpu.CompilerParams(vmem_limit_bytes=32 * 2**20),
        cost_estimate=pl.CostEstimate(
            flops=16 * HEAD_SIZE * work, bytes_accessed=4 * queries.size, transcendentals=work
        ),
        name="attend",
    )(base, lengths, queries, keys, values)


def attend_back(base, lengths, queries, keys, values, attended, gradient, log_total):
    blocks, rows, slots, width = queries.shape
    heads = width // HEAD_SIZE
    chunk = 2 * slots
    query_spec, key_spec, lse_spec = attention_specs(blocks, slots, width)
    total = blocks * slots
    work = rows * heads * total * total // 2
    return pl.pallas_call(
        functools.partial(attend_back_kernel, blocks, slots, heads, chunk),
        grid_spec=pltpu.PrefetchScalarGridSpec(
            num_scalar_prefetch=2,
            grid=(rows, blocks),
            in_specs=[query_spec, key_spec, key_spec, query_spec, query_spec, lse_spec],
            out_specs=[query_spec, key_spec, key_spec],
            scratch_shapes=[
                pltpu.VMEM((total, HEAD_SIZE), bf16),
                pltpu.VMEM((total, HEAD_SIZE), bf16),
                pltpu.VMEM((HEAD_SIZE, total), bf16),
                pltpu.VMEM((total, HEAD_SIZE), f32),
                pltpu.VMEM((total, HEAD_SIZE), f32),
            ],
        ),
        out_shape=[
            jax.ShapeDtypeStruct(queries.shape, f32),
            jax.ShapeDtypeStruct(keys.shape, f32),
            jax.ShapeDtypeStruct(values.shape, f32),
        ],
        compiler_params=pltpu.CompilerParams(vmem_limit_bytes=32 * 2**20),
        cost_estimate=pl.CostEstimate(
            flops=40 * HEAD_SIZE * work, bytes_accessed=12 * queries.size, transcendentals=work
        ),
        name="attend_back",
    )(base, lengths, queries, keys, values, attended, gradient, log_total)


def body(
    inputs,
    lengths,
    attention_gain,
    query_weight,
    key_matrix,
    value_matrix,
    out_weight,
    query_gain,
    key_gain,
    feedforward_gain,
    gate_weight,
    up_weight,
    down_weight,
    cotangent,
):
    rows, slots, width = inputs.shape
    tokens = rows * slots
    parts = lax.axis_size("ctx")
    heads = QUERY_HEADS_TOTAL // parts
    share = parts // KEY_VALUE_HEADS
    query_cols = heads * HEAD_SIZE
    weight_rows = query_weight.shape[0]
    feed = gate_weight.shape[1] // parts
    all_tokens = parts * tokens
    if parts == 8:
        base = lax.axis_index("ctx").astype(jnp.int32)
    else:
        base = jnp.int32(0)

    key_blocks = [
        jnp.repeat(w.reshape(weight_rows, KEY_VALUE_HEADS, HEAD_SIZE), share, axis=1)
        for w in (key_matrix, value_matrix)
    ]
    attention_pack = jnp.concatenate(
        [query_weight.reshape(weight_rows, parts, query_cols)]
        + key_blocks
        + [out_weight.reshape(weight_rows, parts, query_cols)],
        axis=2,
    )
    attention_block = spread_columns(attention_pack)
    gate_weight, up_weight, down_weight, attention_block = lax.optimization_barrier(
        (gate_weight, up_weight, down_weight, attention_block)
    )
    feed_block = spread_columns(
        jnp.concatenate(
            [w.reshape(weight_rows, parts, feed) for w in (gate_weight, up_weight)], axis=2
        )
    )
    down_block = spread_columns(down_weight.reshape(weight_rows, parts, feed))
    attention_full = gather_rows(attention_block)
    feed_full = gather_rows(feed_block)
    down_full = gather_rows(down_block)
    qkv_cols = query_cols + 2 * HEAD_SIZE
    qkv_full = attention_full[:, :qkv_cols]
    out_full = attention_full[:, qkv_cols:]

    flat = inputs.reshape(tokens, width).astype(f32)
    first_scale = rms_scale(flat)
    normed = flat * first_scale
    hidden = gather_tokens((normed * attention_gain).astype(bf16)).reshape(all_tokens, width)
    raw = dot_nn(hidden, qkv_full)
    positions = (
        lax.bitwise_xor(base, jnp.arange(parts, dtype=jnp.int32))[:, None] * slots
        + jnp.arange(slots, dtype=jnp.int32)[None, :]
    )
    cosine, sine = [
        jnp.broadcast_to(
            t.reshape(parts, 1, slots, 1, HEAD_SIZE // 2),
            (parts, rows, slots, 1, HEAD_SIZE // 2),
        ).reshape(all_tokens, 1, HEAD_SIZE // 2)
        for t in rotary_tables(positions.reshape(-1), HEAD_SIZE)
    ]

    def prepare(query_raw, key_raw, gain_of_query, gain_of_key):
        query_heads = query_raw.reshape(all_tokens, heads, HEAD_SIZE)
        key_heads = key_raw.reshape(all_tokens, 1, HEAD_SIZE)
        rotated_query = rotate(query_heads * rms_scale(query_heads) * gain_of_query, cosine, sine)
        rotated_key = rotate(key_heads * rms_scale(key_heads) * gain_of_key, cosine, sine)
        return (
            rotated_query.reshape(all_tokens, query_cols),
            rotated_key.reshape(all_tokens, HEAD_SIZE),
        )

    (rotated_queries, rotated_keys), prepare_pull = jax.vjp(
        prepare,
        raw[:, :query_cols],
        raw[:, query_cols : query_cols + HEAD_SIZE],
        query_gain.astype(f32),
        key_gain.astype(f32),
    )
    queries = rotated_queries.astype(bf16).reshape(parts, rows, slots, query_cols)
    keys = rotated_keys.astype(bf16).reshape(parts, rows, slots, HEAD_SIZE)
    values = raw[:, query_cols + HEAD_SIZE :].astype(bf16).reshape(parts, rows, slots, HEAD_SIZE)
    base_array = base.reshape(1)
    attended, log_total = attend(base_array, lengths, queries, keys, values)
    attended_rows = attended.reshape(all_tokens, query_cols)
    out_part = dot_nt(attended_rows, out_full).astype(bf16)
    mixed = flat + scatter_tokens(out_part.reshape(parts, tokens, width))

    second_scale = rms_scale(mixed)
    normed_again = mixed * second_scale
    hidden_again = gather_tokens((normed_again * feedforward_gain).astype(bf16)).reshape(
        all_tokens, width
    )
    cotangent_flat = cotangent.reshape(tokens, width)
    cotangents = gather_tokens(cotangent_flat).reshape(all_tokens, width)
    gate_up = dot_nn(hidden_again, feed_full)
    gate, upward = gate_up[:, :feed], gate_up[:, feed:]
    sigmoid_gate = jax.nn.sigmoid(gate)
    silu_gate = gate * sigmoid_gate
    inner = (silu_gate * upward).astype(bf16)
    down_gradient = scatter_rows(dot_tn(cotangents, inner))
    grad_inner = dot_nn(cotangents, down_full)
    grad_gate = (grad_inner * upward * sigmoid_gate * (1.0 + gate * (1.0 - sigmoid_gate))).astype(
        bf16
    )
    grad_up = (grad_inner * silu_gate).astype(bf16)
    grad_gate_up = jnp.concatenate([grad_gate, grad_up], axis=1)
    hidden_again_part = dot_nt(grad_gate_up, feed_full).astype(bf16)
    grad_hidden_again = scatter_tokens(hidden_again_part.reshape(parts, tokens, width))
    feed_gradient = scatter_rows(dot_tn(hidden_again, grad_gate_up))
    feed_out = scatter_tokens(dot_nt(inner, down_full).astype(bf16).reshape(parts, tokens, width))
    outputs = (mixed + feed_out).astype(bf16).reshape(rows, slots, width)
    down_weight_gradient = collect_columns(down_gradient).reshape(weight_rows, parts * feed)
    feed_collected = collect_columns(feed_gradient)
    gate_weight_gradient = feed_collected[:, :, :feed].reshape(weight_rows, parts * feed)
    up_weight_gradient = feed_collected[:, :, feed:].reshape(weight_rows, parts * feed)

    feedforward_gain_local = jnp.sum(grad_hidden_again * normed_again, axis=0)
    scaled_again = grad_hidden_again * feedforward_gain
    grad_mixed = cotangent_flat.astype(f32) + second_scale * (
        scaled_again - normed_again * jnp.mean(scaled_again * normed_again, axis=-1, keepdims=True)
    )

    grad_branch = gather_tokens(grad_mixed.astype(bf16)).reshape(all_tokens, width)
    attended_gradient = dot_nn(grad_branch, out_full).astype(bf16)
    grad_queries, grad_keys, grad_values = attend_back(
        base_array,
        lengths,
        queries,
        keys,
        values,
        attended,
        attended_gradient.reshape(parts, rows, slots, query_cols),
        log_total,
    )
    raw_query_term, raw_key_term, query_gain_local, key_gain_local = prepare_pull(
        (
            grad_queries.reshape(all_tokens, query_cols),
            grad_keys.reshape(all_tokens, HEAD_SIZE),
        )
    )
    grad_raw = jnp.concatenate(
        [raw_query_term, raw_key_term, grad_values.reshape(all_tokens, HEAD_SIZE)], axis=1
    ).astype(bf16)
    hidden_part = dot_nt(grad_raw, qkv_full).astype(bf16)
    grad_hidden = scatter_tokens(hidden_part.reshape(parts, tokens, width))
    attention_gradient = scatter_rows(
        jnp.concatenate([dot_tn(hidden, grad_raw), dot_tn(grad_branch, attended_rows)], axis=1)
    )
    attention_collected = collect_columns(attention_gradient)
    query_weight_gradient = attention_collected[:, :, :query_cols].reshape(weight_rows, -1)
    key_weight_gradient, value_weight_gradient = [
        attention_collected[:, :, start : start + HEAD_SIZE]
        .reshape(weight_rows, KEY_VALUE_HEADS, share, HEAD_SIZE)
        .sum(axis=2)
        .reshape(weight_rows, KEY_VALUE_HEADS * HEAD_SIZE)
        for start in (query_cols, query_cols + HEAD_SIZE)
    ]
    out_weight_gradient = attention_collected[:, :, qkv_cols:].reshape(weight_rows, -1)

    attention_gain_local = jnp.sum(grad_hidden * normed, axis=0)
    scaled_first = grad_hidden * attention_gain
    input_gradient = (
        grad_mixed
        + first_scale
        * (scaled_first - normed * jnp.mean(scaled_first * normed, axis=-1, keepdims=True))
    ).astype(bf16)
    attention_gain_gradient, query_gain_gradient, key_gain_gradient, feedforward_gain_gradient = (
        lax.psum(
            (attention_gain_local, query_gain_local, key_gain_local, feedforward_gain_local),
            ("dp", "ctx"),
        )
    )
    return (
        outputs,
        input_gradient.reshape(rows, slots, width),
        attention_gain_gradient,
        query_weight_gradient,
        key_weight_gradient,
        value_weight_gradient,
        out_weight_gradient,
        query_gain_gradient,
        key_gain_gradient,
        feedforward_gain_gradient,
        gate_weight_gradient,
        up_weight_gradient,
        down_weight_gradient,
    )


def solution(mesh):
    weight = P(("dp", "ctx"), None)
    token = P("dp", "ctx", None)
    placed = (
        token, P("dp"), P(), weight, weight, weight, weight, P(), P(), P(), weight, weight, weight, token,
    )
    returned = (
        token, token, P(), weight, weight, weight, weight, P(), P(), P(), weight, weight, weight,
    )
    return jax.shard_map(
        body, mesh=mesh, in_specs=placed, out_specs=returned, check_vma=False
    )
```

```python
import functools

import jax
import jax.numpy as jnp
from jax import lax
from jax.experimental import pallas as pl
from jax.experimental.pallas import tpu as pltpu
from jax.sharding import PartitionSpec as P

QUERY_HEADS_TOTAL = 32
KEY_VALUE_HEADS = 8
HEAD_SIZE = 64
FACTOR = HEAD_SIZE ** (-0.5)

NO_COST = pl.CostEstimate(flops=0, bytes_accessed=0, transcendentals=0)


epsilon = 1e-06
f32 = jnp.float32
bf16 = jnp.bfloat16


def rms_scale(value_rows):
    return lax.rsqrt(jnp.mean(value_rows * value_rows, axis=-1, keepdims=True) + epsilon)


def rotary_tables(positions, width):
    inverse = 10000.0 ** (-(jnp.arange(width // 2, dtype=f32) * 2.0) / width)
    angle_table = positions.astype(f32)[:, None] * inverse[None, :]
    return (jnp.cos(angle_table), jnp.sin(angle_table))


def dot_nn(left, right):
    return jnp.dot(left, right, preferred_element_type=f32)


def dot_tn(left, right):
    return lax.dot_general(left, right, (((0,), (0,)), ((), ())), preferred_element_type=f32)


def dot_nt(left, right):
    return lax.dot_general(left, right, (((1,), (1,)), ((), ())), preferred_element_type=f32)


def fence(values, *earlier):
    count = len(values)
    anywhere = pl.BlockSpec(memory_space=pl.ANY)
    return pl.pallas_call(
        lambda *refs: None,
        in_specs=[anywhere] * (count + len(earlier)),
        out_specs=[anywhere] * count,
        out_shape=[jax.ShapeDtypeStruct(v.shape, v.dtype) for v in values],
        input_output_aliases={i: i for i in range(count)},
        cost_estimate=NO_COST,
        name="fence",
    )(*values, *earlier)


def after(value, *earlier):
    return fence((value,), *earlier)[0]


RELATIVE = (0, 2, 4, 1, 3, 5, 6, 7)


def place_of(own, index, parts):
    if parts != 8:
        return index
    relative = lax.bitwise_xor(own, index)
    near = lax.shift_right_logical(relative, 1) + 3 * lax.bitwise_and(relative, 1)
    return jnp.where(relative < 6, near, relative)


def hop(value, bit):
    return lax.ppermute(value, "ctx", [(i, i ^ bit) for i in range(lax.axis_size("ctx"))])


def gather_tokens(value):
    return gather_tokens_and_start(value)[0]


def gather_tokens_and_start(value):
    if lax.axis_size("ctx") != 8:
        whole = lax.all_gather(value, "ctx", axis=0)
        return whole, (whole, whole)
    half = value.shape[0] // 2
    by_x, by_y = hop(value, 2), hop(value, 4)
    far = jnp.concatenate([hop(by_x[:half], 4), hop(by_y[half:], 2)], axis=0)
    whole = jnp.stack(
        [value, by_x, by_y, hop(value, 1), hop(by_x, 1), hop(by_y, 1), far, hop(far, 1)], axis=0
    )
    return whole, (by_x, by_y)


def partial_products(product, tokens):
    parts = lax.axis_size("ctx")
    if parts != 8:
        return product(0, parts, [(parts * tokens, bf16)], None, ())
    half = (tokens // 2, bf16)
    (far_other,) = product(7, 1, [(tokens, bf16)], None, ())
    far = product(6, 1, [half] * 2, hop(far_other, 1), ())
    (near_other,) = product(3, 3, [(3 * tokens, bf16)], None, (far[0],))
    own, *near = product(0, 3, [(tokens, f32)] + [half] * 4, hop(near_other, 1), ())
    return (own, *near, *far)


def finish_scatter(sums, tokens):
    if lax.axis_size("ctx") != 8:
        (whole,) = sums
        return lax.psum_scatter(whole, "ctx", scatter_dimension=0, tiled=True).astype(f32)
    own, x_first, x_last, y_first, y_last, far_first, far_last = sums
    from_x, from_y = hop(far_first, 2), hop(far_last, 4)
    x_last = (x_last.astype(f32) + from_y.astype(f32)).astype(bf16)
    y_first = (y_first.astype(f32) + from_x.astype(f32)).astype(bf16)
    x_part = jnp.concatenate([hop(x_first, 2), hop(x_last, 2)], axis=0)
    y_part = jnp.concatenate([hop(y_first, 4), hop(y_last, 4)], axis=0)
    return own + x_part.astype(f32) + y_part.astype(f32)


def sum_everywhere(value):
    if lax.axis_size("ctx") != 8 or lax.axis_size("dp") != 4:
        return lax.psum(value, ("dp", "ctx"))
    for bit in (1, 2, 4):
        value = value + hop(value, bit)
    for bit in (1, 2):
        value = value + lax.ppermute(value, "dp", [(i, i ^ bit) for i in range(4)])
    return value


def spread_columns(packed):
    rows, parts, columns = packed.shape
    return lax.all_to_all(
        packed.reshape(rows, parts * columns), "ctx", split_axis=1, concat_axis=0, tiled=True
    )


def gather_rows(block):
    return lax.all_gather(block, "dp", axis=0, tiled=True)


def scatter_rows(gradient):
    return lax.psum_scatter(gradient, "dp", scatter_dimension=0, tiled=True)


def collect_columns(block):
    parts = lax.axis_size("ctx")
    columns = block.shape[1]
    out = lax.all_to_all(block, "ctx", split_axis=0, concat_axis=1, tiled=True)
    return out.reshape(out.shape[0], parts, columns).astype(f32)


def collect_early(gradient):
    groups, parts = lax.axis_size("dp"), lax.axis_size("ctx")
    block = gradient.reshape(groups, parts, -1, gradient.shape[1])
    block = lax.all_to_all(block, "ctx", split_axis=1, concat_axis=1, tiled=True)
    return block.reshape(-1, gradient.shape[1])


def heads_to_columns(block, heads):
    return jnp.concatenate(
        [block[:, h * HEAD_SIZE : (h + 1) * HEAD_SIZE].T for h in range(heads)], axis=1
    )


def columns_to_heads(columns, heads, slots):
    return jnp.concatenate(
        [columns[:, h * slots : (h + 1) * slots].T for h in range(heads)], axis=1
    )


def columns_to_rows(columns, heads, slots):
    return jnp.concatenate(
        [columns[:, h * slots : (h + 1) * slots].T for h in range(heads)], axis=0
    )


def head_scale(raw):
    return lax.rsqrt(jnp.mean(raw * raw, axis=0, keepdims=True) + epsilon)


def prepare(raw, gain, cosine, sine):
    value = raw * head_scale(raw) * gain
    first, second = value[: HEAD_SIZE // 2], value[HEAD_SIZE // 2 :]
    return jnp.concatenate(
        [first * cosine - second * sine, second * cosine + first * sine], axis=0
    )


def prepare_back(gradient, raw, gain, cosine, sine):
    scale = head_scale(raw)
    unit = raw * scale
    first, second = gradient[: HEAD_SIZE // 2], gradient[HEAD_SIZE // 2 :]
    turned = jnp.concatenate(
        [first * cosine + second * sine, second * cosine - first * sine], axis=0
    )
    inside = turned * gain
    middle = jnp.mean(inside * unit, axis=0, keepdims=True)
    return scale * (inside - unit * middle), turned * unit


def fold(values):
    lanes = 128
    return sum(values[:, i : i + lanes] for i in range(0, values.shape[1], lanes))


def repeated(table, heads):
    return jnp.concatenate([table] * heads, axis=1)


def masked_scores(key_block, query_columns, start, query_block, slots, length):
    scores = dot_nn(key_block, query_columns)
    key_pos = start + lax.broadcasted_iota(jnp.int32, scores.shape, 0)
    query_pos = query_block * slots + lax.rem(
        lax.broadcasted_iota(jnp.int32, scores.shape, 1), slots
    )
    return jnp.where((key_pos <= query_pos) & (key_pos < length), scores, -1e30)


def chunks_needed(query_block, slots, length, chunk):
    return lax.div(
        jnp.minimum((query_block + 1) * slots, length) + (chunk - 1), jnp.int32(chunk)
    )


def attend_kernel(
    blocks, slots, heads, chunk,
    base_ref, len_ref, q_ref, kv_ref, qg_ref, kg_ref, cos_ref, sin_ref,
    o_ref, lse_ref, k_all, v_t,
):
    row, query_block = pl.program_id(0), pl.program_id(1)
    base, length = base_ref[0], len_ref[row]

    @pl.when(query_block == 0)
    def _():
        for j in range(blocks):
            at = place_of(base, jnp.int32(j), blocks)
            here = slice(j * slots, (j + 1) * slots)
            both = kv_ref[at, 0].T
            keys = prepare(both[:HEAD_SIZE], kg_ref[...], cos_ref[:, here], sin_ref[:, here])
            k_all[here, :] = keys.T.astype(bf16)
            v_t[:, here] = both[HEAD_SIZE:].astype(bf16)

    count = chunks_needed(query_block, slots, length, chunk)
    here = pl.ds(pl.multiple_of(query_block * slots, slots), slots)
    queries = prepare(
        heads_to_columns(q_ref[0, 0], heads),
        qg_ref[...],
        repeated(cos_ref[:, here], heads),
        repeated(sin_ref[:, here], heads),
    )
    queries = queries.astype(bf16) * FACTOR
    columns = heads * slots

    def step(j, carry):
        top, total, accum = carry
        start = pl.multiple_of(j * chunk, chunk)
        scores = masked_scores(
            k_all[pl.ds(start, chunk), :], queries, start, query_block, slots, length
        )
        new_top = jnp.maximum(top, jnp.max(scores, axis=0, keepdims=True))
        probs = jnp.exp(scores - new_top)
        alpha = jnp.exp(top - new_top)
        total = total * alpha + jnp.sum(probs, axis=0, keepdims=True)
        accum = accum * alpha + dot_nn(v_t[:, pl.ds(start, chunk)], probs.astype(bf16))
        return new_top, total, accum

    top, total, accum = lax.fori_loop(
        0,
        count,
        step,
        (
            jnp.full((1, columns), -1e30, f32),
            jnp.zeros((1, columns), f32),
            jnp.zeros((HEAD_SIZE, columns), f32),
        ),
    )
    o_ref[0, 0] = columns_to_heads(accum / total, heads, slots).astype(bf16)
    lse_ref[0, 0] = top + jnp.log(total)


def attend_back_kernel(
    blocks, slots, heads, chunk,
    base_ref, len_ref, q_ref, kv_ref, qg_ref, kg_ref, cos_ref, sin_ref, o_ref, do_ref, lse_ref,
    dq_ref, dkv_ref, dqg_ref, dkg_ref, k_all, v_all, k_t, dk_all, dv_all,
):
    row, query_block = pl.program_id(0), pl.program_id(1)
    base, length = base_ref[0], len_ref[row]

    @pl.when((row == 0) & (query_block == 0))
    def _():
        dqg_ref[...] = jnp.zeros_like(dqg_ref)
        dkg_ref[...] = jnp.zeros_like(dkg_ref)

    @pl.when(query_block == 0)
    def _():
        for j in range(blocks):
            at = place_of(base, jnp.int32(j), blocks)
            here = slice(j * slots, (j + 1) * slots)
            both = kv_ref[at, 0]
            keys = prepare(both.T[:HEAD_SIZE], kg_ref[...], cos_ref[:, here], sin_ref[:, here])
            k_t[:, here] = keys.astype(bf16)
            k_all[here, :] = keys.T.astype(bf16)
            v_all[here, :] = both[:, HEAD_SIZE:].astype(bf16)
        dk_all[...] = jnp.zeros_like(dk_all)
        dv_all[...] = jnp.zeros_like(dv_all)

    count = chunks_needed(query_block, slots, length, chunk)
    here = pl.ds(pl.multiple_of(query_block * slots, slots), slots)
    cosine, sine = repeated(cos_ref[:, here], heads), repeated(sin_ref[:, here], heads)
    raw = heads_to_columns(q_ref[0, 0], heads)
    queries = prepare(raw, qg_ref[...], cosine, sine).astype(bf16) * FACTOR
    query_rows = columns_to_rows(queries.astype(f32), heads, slots).astype(bf16)
    gradient = heads_to_columns(do_ref[0, 0].astype(f32), heads)
    grad_rows = columns_to_rows(gradient, heads, slots).astype(bf16)
    delta = jnp.sum(
        gradient * heads_to_columns(o_ref[0, 0].astype(f32), heads), axis=0, keepdims=True
    )
    gradient = gradient.astype(bf16)
    log_total = lse_ref[0, 0]

    def step(j, dq_t):
        start = pl.multiple_of(j * chunk, chunk)
        at = pl.ds(start, chunk)
        scores = masked_scores(k_all[at, :], queries, start, query_block, slots, length)
        probs = jnp.exp(scores - log_total)
        grad_probs = dot_nn(v_all[at, :], gradient)
        grad_scores = (probs * (grad_probs - delta)).astype(bf16)
        dv_all[at, :] += dot_nn(probs.astype(bf16), grad_rows)
        dk_all[at, :] += dot_nn(grad_scores, query_rows)
        return dq_t + dot_nn(k_t[:, at], grad_scores)

    dq_t = lax.fori_loop(0, count, step, jnp.zeros((HEAD_SIZE, heads * slots), f32))
    raw_term, gain_term = prepare_back(dq_t * FACTOR, raw, qg_ref[...], cosine, sine)
    dq_ref[0, 0] = columns_to_heads(raw_term, heads, slots).astype(bf16)
    dqg_ref[...] += fold(gain_term)

    @pl.when(query_block == blocks - 1)
    def _():
        for j in range(blocks):
            at = place_of(base, jnp.int32(j), blocks)
            here = slice(j * slots, (j + 1) * slots)
            raw_term, gain_term = prepare_back(
                dk_all[here, :].T,
                kv_ref[at, 0].T[:HEAD_SIZE],
                kg_ref[...],
                cos_ref[:, here],
                sin_ref[:, here],
            )
            dkg_ref[...] += fold(gain_term)
            dkv_ref[at, 0] = jnp.concatenate([raw_term.T, dv_all[here, :]], axis=1).astype(bf16)


def attention_specs(blocks, slots, width, total):
    own = lambda r, i, base, lens: (place_of(base[0], i, blocks), r, 0, 0)
    constant = lambda r, i, base, lens: (0, 0)
    both = 2 * HEAD_SIZE
    return (
        pl.BlockSpec((1, 1, slots, width), own),
        pl.BlockSpec((blocks, 1, slots, both), lambda r, i, base, lens: (0, r, 0, width // both)),
        pl.BlockSpec((blocks, 1, slots, both), lambda r, i, base, lens: (0, r, 0, 0)),
        pl.BlockSpec((HEAD_SIZE, 1), constant),
        pl.BlockSpec((HEAD_SIZE // 2, total), constant),
        pl.BlockSpec((1, 1, 1, width // HEAD_SIZE * slots), own),
        pl.BlockSpec((HEAD_SIZE, 128), constant),
    )


def attend(base, lengths, raw, query_gain, key_gain, cosine, sine):
    blocks, rows, slots, columns = raw.shape
    width = columns - 2 * HEAD_SIZE
    heads = width // HEAD_SIZE
    total = blocks * slots
    query_spec, raw_key_spec, _, gain_spec, table_spec, lse_spec, _ = attention_specs(
        blocks, slots, width, total
    )
    return pl.pallas_call(
        functools.partial(attend_kernel, blocks, slots, heads, 2 * slots),
        grid_spec=pltpu.PrefetchScalarGridSpec(
            num_scalar_prefetch=2,
            grid=(rows, blocks),
            in_specs=[query_spec, raw_key_spec, gain_spec, gain_spec, table_spec, table_spec],
            out_specs=[query_spec, lse_spec],
            scratch_shapes=[
                pltpu.VMEM((total, HEAD_SIZE), bf16),
                pltpu.VMEM((HEAD_SIZE, total), bf16),
            ],
        ),
        out_shape=[
            jax.ShapeDtypeStruct((blocks, rows, slots, width), bf16),
            jax.ShapeDtypeStruct((blocks, rows, 1, heads * slots), f32),
        ],
        compiler_params=pltpu.CompilerParams(vmem_limit_bytes=32 * 2**20),
        cost_estimate=NO_COST,
        name="attend",
    )(base, lengths, raw, raw, query_gain, key_gain, cosine, sine)


def attend_back(
    base, lengths, raw, query_gain, key_gain, cosine, sine, attended, gradient, log_total
):
    blocks, rows, slots, columns = raw.shape
    width = columns - 2 * HEAD_SIZE
    heads = width // HEAD_SIZE
    total = blocks * slots
    query_spec, raw_key_spec, key_spec, gain_spec, table_spec, lse_spec, sum_spec = (
        attention_specs(blocks, slots, width, total)
    )
    return pl.pallas_call(
        functools.partial(attend_back_kernel, blocks, slots, heads, 2 * slots),
        grid_spec=pltpu.PrefetchScalarGridSpec(
            num_scalar_prefetch=2,
            grid=(rows, blocks),
            in_specs=[query_spec, raw_key_spec, gain_spec, gain_spec, table_spec, table_spec]
            + [query_spec, query_spec, lse_spec],
            out_specs=[query_spec, key_spec, sum_spec, sum_spec],
            scratch_shapes=[
                pltpu.VMEM((total, HEAD_SIZE), bf16),
                pltpu.VMEM((total, HEAD_SIZE), bf16),
                pltpu.VMEM((HEAD_SIZE, total), bf16),
                pltpu.VMEM((total, HEAD_SIZE), f32),
                pltpu.VMEM((total, HEAD_SIZE), f32),
            ],
        ),
        out_shape=[
            jax.ShapeDtypeStruct((blocks, rows, slots, width), bf16),
            jax.ShapeDtypeStruct((blocks, rows, slots, 2 * HEAD_SIZE), bf16),
            jax.ShapeDtypeStruct((HEAD_SIZE, 128), f32),
            jax.ShapeDtypeStruct((HEAD_SIZE, 128), f32),
        ],
        compiler_params=pltpu.CompilerParams(vmem_limit_bytes=32 * 2**20),
        cost_estimate=NO_COST,
        name="attend_back",
    )(base, lengths, raw, raw, query_gain, key_gain, cosine, sine, attended, gradient, log_total)


def feed_kernel(hidden_ref, cotangent_ref, weight_ref, inner_ref, grad_ref):
    units = inner_ref.shape[1]
    hidden = hidden_ref[...]
    gate = dot_nn(hidden, weight_ref[:, :units])
    upward = dot_nn(hidden, weight_ref[:, units : 2 * units])
    grad_inner = dot_nn(cotangent_ref[...], weight_ref[:, 2 * units :])
    sigmoid_gate = jax.nn.sigmoid(gate)
    silu_gate = gate * sigmoid_gate
    inner_ref[...] = (silu_gate * upward).astype(bf16)
    grad_ref[:, :units] = (
        grad_inner * upward * sigmoid_gate * (1.0 + gate * (1.0 - sigmoid_gate))
    ).astype(bf16)
    grad_ref[:, units:] = (grad_inner * silu_gate).astype(bf16)


def feed_forward(hidden, cotangents, weights):
    count, width = hidden.shape
    units = weights.shape[1] // 3
    tile = 512
    rows = pl.BlockSpec((tile, width), lambda i: (i, 0))
    return pl.pallas_call(
        feed_kernel,
        grid=(count // tile,),
        in_specs=[rows, rows, pl.BlockSpec(weights.shape, lambda i: (0, 0))],
        out_specs=[
            pl.BlockSpec((tile, units), lambda i: (i, 0)),
            pl.BlockSpec((tile, 2 * units), lambda i: (i, 0)),
        ],
        out_shape=[
            jax.ShapeDtypeStruct((count, units), bf16),
            jax.ShapeDtypeStruct((count, 2 * units), bf16),
        ],
        compiler_params=pltpu.CompilerParams(vmem_limit_bytes=48 * 2**20),
        cost_estimate=NO_COST,
        name="feed_forward",
    )(hidden, cotangents, weights)


def product_kernel(count, adds, outs, *refs):
    rows, weights, rest = refs[:count], refs[count : 2 * count], refs[2 * count : 2 * count + adds]
    total = sum(dot_nt(r[...], w[...]) for r, w in zip(rows, weights))
    for add_ref in rest:
        total += add_ref[...].astype(f32)
    start = 0
    for out_ref in refs[-outs:]:
        out_ref[...] = total[start : start + out_ref.shape[0]].astype(out_ref.dtype)
        start += out_ref.shape[0]


def sum_of_products(lefts, weights, column, tokens, first, count, splits, add, before):
    rows = count * tokens
    width = weights[0].shape[0]
    tile = 512
    operands = list(lefts) + list(weights)
    specs = [pl.BlockSpec((rows, v.shape[1]), lambda i: (first // count, 0)) for v in lefts] + [
        pl.BlockSpec((tile, v.shape[1]), lambda i: (i, column)) for v in lefts
    ]
    if add is not None:
        operands.append(add)
        specs.append(pl.BlockSpec((rows, tile), lambda i: (0, i)))
    operands += before
    specs += [pl.BlockSpec(memory_space=pl.ANY)] * len(before)
    return pl.pallas_call(
        functools.partial(product_kernel, len(lefts), int(add is not None), len(splits)),
        grid=(width // tile,),
        in_specs=specs,
        out_specs=[pl.BlockSpec((r, tile), lambda i: (0, i)) for r, _ in splits],
        out_shape=[jax.ShapeDtypeStruct((r, width), dtype) for r, dtype in splits],
        compiler_params=pltpu.CompilerParams(vmem_limit_bytes=48 * 2**20),
        cost_estimate=NO_COST,
        name="sum_of_products",
    )(*operands)


def body(
    inputs,
    lengths,
    attention_gain,
    query_weight,
    key_matrix,
    value_matrix,
    out_weight,
    query_gain,
    key_gain,
    feedforward_gain,
    gate_weight,
    up_weight,
    down_weight,
    cotangent,
):
    rows, slots, width = inputs.shape
    tokens = rows * slots
    parts = lax.axis_size("ctx")
    heads = QUERY_HEADS_TOTAL // parts
    share = parts // KEY_VALUE_HEADS
    query_cols = heads * HEAD_SIZE
    weight_rows = query_weight.shape[0]
    feed = gate_weight.shape[1] // parts
    all_tokens = parts * tokens
    base = lax.axis_index("ctx").astype(jnp.int32)

    qkv_pack = jnp.concatenate(
        [query_weight.reshape(weight_rows, parts, query_cols)]
        + [
            jnp.repeat(w.reshape(weight_rows, KEY_VALUE_HEADS, HEAD_SIZE), share, axis=1)
            for w in (key_matrix, value_matrix)
        ],
        axis=2,
    )
    qkv_block = spread_columns(qkv_pack)
    out_block = spread_columns(out_weight.reshape(weight_rows, parts, query_cols))
    units = feed // 2
    feed_packs = [
        jnp.concatenate(
            [
                w.reshape(weight_rows, parts, feed)[:, :, start : start + units]
                for w in (gate_weight, up_weight, down_weight)
            ],
            axis=2,
        )
        for start in (0, units)
    ]
    flat = inputs.reshape(tokens, width).astype(f32)
    first_scale = rms_scale(flat)
    normed = flat * first_scale
    hidden, hidden_start = gather_tokens_and_start((normed * attention_gain).astype(bf16))
    hidden = hidden.reshape(all_tokens, width)
    first_block = spread_columns(after(feed_packs[0], out_block, *hidden_start))
    qkv_full = gather_rows(qkv_block)
    out_full = gather_rows(out_block)
    first_full = gather_rows(first_block)
    hidden = after(hidden, first_block)

    raw = dot_nn(hidden, qkv_full).reshape(parts, rows, slots, query_cols + 2 * HEAD_SIZE)
    cotangent_flat = cotangent.reshape(tokens, width)
    cotangents, cotangents_start = gather_tokens_and_start(after(cotangent_flat, first_block))
    cotangents = cotangents.reshape(all_tokens, width)
    last_block = spread_columns(after(feed_packs[1], *cotangents_start))
    cosine, sine = [
        t.T for t in rotary_tables(jnp.arange(parts * slots, dtype=jnp.int32), HEAD_SIZE)
    ]
    base_array = base.reshape(1)
    gains = [g.astype(f32).reshape(HEAD_SIZE, 1) for g in (query_gain, key_gain)]
    attended, log_total = attend(base_array, lengths, raw, *gains, cosine, sine)
    attended_rows = attended.reshape(all_tokens, query_cols)
    sums = partial_products(
        functools.partial(sum_of_products, [attended_rows], [out_full], 0, tokens), tokens
    )
    mixed = flat + finish_scatter(fence(sums, last_block), tokens)

    second_scale = rms_scale(mixed)
    normed_again = mixed * second_scale
    hidden_again = gather_tokens(
        after((normed_again * feedforward_gain).astype(bf16), first_full)
    ).reshape(all_tokens, width)
    last_full = gather_rows(after(last_block, first_full))
    fulls = [first_full, last_full]
    inners, grads, partials = [], [], []
    for which in range(2):
        if which == 1:
            fulls[1] = after(last_full, *partials[0])
        inner, grad = feed_forward(hidden_again, cotangents, fulls[which])
        inners.append(inner)
        grads.append(grad)
        partials.append(
            (dot_tn(hidden_again, grad).astype(bf16), dot_tn(cotangents, inner).astype(bf16))
        )
    first_gradients, last_gradients = [[scatter_rows(p) for p in pair] for pair in partials]
    sums = partial_products(
        functools.partial(sum_of_products, grads, fulls, 0, tokens), tokens
    )
    grad_hidden_again = after(finish_scatter(sums, tokens), first_gradients[1])
    feedforward_gain_local = jnp.sum(grad_hidden_again * normed_again, axis=0)
    scaled_again = grad_hidden_again * feedforward_gain
    grad_mixed = cotangent_flat.astype(f32) + second_scale * (
        scaled_again - normed_again * jnp.mean(scaled_again * normed_again, axis=-1, keepdims=True)
    )

    grad_branch = gather_tokens(grad_mixed.astype(bf16)).reshape(all_tokens, width)
    grad_branch = after(grad_branch, first_gradients[0])
    attended_gradient = dot_nn(grad_branch, out_full).astype(bf16)
    feed_sums = partial_products(
        functools.partial(sum_of_products, inners, fulls, 2, tokens), tokens
    )
    attended_gradient = after(attended_gradient, *feed_sums)
    feed_out = finish_scatter(fence(feed_sums, grad_branch), tokens)
    outputs = (mixed + feed_out).astype(bf16).reshape(rows, slots, width)
    grad_queries, grad_keys_values, query_gain_sums, key_gain_sums = attend_back(
        base_array,
        lengths,
        raw,
        *gains,
        cosine,
        sine,
        attended,
        attended_gradient.reshape(parts, rows, slots, query_cols),
        log_total,
    )
    query_gain_local, key_gain_local = query_gain_sums.sum(axis=1), key_gain_sums.sum(axis=1)
    grad_raw = jnp.concatenate(
        [
            grad_queries.reshape(all_tokens, query_cols),
            grad_keys_values.reshape(all_tokens, 2 * HEAD_SIZE),
        ],
        axis=1,
    )
    attention_partial = jnp.concatenate(
        [dot_tn(hidden, grad_raw), dot_tn(grad_branch, attended_rows)], axis=1
    ).astype(bf16)
    first_collected = [collect_columns(after(g, attended_gradient)) for g in first_gradients]
    attention_partial = after(attention_partial, feed_out, *first_collected)
    early = collect_early(after(attention_partial, last_gradients[1]))
    attention_collected = lax.psum_scatter(
        after(early, last_gradients[0]), "dp", scatter_dimension=0, tiled=True
    )
    attention_collected = jnp.swapaxes(
        attention_collected.reshape(parts, weight_rows, -1), 0, 1
    ).astype(f32)
    sums = partial_products(
        functools.partial(sum_of_products, [grad_raw], [qkv_full], 0, tokens), tokens
    )
    grad_hidden = finish_scatter(fence(sums, early), tokens)
    collected = [
        first_collected,
        [collect_columns(g) for g in last_gradients],
    ]
    gate_weight_gradient, up_weight_gradient = [
        jnp.concatenate([c[0][:, :, start : start + units] for c in collected], axis=2).reshape(
            weight_rows, parts * feed
        )
        for start in (0, units)
    ]
    down_weight_gradient = jnp.concatenate([c[1] for c in collected], axis=2).reshape(
        weight_rows, parts * feed
    )
    query_weight_gradient = attention_collected[:, :, :query_cols].reshape(weight_rows, -1)
    key_weight_gradient, value_weight_gradient = [
        attention_collected[:, :, start : start + HEAD_SIZE]
        .reshape(weight_rows, KEY_VALUE_HEADS, share, HEAD_SIZE)
        .sum(axis=2)
        .reshape(weight_rows, KEY_VALUE_HEADS * HEAD_SIZE)
        for start in (query_cols, query_cols + HEAD_SIZE)
    ]

    out_weight_gradient = attention_collected[:, :, query_cols + 2 * HEAD_SIZE :].reshape(
        weight_rows, -1
    )

    attention_gain_local = jnp.sum(grad_hidden * normed, axis=0)
    scaled_first = grad_hidden * attention_gain
    input_gradient = (
        grad_mixed
        + first_scale
        * (scaled_first - normed * jnp.mean(scaled_first * normed, axis=-1, keepdims=True))
    ).astype(bf16)
    gain_sums = sum_everywhere(
        jnp.concatenate(
            [attention_gain_local, feedforward_gain_local, query_gain_local, key_gain_local]
        )
    )
    attention_gain_gradient, feedforward_gain_gradient = gain_sums[:width], gain_sums[width : 2 * width]
    query_gain_gradient = gain_sums[2 * width : 2 * width + HEAD_SIZE]
    key_gain_gradient = gain_sums[2 * width + HEAD_SIZE :]
    return (
        outputs,
        input_gradient.reshape(rows, slots, width),
        attention_gain_gradient,
        query_weight_gradient,
        key_weight_gradient,
        value_weight_gradient,
        out_weight_gradient,
        query_gain_gradient,
        key_gain_gradient,
        feedforward_gain_gradient,
        gate_weight_gradient,
        up_weight_gradient,
        down_weight_gradient,
    )


def solution(mesh):
    weight = P(("dp", "ctx"), None)
    token = P("dp", "ctx", None)
    placed = (
        token, P("dp"), P(), weight, weight, weight, weight, P(), P(), P(), weight, weight, weight, token,
    )
    returned = (
        token, token, P(), weight, weight, weight, weight, P(), P(), P(), weight, weight, weight,
    )
    return jax.shard_map(
        body, mesh=mesh, in_specs=placed, out_specs=returned, check_vma=False
    )
```

```python
import functools

import jax
import jax.numpy as jnp
from jax import lax
from jax.experimental import pallas as pl
from jax.experimental.pallas import tpu as pltpu
from jax.sharding import PartitionSpec as P

QUERY_HEADS_TOTAL = 32
KEY_VALUE_HEADS = 8
HEAD_SIZE = 64
FACTOR = HEAD_SIZE ** (-0.5)

NO_COST = pl.CostEstimate(flops=0, bytes_accessed=0, transcendentals=0)


def cost(flops, share):
    return pl.CostEstimate(flops=int(flops * share), bytes_accessed=0, transcendentals=0)


epsilon = 1e-06
f32 = jnp.float32
bf16 = jnp.bfloat16


def rms_scale(value_rows):
    return lax.rsqrt(jnp.mean(value_rows * value_rows, axis=-1, keepdims=True) + epsilon)


def rotary_tables(positions, width):
    inverse = 10000.0 ** (-(jnp.arange(width // 2, dtype=f32) * 2.0) / width)
    angle_table = positions.astype(f32)[:, None] * inverse[None, :]
    return (jnp.cos(angle_table), jnp.sin(angle_table))


def dot_nn(left, right):
    return jnp.dot(left, right, preferred_element_type=f32)


def dot_tn(left, right):
    return lax.dot_general(left, right, (((0,), (0,)), ((), ())), preferred_element_type=f32)


def dot_nt(left, right):
    return lax.dot_general(left, right, (((1,), (1,)), ((), ())), preferred_element_type=f32)


def fence(values, *earlier):
    count = len(values)
    anywhere = pl.BlockSpec(memory_space=pl.ANY)
    return pl.pallas_call(
        lambda *refs: None,
        in_specs=[anywhere] * (count + len(earlier)),
        out_specs=[anywhere] * count,
        out_shape=[jax.ShapeDtypeStruct(v.shape, v.dtype) for v in values],
        input_output_aliases={i: i for i in range(count)},
        cost_estimate=NO_COST,
        name="fence",
    )(*values, *earlier)


def after(value, *earlier):
    return fence((value,), *earlier)[0]


def stack_kernel(*refs):
    for k, ref in enumerate(refs[:-1]):

        @pl.when(pl.program_id(0) == k)
        def _():
            refs[-1][...] = ref[...]


def stack(pieces):
    if len(pieces) == 1:
        return pieces[0]
    shape = pieces[0].shape
    return pl.pallas_call(
        stack_kernel,
        grid=(len(pieces),),
        in_specs=[pl.BlockSpec(shape, lambda i: (0, 0))] * len(pieces),
        out_specs=pl.BlockSpec(shape, lambda i: (i, 0)),
        out_shape=jax.ShapeDtypeStruct((len(pieces) * shape[0], shape[1]), pieces[0].dtype),
        compiler_params=pltpu.CompilerParams(vmem_limit_bytes=32 * 2**20),
        cost_estimate=cost(10**9, len(pieces)),
        name="stack",
    )(*pieces)


RELATIVE = (0, 2, 4, 6, 1, 3, 5, 7)


def place_of(own, index, parts):
    if parts != 8:
        return index
    relative = lax.bitwise_xor(own, index)
    return lax.bitwise_or(
        lax.shift_right_logical(relative, 1), lax.shift_left(lax.bitwise_and(relative, 1), 2)
    )


def hop(value, bit):
    return lax.ppermute(value, "ctx", [(i, i ^ bit) for i in range(lax.axis_size("ctx"))])


def halves_kernel(by_x_ref, by_y_ref, *refs):
    refs[-2][...] = by_x_ref[...]
    refs[-1][...] = by_y_ref[...]


def halves(by_x, by_y, before):
    rows, width = by_x.shape
    half = (rows // 2, width)
    return pl.pallas_call(
        halves_kernel,
        grid=(1,),
        in_specs=[pl.BlockSpec(half, lambda i: (0, 0)), pl.BlockSpec(half, lambda i: (1, 0))]
        + [pl.BlockSpec(memory_space=pl.ANY)] * len(before),
        out_specs=[pl.BlockSpec(half, lambda i: (0, 0))] * 2,
        out_shape=[jax.ShapeDtypeStruct(half, by_x.dtype)] * 2,
        cost_estimate=cost(10**9, 1),
        name="halves",
    )(by_x, by_y, *before)


def gather_pieces(value, middle=()):
    if lax.axis_size("ctx") != 8:
        whole = lax.all_gather(value, "ctx", axis=0, tiled=True)
        return (whole,), (whole,)
    by_x, by_y = hop(value, 2), hop(value, 4)
    first, second = halves(by_x, by_y, middle)
    far = stack((hop(first, 4), hop(second, 2)))
    others = [hop(piece, 1) for piece in (value, by_x, by_y)]
    return (value, by_x, by_y, far, *others, hop(far, 1)), (by_x, by_y)


def partial_products(product, tokens, before=()):
    parts = lax.axis_size("ctx")
    if parts != 8:
        return product(0, parts, [(parts * tokens, bf16)], None, before)
    half = (tokens // 2, bf16)
    near_other, far_other = product(4, 4, [(3 * tokens, bf16), (tokens, bf16)], None, before)
    far_other = hop(far_other, 1)
    near_other = after(near_other, far_other)
    far = product(3, 1, [half] * 2, far_other, ())
    own, *near = product(
        0, 3, [(tokens, f32)] + [(tokens, bf16)] * 2, hop(near_other, 1), (far[0],)
    )
    return (own, *near, *far)


def far_step(sums, far_after=(), near_after=()):
    if lax.axis_size("ctx") != 8:
        return fence(sums, *far_after, *near_after) if far_after or near_after else sums
    own, *near, far_first, far_last = sums
    if far_after:
        far_first, far_last = fence((far_first, far_last), *far_after)
    if near_after:
        near = fence(near, *near_after)
    from_x, from_y = hop(far_first, 2), hop(far_last, 4)
    by_x, by_y = near
    rows = by_x.shape[0] // 2
    by_x = by_x + jnp.pad(from_y, ((rows, 0), (0, 0)))
    by_y = by_y + jnp.pad(from_x, ((0, rows), (0, 0)))
    return own, by_x, by_y


def near_hops(sums):
    if lax.axis_size("ctx") != 8:
        (whole,) = sums
        return (lax.psum_scatter(whole, "ctx", scatter_dimension=0, tiled=True),)
    own, by_x, by_y = sums
    return own, hop(by_x, 2), hop(by_y, 4)


def near_step(sums):
    return sum(part.astype(f32) for part in near_hops(sums))


def sum_everywhere(value):
    if lax.axis_size("ctx") != 8 or lax.axis_size("dp") != 4:
        return lax.psum(value, ("dp", "ctx"))
    value = value + hop(value, 1)
    value = value + (hop(value, 2) + hop(value, 4) + hop(value, 6))
    shifted = [
        lax.ppermute(value, "dp", [(i, i ^ bits) for i in range(4)]) for bits in (1, 2, 3)
    ]
    return (value + shifted[0]) + (shifted[1] + shifted[2])


def spread_columns(packed):
    rows, parts, columns = packed.shape
    return lax.all_to_all(
        packed.reshape(rows, parts * columns), "ctx", split_axis=1, concat_axis=0, tiled=True
    )


def gather_rows(block):
    return lax.all_gather(block, "dp", axis=0, tiled=True)


def scatter_rows(gradient):
    return lax.psum_scatter(gradient, "dp", scatter_dimension=0, tiled=True)


def collect_columns(block):
    return lax.all_to_all(block, "ctx", split_axis=0, concat_axis=0, tiled=True)


def place_units_kernel(first_ref, last_ref, *out_refs):
    units = first_ref.shape[1] // 3
    for which, out_ref in enumerate(out_refs):
        for half, ref in enumerate((first_ref, last_ref)):
            out_ref[:, half * units : (half + 1) * units] = ref[
                :, which * units : (which + 1) * units
            ].astype(f32)


def place_units(first, last, parts):
    rows, columns = first.shape[0] // parts, first.shape[1]
    units = columns // 3
    return pl.pallas_call(
        place_units_kernel,
        grid=(parts,),
        in_specs=[pl.BlockSpec((rows, columns), lambda i: (i, 0))] * 2,
        out_specs=[pl.BlockSpec((rows, 2 * units), lambda i: (0, i))] * 3,
        out_shape=[jax.ShapeDtypeStruct((rows, 2 * units * parts), f32)] * 3,
        compiler_params=pltpu.CompilerParams(vmem_limit_bytes=16 * 2**20),
        cost_estimate=cost(10**7, 800),
        name="place_units",
    )(first, last)


def place_heads_kernel(parts, share, block_ref, query_ref, key_ref, value_ref, out_ref):
    rows = query_ref.shape[0]
    width = query_ref.shape[1] // parts
    for part in range(parts):
        block = block_ref[part * rows : (part + 1) * rows, :].astype(f32)
        here = slice(part * width, (part + 1) * width)
        query_ref[:, here] = block[:, :width]
        out_ref[:, here] = block[:, width + 2 * HEAD_SIZE :]
        head = part // share
        for ref, start in ((key_ref, width), (value_ref, width + HEAD_SIZE)):
            columns = slice(head * HEAD_SIZE, (head + 1) * HEAD_SIZE)
            piece = block[:, start : start + HEAD_SIZE]
            ref[:, columns] = piece if part % share == 0 else ref[:, columns] + piece


def place_heads(block, parts, share):
    rows = block.shape[0] // parts
    width = (block.shape[1] - 2 * HEAD_SIZE) // 2 * parts
    whole = pl.BlockSpec(memory_space=pltpu.VMEM)
    shapes = [(rows, width), (rows, parts // share * HEAD_SIZE)]
    shapes += [shapes[1], shapes[0]]
    return pl.pallas_call(
        functools.partial(place_heads_kernel, parts, share),
        in_specs=[whole],
        out_specs=[whole] * 4,
        out_shape=[jax.ShapeDtypeStruct(shape, f32) for shape in shapes],
        compiler_params=pltpu.CompilerParams(vmem_limit_bytes=16 * 2**20),
        cost_estimate=cost(10**7, 400),
        name="place_heads",
    )(block)


def heads_to_columns(block, heads):
    return jnp.concatenate(
        [block[:, h * HEAD_SIZE : (h + 1) * HEAD_SIZE].T for h in range(heads)], axis=1
    )


def columns_to_heads(columns, heads, slots):
    return jnp.concatenate(
        [columns[:, h * slots : (h + 1) * slots].T for h in range(heads)], axis=1
    )


def columns_to_rows(columns, heads, slots):
    return jnp.concatenate(
        [columns[:, h * slots : (h + 1) * slots].T for h in range(heads)], axis=0
    )


def head_scale(raw):
    return lax.rsqrt(jnp.mean(raw * raw, axis=0, keepdims=True) + epsilon)


def prepare(raw, gain, cosine, sine):
    value = raw * head_scale(raw) * gain
    first, second = value[: HEAD_SIZE // 2], value[HEAD_SIZE // 2 :]
    return jnp.concatenate(
        [first * cosine - second * sine, second * cosine + first * sine], axis=0
    )


def prepare_back(gradient, raw, gain, cosine, sine):
    scale = head_scale(raw)
    unit = raw * scale
    first, second = gradient[: HEAD_SIZE // 2], gradient[HEAD_SIZE // 2 :]
    turned = jnp.concatenate(
        [first * cosine + second * sine, second * cosine - first * sine], axis=0
    )
    inside = turned * gain
    middle = jnp.mean(inside * unit, axis=0, keepdims=True)
    return scale * (inside - unit * middle), turned * unit


def fold(values):
    lanes = 128
    return sum(values[:, i : i + lanes] for i in range(0, values.shape[1], lanes))


def repeated(table, heads):
    return jnp.concatenate([table] * heads, axis=1)


def masked_scores(key_block, query_columns, start, query_block, slots, length):
    scores = dot_nn(key_block, query_columns)
    key_pos = start + lax.broadcasted_iota(jnp.int32, scores.shape, 0)
    query_pos = query_block * slots + lax.rem(
        lax.broadcasted_iota(jnp.int32, scores.shape, 1), slots
    )
    return jnp.where((key_pos <= query_pos) & (key_pos < length), scores, -1e30)


def chunks_needed(query_block, slots, length, chunk):
    return lax.div(
        jnp.minimum((query_block + 1) * slots, length) + (chunk - 1), jnp.int32(chunk)
    )


def attend_kernel(
    row, blocks, slots, heads, chunk,
    base_ref, len_ref, q_ref, kv_ref, qg_ref, kg_ref, cos_ref, sin_ref,
    *refs,
):
    o_ref, lse_ref, k_all, v_t = refs[-4:]
    query_block = pl.program_id(0)
    base, length = base_ref[0], len_ref[row]

    @pl.when(query_block == 0)
    def _():
        for j in range(blocks):
            at = place_of(base, jnp.int32(j), blocks)
            here = slice(j * slots, (j + 1) * slots)
            both = kv_ref[at, 0].T
            keys = prepare(both[:HEAD_SIZE], kg_ref[...], cos_ref[:, here], sin_ref[:, here])
            k_all[here, :] = keys.T.astype(bf16)
            v_t[:, here] = both[HEAD_SIZE:].astype(bf16)

    count = chunks_needed(query_block, slots, length, chunk)
    here = pl.ds(pl.multiple_of(query_block * slots, slots), slots)
    queries = prepare(
        heads_to_columns(q_ref[0, 0], heads),
        qg_ref[...],
        repeated(cos_ref[:, here], heads),
        repeated(sin_ref[:, here], heads),
    )
    queries = queries.astype(bf16) * FACTOR
    columns = heads * slots

    def step(j, carry):
        top, total, accum = carry
        start = pl.multiple_of(j * chunk, chunk)
        scores = masked_scores(
            k_all[pl.ds(start, chunk), :], queries, start, query_block, slots, length
        )
        new_top = jnp.maximum(top, jnp.max(scores, axis=0, keepdims=True))
        probs = jnp.exp(scores - new_top)
        alpha = jnp.exp(top - new_top)
        total = total * alpha + jnp.sum(probs, axis=0, keepdims=True)
        accum = accum * alpha + dot_nn(v_t[:, pl.ds(start, chunk)], probs.astype(bf16))
        return new_top, total, accum

    top, total, accum = lax.fori_loop(
        0,
        count,
        step,
        (
            jnp.full((1, columns), -1e30, f32),
            jnp.zeros((1, columns), f32),
            jnp.zeros((HEAD_SIZE, columns), f32),
        ),
    )
    o_ref[0, 0] = columns_to_heads(accum / total, heads, slots).astype(bf16)
    lse_ref[0, 0] = top + jnp.log(total)


def attend_back_kernel(
    row, blocks, slots, heads, chunk,
    base_ref, len_ref, q_ref, kv_ref, qg_ref, kg_ref, cos_ref, sin_ref, o_ref, do_ref, lse_ref,
    *refs,
):
    dq_ref, dkv_ref, dqg_ref, dkg_ref, k_all, v_all, k_t, dk_all, dv_all = refs[-9:]
    query_block = pl.program_id(0)
    base, length = base_ref[0], len_ref[row]

    @pl.when(query_block == 0)
    def _():
        dqg_ref[...] = jnp.zeros_like(dqg_ref)
        dkg_ref[...] = jnp.zeros_like(dkg_ref)
        for j in range(blocks):
            at = place_of(base, jnp.int32(j), blocks)
            here = slice(j * slots, (j + 1) * slots)
            both = kv_ref[at, 0]
            keys = prepare(both.T[:HEAD_SIZE], kg_ref[...], cos_ref[:, here], sin_ref[:, here])
            k_t[:, here] = keys.astype(bf16)
            k_all[here, :] = keys.T.astype(bf16)
            v_all[here, :] = both[:, HEAD_SIZE:].astype(bf16)
        dk_all[...] = jnp.zeros_like(dk_all)
        dv_all[...] = jnp.zeros_like(dv_all)

    count = chunks_needed(query_block, slots, length, chunk)
    here = pl.ds(pl.multiple_of(query_block * slots, slots), slots)
    cosine, sine = repeated(cos_ref[:, here], heads), repeated(sin_ref[:, here], heads)
    raw = heads_to_columns(q_ref[0, 0], heads)
    queries = prepare(raw, qg_ref[...], cosine, sine).astype(bf16) * FACTOR
    query_rows = columns_to_rows(queries.astype(f32), heads, slots).astype(bf16)
    gradient = heads_to_columns(do_ref[0, 0].astype(f32), heads)
    grad_rows = columns_to_rows(gradient, heads, slots).astype(bf16)
    delta = jnp.sum(
        gradient * heads_to_columns(o_ref[0, 0].astype(f32), heads), axis=0, keepdims=True
    )
    gradient = gradient.astype(bf16)
    log_total = lse_ref[0, 0]

    def step(j, dq_t):
        start = pl.multiple_of(j * chunk, chunk)
        at = pl.ds(start, chunk)
        scores = masked_scores(k_all[at, :], queries, start, query_block, slots, length)
        probs = jnp.exp(scores - log_total)
        grad_probs = dot_nn(v_all[at, :], gradient)
        grad_scores = (probs * (grad_probs - delta)).astype(bf16)
        dv_all[at, :] += dot_nn(probs.astype(bf16), grad_rows)
        dk_all[at, :] += dot_nn(grad_scores, query_rows)
        return dq_t + dot_nn(k_t[:, at], grad_scores)

    dq_t = lax.fori_loop(0, count, step, jnp.zeros((HEAD_SIZE, heads * slots), f32))
    raw_term, gain_term = prepare_back(dq_t * FACTOR, raw, qg_ref[...], cosine, sine)
    dq_ref[0, 0] = columns_to_heads(raw_term, heads, slots).astype(bf16)
    dqg_ref[...] += fold(gain_term)

    @pl.when(query_block == blocks - 1)
    def _():
        for j in range(blocks):
            at = place_of(base, jnp.int32(j), blocks)
            here = slice(j * slots, (j + 1) * slots)
            raw_term, gain_term = prepare_back(
                dk_all[here, :].T,
                kv_ref[at, 0].T[:HEAD_SIZE],
                kg_ref[...],
                cos_ref[:, here],
                sin_ref[:, here],
            )
            dkg_ref[...] += fold(gain_term)
            dkv_ref[at, 0] = jnp.concatenate([raw_term.T, dv_all[here, :]], axis=1).astype(bf16)


def attention_specs(row, blocks, slots, width, total):
    own = lambda i, base, lens: (place_of(base[0], i, blocks), row, 0, 0)
    constant = lambda i, base, lens: (0, 0)
    both = 2 * HEAD_SIZE
    return (
        pl.BlockSpec((1, 1, slots, width), own),
        pl.BlockSpec((blocks, 1, slots, both), lambda i, base, lens: (0, row, 0, width // both)),
        pl.BlockSpec((blocks, 1, slots, both), lambda i, base, lens: (0, row, 0, 0)),
        pl.BlockSpec((HEAD_SIZE, 1), constant),
        pl.BlockSpec((HEAD_SIZE // 2, total), constant),
        pl.BlockSpec((1, 1, 1, width // HEAD_SIZE * slots), own),
        pl.BlockSpec((HEAD_SIZE, 128), constant),
    )


def attend(row, previous, base, lengths, raw, query_gain, key_gain, cosine, sine):
    blocks, rows, slots, columns = raw.shape
    width = columns - 2 * HEAD_SIZE
    heads = width // HEAD_SIZE
    total = blocks * slots
    query_spec, raw_key_spec, _, gain_spec, table_spec, lse_spec, _ = attention_specs(
        row, blocks, slots, width, total
    )
    operands = (base, lengths, raw, raw, query_gain, key_gain, cosine, sine)
    return pl.pallas_call(
        functools.partial(attend_kernel, row, blocks, slots, heads, 2 * slots),
        grid_spec=pltpu.PrefetchScalarGridSpec(
            num_scalar_prefetch=2,
            grid=(blocks,),
            in_specs=[query_spec, raw_key_spec, gain_spec, gain_spec, table_spec, table_spec]
            + [pl.BlockSpec(memory_space=pl.ANY)] * len(previous),
            out_specs=[query_spec, lse_spec],
            scratch_shapes=[
                pltpu.VMEM((total, HEAD_SIZE), bf16),
                pltpu.VMEM((HEAD_SIZE, total), bf16),
            ],
        ),
        out_shape=[
            jax.ShapeDtypeStruct((blocks, rows, slots, width), bf16),
            jax.ShapeDtypeStruct((blocks, rows, 1, heads * slots), f32),
        ],
        input_output_aliases={len(operands) + i: i for i in range(len(previous))},
        compiler_params=pltpu.CompilerParams(vmem_limit_bytes=32 * 2**20),
        cost_estimate=cost(2 * HEAD_SIZE * heads * total * total, 24),
        name="attend",
    )(*operands, *previous)


def attend_back(
    row, previous, base, lengths, raw, query_gain, key_gain, cosine, sine, attended, gradient, log_total
):
    blocks, rows, slots, columns = raw.shape
    width = columns - 2 * HEAD_SIZE
    heads = width // HEAD_SIZE
    total = blocks * slots
    query_spec, raw_key_spec, key_spec, gain_spec, table_spec, lse_spec, sum_spec = (
        attention_specs(row, blocks, slots, width, total)
    )
    operands = (base, lengths, raw, raw, query_gain, key_gain, cosine, sine)
    operands += (attended, gradient, log_total)
    return pl.pallas_call(
        functools.partial(attend_back_kernel, row, blocks, slots, heads, 2 * slots),
        grid_spec=pltpu.PrefetchScalarGridSpec(
            num_scalar_prefetch=2,
            grid=(blocks,),
            in_specs=[query_spec, raw_key_spec, gain_spec, gain_spec, table_spec, table_spec]
            + [query_spec, query_spec, lse_spec]
            + [pl.BlockSpec(memory_space=pl.ANY)] * len(previous),
            out_specs=[query_spec, key_spec, sum_spec, sum_spec],
            scratch_shapes=[
                pltpu.VMEM((total, HEAD_SIZE), bf16),
                pltpu.VMEM((total, HEAD_SIZE), bf16),
                pltpu.VMEM((HEAD_SIZE, total), bf16),
                pltpu.VMEM((total, HEAD_SIZE), f32),
                pltpu.VMEM((total, HEAD_SIZE), f32),
            ],
        ),
        out_shape=[
            jax.ShapeDtypeStruct((blocks, rows, slots, width), bf16),
            jax.ShapeDtypeStruct((blocks, rows, slots, 2 * HEAD_SIZE), bf16),
            jax.ShapeDtypeStruct((HEAD_SIZE, 128), f32),
            jax.ShapeDtypeStruct((HEAD_SIZE, 128), f32),
        ],
        input_output_aliases={len(operands) + i: i for i in range(len(previous))},
        compiler_params=pltpu.CompilerParams(vmem_limit_bytes=32 * 2**20),
        cost_estimate=cost(5 * HEAD_SIZE * heads * total * total, 16),
        name="attend_back",
    )(*operands, *previous)


def feed_kernel(hidden_ref, cotangent_ref, weight_ref, inner_ref, grad_ref):
    units = inner_ref.shape[1]
    hidden = hidden_ref[...]
    gate = dot_nn(hidden, weight_ref[:, :units])
    upward = dot_nn(hidden, weight_ref[:, units : 2 * units])
    grad_inner = dot_nn(cotangent_ref[...], weight_ref[:, 2 * units :])
    sigmoid_gate = jax.nn.sigmoid(gate)
    silu_gate = gate * sigmoid_gate
    inner_ref[...] = (silu_gate * upward).astype(bf16)
    grad_ref[:, :units] = (
        grad_inner * upward * sigmoid_gate * (1.0 + gate * (1.0 - sigmoid_gate))
    ).astype(bf16)
    grad_ref[:, units:] = (grad_inner * silu_gate).astype(bf16)


def feed_forward(hidden, cotangents, weights):
    count, width = hidden.shape
    units = weights.shape[1] // 3
    tile = 512
    rows = pl.BlockSpec((tile, width), lambda i: (i, 0))
    return pl.pallas_call(
        feed_kernel,
        grid=(count // tile,),
        in_specs=[rows, rows, pl.BlockSpec(weights.shape, lambda i: (0, 0))],
        out_specs=[
            pl.BlockSpec((tile, units), lambda i: (i, 0)),
            pl.BlockSpec((tile, 2 * units), lambda i: (i, 0)),
        ],
        out_shape=[
            jax.ShapeDtypeStruct((count, units), bf16),
            jax.ShapeDtypeStruct((count, 2 * units), bf16),
        ],
        compiler_params=pltpu.CompilerParams(vmem_limit_bytes=48 * 2**20),
        cost_estimate=cost(6 * count * width * units, 1.7),
        name="feed_forward",
    )(hidden, cotangents, weights)


def feed_gradient_kernel(hidden_ref, cotangent_ref, grad_ref, inner_ref, out_ref):
    split = grad_ref.shape[1]
    out_ref[:, :split] = dot_tn(hidden_ref[...], grad_ref[...]).astype(bf16)
    out_ref[:, split:] = dot_tn(cotangent_ref[...], inner_ref[...]).astype(bf16)


def feed_gradient(hidden, cotangents, grad, inner):
    count, width = hidden.shape
    tile = 256
    columns = pl.BlockSpec((count, tile), lambda i: (0, i))
    total = grad.shape[1] + inner.shape[1]
    return pl.pallas_call(
        feed_gradient_kernel,
        grid=(width // tile,),
        in_specs=[columns, columns]
        + [pl.BlockSpec(v.shape, lambda i: (0, 0)) for v in (grad, inner)],
        out_specs=pl.BlockSpec((tile, total), lambda i: (i, 0)),
        out_shape=jax.ShapeDtypeStruct((width, total), bf16),
        compiler_params=pltpu.CompilerParams(vmem_limit_bytes=48 * 2**20),
        cost_estimate=cost(2 * count * width * total, 1.6),
        name="feed_gradient",
    )(hidden, cotangents, grad, inner)


def product_kernel(count, adds, outs, *refs):
    rows, weights, rest = refs[:count], refs[count : 2 * count], refs[2 * count : 2 * count + adds]
    total = sum(dot_nt(r[...], w[...]) for r, w in zip(rows, weights))
    for add_ref in rest:
        total += add_ref[...].astype(f32)
    start = 0
    for out_ref in refs[-outs:]:
        out_ref[...] = total[start : start + out_ref.shape[0]].astype(out_ref.dtype)
        start += out_ref.shape[0]


def sum_of_products(share, lefts, weights, column, tokens, first, count, splits, add, before):
    rows = count * tokens
    width = weights[0].shape[0]
    tile = 512
    operands = list(lefts) + list(weights)
    specs = [pl.BlockSpec((rows, v.shape[1]), lambda i: (first // count, 0)) for v in lefts] + [
        pl.BlockSpec((tile, v.shape[1]), lambda i: (i, column)) for v in lefts
    ]
    if add is not None:
        operands.append(add)
        specs.append(pl.BlockSpec((rows, tile), lambda i: (0, i)))
    operands += before
    specs += [pl.BlockSpec(memory_space=pl.ANY)] * len(before)
    return pl.pallas_call(
        functools.partial(product_kernel, len(lefts), int(add is not None), len(splits)),
        grid=(width // tile,),
        in_specs=specs,
        out_specs=[pl.BlockSpec((r, tile), lambda i: (0, i)) for r, _ in splits],
        out_shape=[jax.ShapeDtypeStruct((r, width), dtype) for r, dtype in splits],
        compiler_params=pltpu.CompilerParams(vmem_limit_bytes=48 * 2**20),
        cost_estimate=cost(2 * rows * width * sum(v.shape[1] for v in lefts), share),
        name="sum_of_products",
    )(*operands)


def body(
    inputs,
    lengths,
    attention_gain,
    query_weight,
    key_matrix,
    value_matrix,
    out_weight,
    query_gain,
    key_gain,
    feedforward_gain,
    gate_weight,
    up_weight,
    down_weight,
    cotangent,
):
    rows, slots, width = inputs.shape
    tokens = rows * slots
    parts = lax.axis_size("ctx")
    heads = QUERY_HEADS_TOTAL // parts
    share = parts // KEY_VALUE_HEADS
    query_cols = heads * HEAD_SIZE
    weight_rows = query_weight.shape[0]
    feed = gate_weight.shape[1] // parts
    all_tokens = parts * tokens
    base = lax.axis_index("ctx").astype(jnp.int32)

    qkv_pack = jnp.concatenate(
        [query_weight.reshape(weight_rows, parts, query_cols)]
        + [
            jnp.repeat(w.reshape(weight_rows, KEY_VALUE_HEADS, HEAD_SIZE), share, axis=1)
            for w in (key_matrix, value_matrix)
        ],
        axis=2,
    )
    qkv_block = spread_columns(qkv_pack)
    out_block = spread_columns(out_weight.reshape(weight_rows, parts, query_cols))
    units = feed // 2
    feed_packs = [
        jnp.concatenate(
            [
                w.reshape(weight_rows, parts, feed)[:, :, start : start + units]
                for w in (gate_weight, up_weight, down_weight)
            ],
            axis=2,
        )
        for start in (0, units)
    ]
    flat = inputs.reshape(tokens, width).astype(f32)
    first_scale = rms_scale(flat)
    normed = flat * first_scale
    hidden_pieces, hidden_start = gather_pieces((normed * attention_gain).astype(bf16))
    hidden = stack(hidden_pieces)
    first_block = spread_columns(after(feed_packs[0], out_block, *hidden_start))
    qkv_full = gather_rows(qkv_block)
    out_full = gather_rows(out_block)
    first_full = gather_rows(first_block)

    raw = jnp.concatenate([dot_nn(piece, qkv_full) for piece in hidden_pieces], axis=0)
    cotangent_flat = cotangent.reshape(tokens, width)
    cotangent_pieces, cotangents_start = gather_pieces(after(cotangent_flat, first_block))
    cotangents = stack(cotangent_pieces)
    raw = after(raw, *cotangents_start).reshape(parts, rows, slots, query_cols + 2 * HEAD_SIZE)
    last_block = spread_columns(after(feed_packs[1], *cotangents_start))
    cosine, sine = [
        t.T for t in rotary_tables(jnp.arange(parts * slots, dtype=jnp.int32), HEAD_SIZE)
    ]
    base_array = base.reshape(1)
    gains = [g.astype(f32).reshape(HEAD_SIZE, 1) for g in (query_gain, key_gain)]
    results = ()
    for row in range(rows):
        if row == rows - 1:
            results = fence(results, last_block) if results else results
        results = attend(row, results, base_array, lengths, raw, *gains, cosine, sine)
    attended, log_total = results
    attended_rows = attended.reshape(all_tokens, query_cols)
    sums = partial_products(
        functools.partial(sum_of_products, 2.4, [attended_rows], [out_full], 0, tokens), tokens
    )
    mixed = flat + near_step(far_step(sums, (), cotangent_pieces[-1:]))

    second_scale = rms_scale(mixed)
    normed_again = mixed * second_scale
    pieces, _ = gather_pieces((normed_again * feedforward_gain).astype(bf16))
    hidden_again = after(stack(pieces), first_full)
    last_full = gather_rows(after(last_block, first_full))
    fulls = [first_full, last_full]
    inners, grads, partials = [], [], []
    for which in range(2):
        if which == 1:
            fulls[1] = after(last_full, partials[0])
        inner, grad = feed_forward(hidden_again, cotangents, fulls[which])
        inners.append(inner)
        grads.append(grad)
        partials.append(feed_gradient(hidden_again, cotangents, grad, inner))
    first_gradient = scatter_rows(partials[0])
    last_gradient = scatter_rows(after(partials[1], first_gradient))
    sums = partial_products(
        functools.partial(sum_of_products, 0, grads, fulls, 0, tokens), tokens
    )
    feed_sums = partial_products(
        functools.partial(sum_of_products, 2.4, inners, fulls, 2, tokens), tokens, (sums[0],)
    )
    grad_hidden_again = after(near_step(far_step(sums)), feed_sums[-1])
    feedforward_gain_local = jnp.sum(grad_hidden_again * normed_again, axis=0)
    scaled_again = grad_hidden_again * feedforward_gain
    grad_mixed = cotangent_flat.astype(f32) + second_scale * (
        scaled_again - normed_again * jnp.mean(scaled_again * normed_again, axis=-1, keepdims=True)
    )

    pieces, _ = gather_pieces(grad_mixed.astype(bf16), (feed_sums[0], first_gradient))
    grad_branch = stack(pieces)
    attended_gradient = jnp.concatenate(
        [dot_nn(piece, out_full).astype(bf16) for piece in pieces], axis=0
    )
    first_collected = collect_columns(after(first_gradient, attended_gradient))
    feed_sums = far_step(feed_sums, (attended_gradient,))
    feed_parts = near_hops(feed_sums)
    feed_out = sum(part.astype(f32) for part in feed_parts)
    outputs = (mixed + feed_out).astype(bf16).reshape(rows, slots, width)
    attended_gradient = attended_gradient.reshape(parts, rows, slots, query_cols)
    grad_queries_keys_values, gain_sums = (), []
    for row in range(rows):
        if row == rows - 1 and grad_queries_keys_values:
            grad_queries_keys_values = fence(
                grad_queries_keys_values, first_collected, *feed_sums[1:]
            )
        *grad_queries_keys_values, query_gain_sums, key_gain_sums = attend_back(
            row,
            tuple(grad_queries_keys_values),
            base_array,
            lengths,
            raw,
            *gains,
            cosine,
            sine,
            attended,
            attended_gradient,
            log_total,
        )
        gain_sums.append((query_gain_sums, key_gain_sums))
    grad_queries, grad_keys_values = grad_queries_keys_values
    query_gain_sums, key_gain_sums = [sum(g) for g in zip(*gain_sums)]
    query_gain_local, key_gain_local = query_gain_sums.sum(axis=1), key_gain_sums.sum(axis=1)
    grad_raw = jnp.concatenate(
        [
            grad_queries.reshape(all_tokens, query_cols),
            grad_keys_values.reshape(all_tokens, 2 * HEAD_SIZE),
        ],
        axis=1,
    )
    grad_raw = after(grad_raw, *feed_parts[1:])
    attention_partial = jnp.concatenate(
        [dot_tn(hidden, grad_raw), dot_tn(grad_branch, after(attended_rows, grad_raw))], axis=1
    ).astype(bf16)
    attention_gradient = scatter_rows(after(attention_partial, last_gradient))
    attention_collected = collect_columns(attention_gradient)
    query_weight_gradient, key_weight_gradient, value_weight_gradient, out_weight_gradient = (
        place_heads(attention_collected, parts, share)
    )
    sums = partial_products(
        functools.partial(sum_of_products, 2.4, [grad_raw], [qkv_full], 0, tokens),
        tokens,
        (attention_partial,),
    )
    last_collected = collect_columns(last_gradient)
    grad_hidden = near_step(far_step(sums, (feed_out, last_collected), (feed_out,)))
    gate_weight_gradient, up_weight_gradient, down_weight_gradient = place_units(
        first_collected, last_collected, parts
    )
    grad_hidden = after(grad_hidden, attention_gradient)

    attention_gain_local = jnp.sum(grad_hidden * normed, axis=0)
    scaled_first = grad_hidden * attention_gain
    input_gradient = (
        grad_mixed
        + first_scale
        * (scaled_first - normed * jnp.mean(scaled_first * normed, axis=-1, keepdims=True))
    ).astype(bf16)
    gain_sums = sum_everywhere(
        after(
            jnp.concatenate(
                [attention_gain_local, feedforward_gain_local, query_gain_local, key_gain_local]
            ),
            attention_collected,
        )
    )
    attention_gain_gradient, feedforward_gain_gradient = gain_sums[:width], gain_sums[width : 2 * width]
    query_gain_gradient = gain_sums[2 * width : 2 * width + HEAD_SIZE]
    key_gain_gradient = gain_sums[2 * width + HEAD_SIZE :]
    return (
        outputs,
        input_gradient.reshape(rows, slots, width),
        attention_gain_gradient,
        query_weight_gradient,
        key_weight_gradient,
        value_weight_gradient,
        out_weight_gradient,
        query_gain_gradient,
        key_gain_gradient,
        feedforward_gain_gradient,
        gate_weight_gradient,
        up_weight_gradient,
        down_weight_gradient,
    )


def solution(mesh):
    weight = P(("dp", "ctx"), None)
    token = P("dp", "ctx", None)
    placed = (
        token, P("dp"), P(), weight, weight, weight, weight, P(), P(), P(), weight, weight, weight, token,
    )
    returned = (
        token, token, P(), weight, weight, weight, weight, P(), P(), P(), weight, weight, weight,
    )
    return jax.shard_map(
        body, mesh=mesh, in_specs=placed, out_specs=returned, check_vma=False
    )
```

```python
import functools

import jax
import jax.numpy as jnp
from jax import lax
from jax.experimental import pallas as pl
from jax.experimental.pallas import tpu as pltpu
from jax.sharding import PartitionSpec as P

QUERY_HEADS_TOTAL = 32
KEY_VALUE_HEADS = 8
HEAD_SIZE = 64
FACTOR = HEAD_SIZE ** (-0.5)

NO_COST = pl.CostEstimate(flops=0, bytes_accessed=0, transcendentals=0)


def cost(flops, share):
    return pl.CostEstimate(flops=int(flops * share), bytes_accessed=0, transcendentals=0)


epsilon = 1e-06
f32 = jnp.float32
bf16 = jnp.bfloat16


def rms_scale(value_rows):
    return lax.rsqrt(jnp.mean(value_rows * value_rows, axis=-1, keepdims=True) + epsilon)


def rotary_tables(positions, width):
    inverse = 10000.0 ** (-(jnp.arange(width // 2, dtype=f32) * 2.0) / width)
    angle_table = positions.astype(f32)[:, None] * inverse[None, :]
    return (jnp.cos(angle_table), jnp.sin(angle_table))


def dot_nn(left, right):
    return jnp.dot(left, right, preferred_element_type=f32)


def dot_tn(left, right):
    return lax.dot_general(left, right, (((0,), (0,)), ((), ())), preferred_element_type=f32)


def dot_nt(left, right):
    return lax.dot_general(left, right, (((1,), (1,)), ((), ())), preferred_element_type=f32)


def fence(values, *earlier):
    count = len(values)
    anywhere = pl.BlockSpec(memory_space=pl.ANY)
    return pl.pallas_call(
        lambda *refs: None,
        in_specs=[anywhere] * (count + len(earlier)),
        out_specs=[anywhere] * count,
        out_shape=[jax.ShapeDtypeStruct(v.shape, v.dtype) for v in values],
        input_output_aliases={i: i for i in range(count)},
        cost_estimate=NO_COST,
        name="fence",
    )(*values, *earlier)


def after(value, *earlier):
    return fence((value,), *earlier)[0]


def stack_kernel(*refs):
    for k, ref in enumerate(refs[:-1]):

        @pl.when(pl.program_id(0) == k)
        def _():
            refs[-1][...] = ref[...]


def stack(pieces):
    if len(pieces) == 1:
        return pieces[0]
    shape = pieces[0].shape
    return pl.pallas_call(
        stack_kernel,
        grid=(len(pieces),),
        in_specs=[pl.BlockSpec(shape, lambda i: (0, 0))] * len(pieces),
        out_specs=pl.BlockSpec(shape, lambda i: (i, 0)),
        out_shape=jax.ShapeDtypeStruct((len(pieces) * shape[0], shape[1]), pieces[0].dtype),
        compiler_params=pltpu.CompilerParams(vmem_limit_bytes=32 * 2**20),
        cost_estimate=cost(10**9, len(pieces)),
        name="stack",
    )(*pieces)


RELATIVE = (0, 2, 4, 6, 1, 3, 5, 7)


def place_of(own, index, parts):
    if parts != 8:
        return index
    relative = lax.bitwise_xor(own, index)
    return lax.bitwise_or(
        lax.shift_right_logical(relative, 1), lax.shift_left(lax.bitwise_and(relative, 1), 2)
    )


def hop(value, bit):
    return lax.ppermute(value, "ctx", [(i, i ^ bit) for i in range(lax.axis_size("ctx"))])


def halves_kernel(by_x_ref, by_y_ref, *refs):
    refs[-2][...] = by_x_ref[...]
    refs[-1][...] = by_y_ref[...]


def halves(by_x, by_y, before):
    rows, width = by_x.shape
    half = (rows // 2, width)
    return pl.pallas_call(
        halves_kernel,
        grid=(1,),
        in_specs=[pl.BlockSpec(half, lambda i: (0, 0)), pl.BlockSpec(half, lambda i: (1, 0))]
        + [pl.BlockSpec(memory_space=pl.ANY)] * len(before),
        out_specs=[pl.BlockSpec(half, lambda i: (0, 0))] * 2,
        out_shape=[jax.ShapeDtypeStruct(half, by_x.dtype)] * 2,
        cost_estimate=cost(10**9, 1),
        name="halves",
    )(by_x, by_y, *before)


def gather_pieces(value, middle=()):
    if lax.axis_size("ctx") != 8:
        whole = lax.all_gather(value, "ctx", axis=0, tiled=True)
        return (whole,), (whole,)
    by_x, by_y = hop(value, 2), hop(value, 4)
    first, second = halves(by_x, by_y, middle)
    far = stack((hop(first, 4), hop(second, 2)))
    others = [hop(piece, 1) for piece in (value, by_x, by_y)]
    return (value, by_x, by_y, far, *others, hop(far, 1)), (by_x, by_y)


def partial_products(product, tokens, before=()):
    parts = lax.axis_size("ctx")
    if parts != 8:
        return product(0, parts, [(parts * tokens, bf16)], None, before)
    half = (tokens // 2, bf16)
    near_other, far_other = product(4, 4, [(3 * tokens, bf16), (tokens, bf16)], None, before)
    far_other = hop(far_other, 1)
    near_other = after(near_other, far_other)
    far = product(3, 1, [half] * 2, far_other, ())
    own, *near = product(
        0, 3, [(tokens, f32)] + [(tokens, bf16)] * 2, hop(near_other, 1), (far[0],)
    )
    return (own, *near, *far)


def far_hops(sums, far_after=()):
    if lax.axis_size("ctx") != 8:
        return ()
    far_first, far_last = sums[3:]
    if far_after:
        far_first, far_last = fence((far_first, far_last), *far_after)
    return hop(far_first, 2), hop(far_last, 4)


def far_add(sums, arrived, near_after=()):
    if lax.axis_size("ctx") != 8:
        return fence(sums, *near_after) if near_after else sums
    own, by_x, by_y = sums[:3]
    if near_after:
        by_x, by_y = fence((by_x, by_y), *near_after)
    from_x, from_y = arrived
    rows = by_x.shape[0] // 2
    by_x = by_x + jnp.pad(from_y, ((rows, 0), (0, 0)))
    by_y = by_y + jnp.pad(from_x, ((0, rows), (0, 0)))
    return own, by_x, by_y


def far_step(sums, far_after=(), near_after=()):
    return far_add(sums, far_hops(sums, far_after), near_after)


def near_hops(sums):
    if lax.axis_size("ctx") != 8:
        (whole,) = sums
        return (lax.psum_scatter(whole, "ctx", scatter_dimension=0, tiled=True),)
    own, by_x, by_y = sums
    return own, hop(by_x, 2), hop(by_y, 4)


def near_step(sums):
    return sum(part.astype(f32) for part in near_hops(sums))


def sum_everywhere(value):
    if lax.axis_size("ctx") != 8 or lax.axis_size("dp") != 4:
        return lax.psum(value, ("dp", "ctx"))
    value = value + hop(value, 1)
    value = value + (hop(value, 2) + hop(value, 4) + hop(value, 6))
    shifted = [
        lax.ppermute(value, "dp", [(i, i ^ bits) for i in range(4)]) for bits in (1, 2, 3)
    ]
    return (value + shifted[0]) + (shifted[1] + shifted[2])


def spread_columns(packed):
    rows, parts, columns = packed.shape
    return lax.all_to_all(
        packed.reshape(rows, parts * columns), "ctx", split_axis=1, concat_axis=0, tiled=True
    )


def gather_rows(block):
    return lax.all_gather(block, "dp", axis=0, tiled=True)


def scatter_rows(gradient):
    return lax.psum_scatter(gradient, "dp", scatter_dimension=0, tiled=True)


def collect_columns(block):
    return lax.all_to_all(block, "ctx", split_axis=0, concat_axis=0, tiled=True)


def place_units_kernel(first_ref, last_ref, *out_refs):
    for which, out_ref in enumerate(out_refs):
        start = 0
        for ref in (first_ref, last_ref):
            units = ref.shape[1] // 3
            out_ref[:, start : start + units] = ref[
                :, which * units : (which + 1) * units
            ].astype(f32)
            start += units


def place_units(first, last, parts):
    rows = first.shape[0] // parts
    units = (first.shape[1] + last.shape[1]) // 3
    return pl.pallas_call(
        place_units_kernel,
        grid=(parts,),
        in_specs=[pl.BlockSpec((rows, v.shape[1]), lambda i: (i, 0)) for v in (first, last)],
        out_specs=[pl.BlockSpec((rows, units), lambda i: (0, i))] * 3,
        out_shape=[jax.ShapeDtypeStruct((rows, units * parts), f32)] * 3,
        compiler_params=pltpu.CompilerParams(vmem_limit_bytes=16 * 2**20),
        cost_estimate=cost(10**7, 800),
        name="place_units",
    )(first, last)


def place_heads_kernel(parts, share, block_ref, query_ref, key_ref, value_ref, out_ref):
    rows = query_ref.shape[0]
    width = query_ref.shape[1] // parts
    for part in range(parts):
        block = block_ref[part * rows : (part + 1) * rows, :].astype(f32)
        here = slice(part * width, (part + 1) * width)
        query_ref[:, here] = block[:, :width]
        out_ref[:, here] = block[:, width + 2 * HEAD_SIZE :]
        head = part // share
        for ref, start in ((key_ref, width), (value_ref, width + HEAD_SIZE)):
            columns = slice(head * HEAD_SIZE, (head + 1) * HEAD_SIZE)
            piece = block[:, start : start + HEAD_SIZE]
            ref[:, columns] = piece if part % share == 0 else ref[:, columns] + piece


def place_heads(block, parts, share):
    rows = block.shape[0] // parts
    width = (block.shape[1] - 2 * HEAD_SIZE) // 2 * parts
    whole = pl.BlockSpec(memory_space=pltpu.VMEM)
    shapes = [(rows, width), (rows, parts // share * HEAD_SIZE)]
    shapes += [shapes[1], shapes[0]]
    return pl.pallas_call(
        functools.partial(place_heads_kernel, parts, share),
        in_specs=[whole],
        out_specs=[whole] * 4,
        out_shape=[jax.ShapeDtypeStruct(shape, f32) for shape in shapes],
        compiler_params=pltpu.CompilerParams(vmem_limit_bytes=16 * 2**20),
        cost_estimate=cost(10**7, 400),
        name="place_heads",
    )(block)


def heads_to_columns(block, heads):
    return jnp.concatenate(
        [block[:, h * HEAD_SIZE : (h + 1) * HEAD_SIZE].T for h in range(heads)], axis=1
    )


def columns_to_heads(columns, heads, slots):
    return jnp.concatenate(
        [columns[:, h * slots : (h + 1) * slots].T for h in range(heads)], axis=1
    )


def columns_to_rows(columns, heads, slots):
    return jnp.concatenate(
        [columns[:, h * slots : (h + 1) * slots].T for h in range(heads)], axis=0
    )


def head_scale(raw):
    return lax.rsqrt(jnp.mean(raw * raw, axis=0, keepdims=True) + epsilon)


def prepare(raw, gain, cosine, sine):
    value = raw * head_scale(raw) * gain
    first, second = value[: HEAD_SIZE // 2], value[HEAD_SIZE // 2 :]
    return jnp.concatenate(
        [first * cosine - second * sine, second * cosine + first * sine], axis=0
    )


def prepare_back(gradient, raw, gain, cosine, sine):
    scale = head_scale(raw)
    unit = raw * scale
    first, second = gradient[: HEAD_SIZE // 2], gradient[HEAD_SIZE // 2 :]
    turned = jnp.concatenate(
        [first * cosine + second * sine, second * cosine - first * sine], axis=0
    )
    inside = turned * gain
    middle = jnp.mean(inside * unit, axis=0, keepdims=True)
    return scale * (inside - unit * middle), turned * unit


def fold(values):
    lanes = 128
    return sum(values[:, i : i + lanes] for i in range(0, values.shape[1], lanes))


def repeated(table, heads):
    return jnp.concatenate([table] * heads, axis=1)


def masked_scores(key_block, query_columns, start, query_block, slots, length):
    scores = dot_nn(key_block, query_columns)
    key_pos = start + lax.broadcasted_iota(jnp.int32, scores.shape, 0)
    query_pos = query_block * slots + lax.rem(
        lax.broadcasted_iota(jnp.int32, scores.shape, 1), slots
    )
    return jnp.where((key_pos <= query_pos) & (key_pos < length), scores, -1e30)


def chunks_needed(query_block, slots, length, chunk):
    return lax.div(
        jnp.minimum((query_block + 1) * slots, length) + (chunk - 1), jnp.int32(chunk)
    )


def attend_kernel(
    row, blocks, slots, heads, chunk,
    base_ref, len_ref, q_ref, kv_ref, qg_ref, kg_ref, cos_ref, sin_ref,
    *refs,
):
    o_ref, lse_ref, k_all, v_t = refs[-4:]
    query_block = pl.program_id(0)
    base, length = base_ref[0], len_ref[row]

    @pl.when(query_block == 0)
    def _():
        for j in range(blocks):
            at = place_of(base, jnp.int32(j), blocks)
            here = slice(j * slots, (j + 1) * slots)
            both = kv_ref[at, 0].T
            keys = prepare(both[:HEAD_SIZE], kg_ref[...], cos_ref[:, here], sin_ref[:, here])
            k_all[here, :] = keys.T.astype(bf16)
            v_t[:, here] = both[HEAD_SIZE:].astype(bf16)

    count = chunks_needed(query_block, slots, length, chunk)
    here = pl.ds(pl.multiple_of(query_block * slots, slots), slots)
    queries = prepare(
        heads_to_columns(q_ref[0, 0], heads),
        qg_ref[...],
        repeated(cos_ref[:, here], heads),
        repeated(sin_ref[:, here], heads),
    )
    queries = queries.astype(bf16) * FACTOR
    columns = heads * slots

    def step(j, carry):
        top, total, accum = carry
        start = pl.multiple_of(j * chunk, chunk)
        scores = masked_scores(
            k_all[pl.ds(start, chunk), :], queries, start, query_block, slots, length
        )
        new_top = jnp.maximum(top, jnp.max(scores, axis=0, keepdims=True))
        probs = jnp.exp(scores - new_top)
        alpha = jnp.exp(top - new_top)
        total = total * alpha + jnp.sum(probs, axis=0, keepdims=True)
        accum = accum * alpha + dot_nn(v_t[:, pl.ds(start, chunk)], probs.astype(bf16))
        return new_top, total, accum

    top, total, accum = lax.fori_loop(
        0,
        count,
        step,
        (
            jnp.full((1, columns), -1e30, f32),
            jnp.zeros((1, columns), f32),
            jnp.zeros((HEAD_SIZE, columns), f32),
        ),
    )
    o_ref[0, 0] = columns_to_heads(accum / total, heads, slots).astype(bf16)
    lse_ref[0, 0] = top + jnp.log(total)


def attend_back_kernel(
    blocks, slots, heads, chunk,
    base_ref, len_ref, q_ref, kv_ref, qg_ref, kg_ref, cos_ref, sin_ref, o_ref, do_ref, lse_ref,
    dq_ref, dkv_ref, dqg_ref, dkg_ref, k_all, v_all, k_t, dk_all, dv_all,
):
    row, query_block = pl.program_id(0), pl.program_id(1)
    base, length = base_ref[0], len_ref[row]

    @pl.when((row == 0) & (query_block == 0))
    def _():
        dqg_ref[...] = jnp.zeros_like(dqg_ref)
        dkg_ref[...] = jnp.zeros_like(dkg_ref)

    @pl.when(query_block == 0)
    def _():
        for j in range(blocks):
            at = place_of(base, jnp.int32(j), blocks)
            here = slice(j * slots, (j + 1) * slots)
            both = kv_ref[at, 0]
            keys = prepare(both.T[:HEAD_SIZE], kg_ref[...], cos_ref[:, here], sin_ref[:, here])
            k_t[:, here] = keys.astype(bf16)
            k_all[here, :] = keys.T.astype(bf16)
            v_all[here, :] = both[:, HEAD_SIZE:].astype(bf16)
        dk_all[...] = jnp.zeros_like(dk_all)
        dv_all[...] = jnp.zeros_like(dv_all)

    count = chunks_needed(query_block, slots, length, chunk)
    here = pl.ds(pl.multiple_of(query_block * slots, slots), slots)
    cosine, sine = repeated(cos_ref[:, here], heads), repeated(sin_ref[:, here], heads)
    raw = heads_to_columns(q_ref[0, 0], heads)
    queries = prepare(raw, qg_ref[...], cosine, sine).astype(bf16) * FACTOR
    query_rows = columns_to_rows(queries.astype(f32), heads, slots).astype(bf16)
    gradient = heads_to_columns(do_ref[0, 0].astype(f32), heads)
    grad_rows = columns_to_rows(gradient, heads, slots).astype(bf16)
    delta = jnp.sum(
        gradient * heads_to_columns(o_ref[0, 0].astype(f32), heads), axis=0, keepdims=True
    )
    gradient = gradient.astype(bf16)
    log_total = lse_ref[0, 0]

    def step(j, dq_t):
        start = pl.multiple_of(j * chunk, chunk)
        at = pl.ds(start, chunk)
        scores = masked_scores(k_all[at, :], queries, start, query_block, slots, length)
        probs = jnp.exp(scores - log_total)
        grad_probs = dot_nn(v_all[at, :], gradient)
        grad_scores = (probs * (grad_probs - delta)).astype(bf16)
        dv_all[at, :] += dot_nn(probs.astype(bf16), grad_rows)
        dk_all[at, :] += dot_nn(grad_scores, query_rows)
        return dq_t + dot_nn(k_t[:, at], grad_scores)

    dq_t = lax.fori_loop(0, count, step, jnp.zeros((HEAD_SIZE, heads * slots), f32))
    raw_term, gain_term = prepare_back(dq_t * FACTOR, raw, qg_ref[...], cosine, sine)
    dq_ref[0, 0] = columns_to_heads(raw_term, heads, slots).astype(bf16)
    dqg_ref[...] += fold(gain_term)

    @pl.when(query_block == blocks - 1)
    def _():
        for j in range(blocks):
            at = place_of(base, jnp.int32(j), blocks)
            here = slice(j * slots, (j + 1) * slots)
            raw_term, gain_term = prepare_back(
                dk_all[here, :].T,
                kv_ref[at, 0].T[:HEAD_SIZE],
                kg_ref[...],
                cos_ref[:, here],
                sin_ref[:, here],
            )
            dkg_ref[...] += fold(gain_term)
            dkv_ref[at, 0] = jnp.concatenate([raw_term.T, dv_all[here, :]], axis=1).astype(bf16)


def attention_specs(row, blocks, slots, width, total):
    def place(*grid):
        (i, base, _), r = (grid, row) if row is not None else (grid[1:], grid[0])
        return place_of(base[0], i, blocks), r, 0, 0

    row_of = lambda *grid: grid[0] if row is None else row
    constant = lambda *grid: (0, 0)
    both = 2 * HEAD_SIZE
    return (
        pl.BlockSpec((1, 1, slots, width), place),
        pl.BlockSpec((blocks, 1, slots, both), lambda *g: (0, row_of(*g), 0, width // both)),
        pl.BlockSpec((blocks, 1, slots, both), lambda *g: (0, row_of(*g), 0, 0)),
        pl.BlockSpec((HEAD_SIZE, 1), constant),
        pl.BlockSpec((HEAD_SIZE // 2, total), constant),
        pl.BlockSpec((1, 1, 1, width // HEAD_SIZE * slots), place),
        pl.BlockSpec((HEAD_SIZE, 128), constant),
    )


def attend(row, previous, base, lengths, raw, query_gain, key_gain, cosine, sine):
    blocks, rows, slots, columns = raw.shape
    width = columns - 2 * HEAD_SIZE
    heads = width // HEAD_SIZE
    total = blocks * slots
    query_spec, raw_key_spec, _, gain_spec, table_spec, lse_spec, _ = attention_specs(
        row, blocks, slots, width, total
    )
    operands = (base, lengths, raw, raw, query_gain, key_gain, cosine, sine)
    return pl.pallas_call(
        functools.partial(attend_kernel, row, blocks, slots, heads, 2 * slots),
        grid_spec=pltpu.PrefetchScalarGridSpec(
            num_scalar_prefetch=2,
            grid=(blocks,),
            in_specs=[query_spec, raw_key_spec, gain_spec, gain_spec, table_spec, table_spec]
            + [pl.BlockSpec(memory_space=pl.ANY)] * len(previous),
            out_specs=[query_spec, lse_spec],
            scratch_shapes=[
                pltpu.VMEM((total, HEAD_SIZE), bf16),
                pltpu.VMEM((HEAD_SIZE, total), bf16),
            ],
        ),
        out_shape=[
            jax.ShapeDtypeStruct((blocks, rows, slots, width), bf16),
            jax.ShapeDtypeStruct((blocks, rows, 1, heads * slots), f32),
        ],
        input_output_aliases={len(operands) + i: i for i in range(len(previous))},
        compiler_params=pltpu.CompilerParams(vmem_limit_bytes=32 * 2**20),
        cost_estimate=cost(2 * HEAD_SIZE * heads * total * total, 24),
        name="attend",
    )(*operands, *previous)


def attend_back(
    base, lengths, raw, query_gain, key_gain, cosine, sine, attended, gradient, log_total
):
    blocks, rows, slots, columns = raw.shape
    width = columns - 2 * HEAD_SIZE
    heads = width // HEAD_SIZE
    total = blocks * slots
    query_spec, raw_key_spec, key_spec, gain_spec, table_spec, lse_spec, sum_spec = (
        attention_specs(None, blocks, slots, width, total)
    )
    operands = (base, lengths, raw, raw, query_gain, key_gain, cosine, sine)
    operands += (attended, gradient, log_total)
    return pl.pallas_call(
        functools.partial(attend_back_kernel, blocks, slots, heads, 2 * slots),
        grid_spec=pltpu.PrefetchScalarGridSpec(
            num_scalar_prefetch=2,
            grid=(rows, blocks),
            in_specs=[query_spec, raw_key_spec, gain_spec, gain_spec, table_spec, table_spec]
            + [query_spec, query_spec, lse_spec],
            out_specs=[query_spec, key_spec, sum_spec, sum_spec],
            scratch_shapes=[
                pltpu.VMEM((total, HEAD_SIZE), bf16),
                pltpu.VMEM((total, HEAD_SIZE), bf16),
                pltpu.VMEM((HEAD_SIZE, total), bf16),
                pltpu.VMEM((total, HEAD_SIZE), f32),
                pltpu.VMEM((total, HEAD_SIZE), f32),
            ],
        ),
        out_shape=[
            jax.ShapeDtypeStruct((blocks, rows, slots, width), bf16),
            jax.ShapeDtypeStruct((blocks, rows, slots, 2 * HEAD_SIZE), bf16),
            jax.ShapeDtypeStruct((HEAD_SIZE, 128), f32),
            jax.ShapeDtypeStruct((HEAD_SIZE, 128), f32),
        ],
        compiler_params=pltpu.CompilerParams(vmem_limit_bytes=32 * 2**20),
        cost_estimate=cost(5 * HEAD_SIZE * rows * heads * total * total, 16),
        name="attend_back",
    )(*operands)


def feed_kernel(hidden_ref, cotangent_ref, weight_ref, inner_ref, grad_ref):
    units = inner_ref.shape[1]
    hidden = hidden_ref[...]
    gate = dot_nn(hidden, weight_ref[:, :units])
    upward = dot_nn(hidden, weight_ref[:, units : 2 * units])
    grad_inner = dot_nn(cotangent_ref[...], weight_ref[:, 2 * units :])
    sigmoid_gate = jax.nn.sigmoid(gate)
    silu_gate = gate * sigmoid_gate
    inner_ref[...] = (silu_gate * upward).astype(bf16)
    grad_ref[:, :units] = (
        grad_inner * upward * sigmoid_gate * (1.0 + gate * (1.0 - sigmoid_gate))
    ).astype(bf16)
    grad_ref[:, units:] = (grad_inner * silu_gate).astype(bf16)


def feed_forward(hidden, cotangents, weights):
    count, width = hidden.shape
    units = weights.shape[1] // 3
    tile = 512
    rows = pl.BlockSpec((tile, width), lambda i: (i, 0))
    return pl.pallas_call(
        feed_kernel,
        grid=(count // tile,),
        in_specs=[rows, rows, pl.BlockSpec(weights.shape, lambda i: (0, 0))],
        out_specs=[
            pl.BlockSpec((tile, units), lambda i: (i, 0)),
            pl.BlockSpec((tile, 2 * units), lambda i: (i, 0)),
        ],
        out_shape=[
            jax.ShapeDtypeStruct((count, units), bf16),
            jax.ShapeDtypeStruct((count, 2 * units), bf16),
        ],
        compiler_params=pltpu.CompilerParams(vmem_limit_bytes=48 * 2**20),
        cost_estimate=cost(6 * count * width * units, 1.7),
        name="feed_forward",
    )(hidden, cotangents, weights)


def feed_gradient_kernel(hidden_ref, cotangent_ref, grad_ref, inner_ref, out_ref):
    split = grad_ref.shape[1]
    out_ref[:, :split] = dot_tn(hidden_ref[...], grad_ref[...]).astype(bf16)
    out_ref[:, split:] = dot_tn(cotangent_ref[...], inner_ref[...]).astype(bf16)


def feed_gradient(hidden, cotangents, grad, inner):
    count, width = hidden.shape
    tile = 256
    columns = pl.BlockSpec((count, tile), lambda i: (0, i))
    total = grad.shape[1] + inner.shape[1]
    return pl.pallas_call(
        feed_gradient_kernel,
        grid=(width // tile,),
        in_specs=[columns, columns]
        + [pl.BlockSpec(v.shape, lambda i: (0, 0)) for v in (grad, inner)],
        out_specs=pl.BlockSpec((tile, total), lambda i: (i, 0)),
        out_shape=jax.ShapeDtypeStruct((width, total), bf16),
        compiler_params=pltpu.CompilerParams(vmem_limit_bytes=48 * 2**20),
        cost_estimate=cost(2 * count * width * total, 1.6),
        name="feed_gradient",
    )(hidden, cotangents, grad, inner)


def product_kernel(count, weighed, adds, outs, *refs):
    rows, weights, rest = refs[:count], refs[count : 2 * count], refs[2 * count :]
    out_refs = rest[-outs:]
    total = sum(dot_nt(r[...], w[...]) for r, w in zip(rows, weights))
    if weighed:
        *out_refs, sum_ref = out_refs
        sum_ref[...] = jnp.sum(total * rest[0][...].astype(f32), axis=0, keepdims=True)
    if adds:
        total += rest[weighed][...].astype(f32)
    start = 0
    for out_ref in out_refs:
        out_ref[...] = total[start : start + out_ref.shape[0]].astype(out_ref.dtype)
        start += out_ref.shape[0]


def sum_of_products(
    share, lefts, weights, column, tokens, first, count, splits, add, before, weigh=None
):
    rows = count * tokens
    width = weights[0].shape[0]
    tile = 512
    operands = list(lefts) + list(weights)
    specs = [pl.BlockSpec((rows, v.shape[1]), lambda i: (first // count, 0)) for v in lefts] + [
        pl.BlockSpec((tile, v.shape[1]), lambda i: (i, column)) for v in lefts
    ]
    out_specs = [pl.BlockSpec((r, tile), lambda i: (0, i)) for r, _ in splits]
    out_shape = [jax.ShapeDtypeStruct((r, width), dtype) for r, dtype in splits]
    if weigh is not None:
        operands.append(weigh)
        specs.append(pl.BlockSpec((rows, tile), lambda i: (first // count, i)))
        out_specs.append(pl.BlockSpec((1, tile), lambda i: (0, i)))
        out_shape.append(jax.ShapeDtypeStruct((1, width), f32))
    if add is not None:
        operands.append(add)
        specs.append(pl.BlockSpec((rows, tile), lambda i: (0, i)))
    operands += before
    specs += [pl.BlockSpec(memory_space=pl.ANY)] * len(before)
    return pl.pallas_call(
        functools.partial(
            product_kernel,
            len(lefts),
            int(weigh is not None),
            int(add is not None),
            len(out_shape),
        ),
        grid=(width // tile,),
        in_specs=specs,
        out_specs=out_specs,
        out_shape=out_shape,
        compiler_params=pltpu.CompilerParams(vmem_limit_bytes=48 * 2**20),
        cost_estimate=cost(2 * rows * width * sum(v.shape[1] for v in lefts), share),
        name="sum_of_products",
    )(*operands)


def body(
    inputs,
    lengths,
    attention_gain,
    query_weight,
    key_matrix,
    value_matrix,
    out_weight,
    query_gain,
    key_gain,
    feedforward_gain,
    gate_weight,
    up_weight,
    down_weight,
    cotangent,
):
    rows, slots, width = inputs.shape
    tokens = rows * slots
    parts = lax.axis_size("ctx")
    heads = QUERY_HEADS_TOTAL // parts
    share = parts // KEY_VALUE_HEADS
    query_cols = heads * HEAD_SIZE
    weight_rows = query_weight.shape[0]
    feed = gate_weight.shape[1] // parts
    all_tokens = parts * tokens
    base = lax.axis_index("ctx").astype(jnp.int32)

    qkv_pack = jnp.concatenate(
        [query_weight.reshape(weight_rows, parts, query_cols)]
        + [
            jnp.repeat(w.reshape(weight_rows, KEY_VALUE_HEADS, HEAD_SIZE), share, axis=1)
            for w in (key_matrix, value_matrix)
        ],
        axis=2,
    )
    qkv_block = spread_columns(qkv_pack)
    out_block = spread_columns(out_weight.reshape(weight_rows, parts, query_cols))
    first_units = feed * 4 // 8 // 128 * 128
    feed_packs = [
        jnp.concatenate(
            [
                w.reshape(weight_rows, parts, feed)[:, :, start:stop]
                for w in (gate_weight, up_weight, down_weight)
            ],
            axis=2,
        )
        for start, stop in ((0, first_units), (first_units, feed))
    ]
    flat = inputs.reshape(tokens, width).astype(f32)
    first_scale = rms_scale(flat)
    normed = flat * first_scale
    hidden_pieces, hidden_start = gather_pieces((normed * attention_gain).astype(bf16))
    hidden = stack(hidden_pieces)
    first_block = spread_columns(after(feed_packs[0], out_block, *hidden_start))
    qkv_full = gather_rows(qkv_block)
    out_full = gather_rows(out_block)
    first_full = gather_rows(first_block)

    raw = jnp.concatenate([dot_nn(piece, qkv_full) for piece in hidden_pieces], axis=0)
    cotangent_flat = cotangent.reshape(tokens, width)
    cotangent_pieces, cotangents_start = gather_pieces(after(cotangent_flat, first_block))
    cotangents = stack(cotangent_pieces)
    raw = after(raw, *cotangents_start).reshape(parts, rows, slots, query_cols + 2 * HEAD_SIZE)
    last_block = spread_columns(after(feed_packs[1], *cotangents_start))
    cosine, sine = [
        t.T for t in rotary_tables(jnp.arange(parts * slots, dtype=jnp.int32), HEAD_SIZE)
    ]
    base_array = base.reshape(1)
    gains = [g.astype(f32).reshape(HEAD_SIZE, 1) for g in (query_gain, key_gain)]
    results = ()
    for row in range(rows):
        if row == rows - 1:
            results = fence(results, last_block, cotangent_pieces[-1]) if results else results
        results = attend(row, results, base_array, lengths, raw, *gains, cosine, sine)
    attended, log_total = results
    attended_rows = attended.reshape(all_tokens, query_cols)
    sums = partial_products(
        functools.partial(sum_of_products, 2.4, [attended_rows], [out_full], 0, tokens), tokens
    )
    mixed = flat + near_step(far_step(sums))

    second_scale = rms_scale(mixed)
    normed_again = mixed * second_scale
    pieces, _ = gather_pieces((normed_again * feedforward_gain).astype(bf16), (cotangents,))
    hidden_again = after(stack(pieces), first_full)
    last_full = gather_rows(after(last_block, first_full))
    fulls = [first_full, last_full]
    inners, grads, partials = [], [], []
    for which in range(2):
        if which == 1:
            fulls[1] = after(last_full, partials[0])
        inner, grad = feed_forward(hidden_again, cotangents, fulls[which])
        inners.append(inner)
        grads.append(grad)
        partials.append(feed_gradient(hidden_again, cotangents, grad, inner))
    first_gradient = scatter_rows(partials[0])
    last_gradient = scatter_rows(after(partials[1], first_gradient))
    sums = partial_products(
        functools.partial(sum_of_products, 0, grads, fulls, 0, tokens), tokens
    )
    sums = far_step(sums)
    feed_sums = partial_products(
        functools.partial(sum_of_products, 2.4, inners, fulls, 2, tokens), tokens, tuple(sums[1:])
    )
    feed_arrived = far_hops(feed_sums)
    own, *arrived = near_hops(sums)
    if arrived:
        arrived = fence(arrived, feed_sums[0])
    grad_hidden_again = sum(part.astype(f32) for part in (own, *arrived))
    feedforward_gain_local = jnp.sum(grad_hidden_again * normed_again, axis=0)
    scaled_again = grad_hidden_again * feedforward_gain
    grad_mixed = cotangent_flat.astype(f32) + second_scale * (
        scaled_again - normed_again * jnp.mean(scaled_again * normed_again, axis=-1, keepdims=True)
    )

    pieces, _ = gather_pieces(
        after(grad_mixed.astype(bf16), first_gradient, *feed_arrived)
    )
    grad_branch = stack(pieces)
    attended_gradient = jnp.concatenate(
        [dot_nn(piece, out_full).astype(bf16) for piece in pieces], axis=0
    )
    first_collected = collect_columns(after(first_gradient, attended_gradient))
    feed_parts = near_hops(far_add(feed_sums, feed_arrived, (attended_gradient,)))
    feed_out = sum(part.astype(f32) for part in feed_parts)
    outputs = (mixed + feed_out).astype(bf16).reshape(rows, slots, width)
    grad_queries, grad_keys_values, query_gain_sums, key_gain_sums = attend_back(
        base_array,
        lengths,
        raw,
        *gains,
        cosine,
        sine,
        attended,
        attended_gradient.reshape(parts, rows, slots, query_cols),
        log_total,
    )
    query_gain_local, key_gain_local = query_gain_sums.sum(axis=1), key_gain_sums.sum(axis=1)
    grad_raw = jnp.concatenate(
        [
            grad_queries.reshape(all_tokens, query_cols),
            grad_keys_values.reshape(all_tokens, 2 * HEAD_SIZE),
        ],
        axis=1,
    )
    grad_raw = after(grad_raw, *feed_parts[1:], first_collected)
    attention_partial = jnp.concatenate(
        [dot_tn(hidden, grad_raw), dot_tn(grad_branch, after(attended_rows, grad_raw))], axis=1
    ).astype(bf16)
    attention_gradient = scatter_rows(after(attention_partial, last_gradient))
    attention_collected = collect_columns(attention_gradient)
    query_weight_gradient, key_weight_gradient, value_weight_gradient, out_weight_gradient = (
        place_heads(attention_collected, parts, share)
    )
    weighed_sums = []

    def hidden_product(*arguments):
        *sums, weighed = sum_of_products(
            2.4, [grad_raw], [qkv_full], 0, tokens, *arguments, weigh=hidden
        )
        weighed_sums.append(weighed[0])
        return sums

    sums = partial_products(hidden_product, tokens, (attention_partial,))
    last_collected = collect_columns(last_gradient)
    sums = far_step(sums, (feed_out,), (last_collected,))
    grad_hidden = after(near_step(sums), attention_collected)
    gate_weight_gradient, up_weight_gradient, down_weight_gradient = place_units(
        first_collected, last_collected, parts
    )

    attention_gain_local = sum(weighed_sums) / attention_gain.astype(f32)
    scaled_first = grad_hidden * attention_gain
    input_gradient = (
        grad_mixed
        + first_scale
        * (scaled_first - normed * jnp.mean(scaled_first * normed, axis=-1, keepdims=True))
    ).astype(bf16)
    gain_sums = sum_everywhere(
        after(
            jnp.concatenate(
                [attention_gain_local, feedforward_gain_local, query_gain_local, key_gain_local]
            ),
            *sums[1:],
        )
    )
    attention_gain_gradient, feedforward_gain_gradient = gain_sums[:width], gain_sums[width : 2 * width]
    query_gain_gradient = gain_sums[2 * width : 2 * width + HEAD_SIZE]
    key_gain_gradient = gain_sums[2 * width + HEAD_SIZE :]
    return (
        outputs,
        input_gradient.reshape(rows, slots, width),
        attention_gain_gradient,
        query_weight_gradient,
        key_weight_gradient,
        value_weight_gradient,
        out_weight_gradient,
        query_gain_gradient,
        key_gain_gradient,
        feedforward_gain_gradient,
        gate_weight_gradient,
        up_weight_gradient,
        down_weight_gradient,
    )


def solution(mesh):
    weight = P(("dp", "ctx"), None)
    token = P("dp", "ctx", None)
    placed = (
        token, P("dp"), P(), weight, weight, weight, weight, P(), P(), P(), weight, weight, weight, token,
    )
    returned = (
        token, token, P(), weight, weight, weight, weight, P(), P(), P(), weight, weight, weight,
    )
    return jax.shard_map(
        body, mesh=mesh, in_specs=placed, out_specs=returned, check_vma=False
    )
```

```python
import functools

import jax
import jax.numpy as jnp
from jax import lax
from jax.experimental import pallas as pl
from jax.experimental.pallas import tpu as pltpu
from jax.sharding import PartitionSpec as P

QUERY_HEADS_TOTAL = 32
KEY_VALUE_HEADS = 8
HEAD_SIZE = 64
FACTOR = HEAD_SIZE ** (-0.5)

NO_COST = pl.CostEstimate(flops=0, bytes_accessed=0, transcendentals=0)


def cost(flops, share):
    return pl.CostEstimate(flops=int(flops * share), bytes_accessed=0, transcendentals=0)


epsilon = 1e-06
f32 = jnp.float32
bf16 = jnp.bfloat16


def rms_scale(value_rows):
    return lax.rsqrt(jnp.mean(value_rows * value_rows, axis=-1, keepdims=True) + epsilon)


def rotary_tables(positions, width):
    inverse = 10000.0 ** (-(jnp.arange(width // 2, dtype=f32) * 2.0) / width)
    angle_table = positions.astype(f32)[:, None] * inverse[None, :]
    return (jnp.cos(angle_table), jnp.sin(angle_table))


def dot_nn(left, right):
    return jnp.dot(left, right, preferred_element_type=f32)


def dot_tn(left, right):
    return lax.dot_general(left, right, (((0,), (0,)), ((), ())), preferred_element_type=f32)


def dot_nt(left, right):
    return lax.dot_general(left, right, (((1,), (1,)), ((), ())), preferred_element_type=f32)


def fence(values, *earlier):
    count = len(values)
    anywhere = pl.BlockSpec(memory_space=pl.ANY)
    return pl.pallas_call(
        lambda *refs: None,
        in_specs=[anywhere] * (count + len(earlier)),
        out_specs=[anywhere] * count,
        out_shape=[jax.ShapeDtypeStruct(v.shape, v.dtype) for v in values],
        input_output_aliases={i: i for i in range(count)},
        cost_estimate=NO_COST,
        name="fence",
    )(*values, *earlier)


def after(value, *earlier):
    return fence((value,), *earlier)[0]


def stack_kernel(*refs):
    for k, ref in enumerate(refs[:-1]):

        @pl.when(pl.program_id(0) == k)
        def _():
            refs[-1][...] = ref[...]


def stack(pieces):
    if len(pieces) == 1:
        return pieces[0]
    shape = pieces[0].shape
    return pl.pallas_call(
        stack_kernel,
        grid=(len(pieces),),
        in_specs=[pl.BlockSpec(shape, lambda i: (0, 0))] * len(pieces),
        out_specs=pl.BlockSpec(shape, lambda i: (i, 0)),
        out_shape=jax.ShapeDtypeStruct((len(pieces) * shape[0], shape[1]), pieces[0].dtype),
        compiler_params=pltpu.CompilerParams(vmem_limit_bytes=32 * 2**20),
        cost_estimate=NO_COST,
        name="stack",
    )(*pieces)


RELATIVE = (0, 2, 4, 6, 1, 3, 5, 7)


def place_of(own, index, parts):
    if parts != 8:
        return index
    relative = lax.bitwise_xor(own, index)
    return lax.bitwise_or(
        lax.shift_right_logical(relative, 1), lax.shift_left(lax.bitwise_and(relative, 1), 2)
    )


def hop(value, bit):
    return lax.ppermute(value, "ctx", [(i, i ^ bit) for i in range(lax.axis_size("ctx"))])


def halves_kernel(by_x_ref, by_y_ref, *refs):
    refs[-2][...] = by_x_ref[...]
    refs[-1][...] = by_y_ref[...]


def halves(by_x, by_y, before):
    rows, width = by_x.shape
    half = (rows // 2, width)
    return pl.pallas_call(
        halves_kernel,
        grid=(1,),
        in_specs=[pl.BlockSpec(half, lambda i: (0, 0)), pl.BlockSpec(half, lambda i: (1, 0))]
        + [pl.BlockSpec(memory_space=pl.ANY)] * len(before),
        out_specs=[pl.BlockSpec(half, lambda i: (0, 0))] * 2,
        out_shape=[jax.ShapeDtypeStruct(half, by_x.dtype)] * 2,
        cost_estimate=cost(10**9, 1),
        name="halves",
    )(by_x, by_y, *before)


def gather_pieces(value, middle=()):
    if lax.axis_size("ctx") != 8:
        whole = lax.all_gather(value, "ctx", axis=0, tiled=True)
        return (whole,), (whole,)
    by_x, by_y = hop(value, 2), hop(value, 4)
    first, second = halves(by_x, by_y, middle)
    far = stack((hop(first, 4), hop(second, 2)))
    others = [hop(piece, 1) for piece in (value, by_x, by_y)]
    return (value, by_x, by_y, far, *others, hop(far, 1)), (by_x, by_y)


def partial_products(product, tokens, before=()):
    parts = lax.axis_size("ctx")
    if parts != 8:
        return product(0, parts, [(parts * tokens, bf16)], None, before)
    half = (tokens // 2, bf16)
    near_other, far_other = product(4, 4, [(3 * tokens, bf16), (tokens, bf16)], None, before)
    far_other = hop(far_other, 1)
    near_other = after(near_other, far_other)
    far = product(3, 1, [half] * 2, far_other, ())
    own, *near = product(
        0, 3, [(tokens, f32)] + [(tokens, bf16)] * 2, hop(near_other, 1), (far[0],)
    )
    return (own, *near, *far)


def far_hops(sums, far_after=()):
    if lax.axis_size("ctx") != 8:
        return ()
    far_first, far_last = sums[3:]
    if far_after:
        far_first, far_last = fence((far_first, far_last), *far_after)
    return hop(far_first, 2), hop(far_last, 4)


def far_add(sums, arrived, near_after=()):
    if lax.axis_size("ctx") != 8:
        return fence(sums, *near_after) if near_after else sums
    own, by_x, by_y = sums[:3]
    if near_after:
        by_x, by_y = fence((by_x, by_y), *near_after)
    from_x, from_y = arrived
    rows = by_x.shape[0] // 2
    by_x = by_x + jnp.pad(from_y, ((rows, 0), (0, 0)))
    by_y = by_y + jnp.pad(from_x, ((0, rows), (0, 0)))
    return own, by_x, by_y


def far_step(sums, far_after=(), near_after=()):
    return far_add(sums, far_hops(sums, far_after), near_after)


def near_hops(sums):
    if lax.axis_size("ctx") != 8:
        (whole,) = sums
        return (lax.psum_scatter(whole, "ctx", scatter_dimension=0, tiled=True),)
    own, by_x, by_y = sums
    return own, hop(by_x, 2), hop(by_y, 4)


def near_step(sums):
    return sum(part.astype(f32) for part in near_hops(sums))


def sum_everywhere(value):
    if lax.axis_size("ctx") != 8 or lax.axis_size("dp") != 4:
        return lax.psum(value, ("dp", "ctx"))
    value = value + hop(value, 1)
    value = value + (hop(value, 2) + hop(value, 4) + hop(value, 6))
    shifted = [
        lax.ppermute(value, "dp", [(i, i ^ bits) for i in range(4)]) for bits in (1, 2, 3)
    ]
    return (value + shifted[0]) + (shifted[1] + shifted[2])


def spread_columns(packed):
    rows, parts, columns = packed.shape
    return lax.all_to_all(
        packed.reshape(rows, parts * columns), "ctx", split_axis=1, concat_axis=0, tiled=True
    )


def gather_rows(block):
    return lax.all_gather(block, "dp", axis=0, tiled=True)


def scatter_rows(gradient):
    return lax.psum_scatter(gradient, "dp", scatter_dimension=0, tiled=True)


def collect_columns(block):
    return lax.all_to_all(block, "ctx", split_axis=0, concat_axis=0, tiled=True)


def place_units_kernel(first_ref, last_ref, *out_refs):
    for which, out_ref in enumerate(out_refs):
        start = 0
        for ref in (first_ref, last_ref):
            units = ref.shape[1] // 3
            out_ref[:, start : start + units] = ref[
                :, which * units : (which + 1) * units
            ].astype(f32)
            start += units


def place_units(first, last, parts):
    rows = first.shape[0] // parts
    units = (first.shape[1] + last.shape[1]) // 3
    return pl.pallas_call(
        place_units_kernel,
        grid=(parts,),
        in_specs=[pl.BlockSpec((rows, v.shape[1]), lambda i: (i, 0)) for v in (first, last)],
        out_specs=[pl.BlockSpec((rows, units), lambda i: (0, i))] * 3,
        out_shape=[jax.ShapeDtypeStruct((rows, units * parts), f32)] * 3,
        compiler_params=pltpu.CompilerParams(vmem_limit_bytes=16 * 2**20),
        cost_estimate=cost(10**7, 800),
        name="place_units",
    )(first, last)


def place_heads_kernel(parts, share, block_ref, query_ref, key_ref, value_ref, out_ref):
    rows = query_ref.shape[0]
    width = query_ref.shape[1] // parts
    for part in range(parts):
        block = block_ref[part * rows : (part + 1) * rows, :].astype(f32)
        here = slice(part * width, (part + 1) * width)
        query_ref[:, here] = block[:, :width]
        out_ref[:, here] = block[:, width + 2 * HEAD_SIZE :]
        head = part // share
        for ref, start in ((key_ref, width), (value_ref, width + HEAD_SIZE)):
            columns = slice(head * HEAD_SIZE, (head + 1) * HEAD_SIZE)
            piece = block[:, start : start + HEAD_SIZE]
            ref[:, columns] = piece if part % share == 0 else ref[:, columns] + piece


def place_heads(block, parts, share):
    rows = block.shape[0] // parts
    width = (block.shape[1] - 2 * HEAD_SIZE) // 2 * parts
    whole = pl.BlockSpec(memory_space=pltpu.VMEM)
    shapes = [(rows, width), (rows, parts // share * HEAD_SIZE)]
    shapes += [shapes[1], shapes[0]]
    return pl.pallas_call(
        functools.partial(place_heads_kernel, parts, share),
        in_specs=[whole],
        out_specs=[whole] * 4,
        out_shape=[jax.ShapeDtypeStruct(shape, f32) for shape in shapes],
        compiler_params=pltpu.CompilerParams(vmem_limit_bytes=16 * 2**20),
        cost_estimate=cost(10**7, 400),
        name="place_heads",
    )(block)


def heads_to_columns(block, heads):
    return jnp.concatenate(
        [block[:, h * HEAD_SIZE : (h + 1) * HEAD_SIZE].T for h in range(heads)], axis=1
    )


def columns_to_heads(columns, heads, slots):
    return jnp.concatenate(
        [columns[:, h * slots : (h + 1) * slots].T for h in range(heads)], axis=1
    )


def columns_to_rows(columns, heads, slots):
    return jnp.concatenate(
        [columns[:, h * slots : (h + 1) * slots].T for h in range(heads)], axis=0
    )


def head_scale(raw):
    return lax.rsqrt(jnp.mean(raw * raw, axis=0, keepdims=True) + epsilon)


def prepare(raw, gain, cosine, sine):
    value = raw * head_scale(raw) * gain
    first, second = value[: HEAD_SIZE // 2], value[HEAD_SIZE // 2 :]
    return jnp.concatenate(
        [first * cosine - second * sine, second * cosine + first * sine], axis=0
    )


def prepare_back(gradient, raw, gain, cosine, sine):
    scale = head_scale(raw)
    unit = raw * scale
    first, second = gradient[: HEAD_SIZE // 2], gradient[HEAD_SIZE // 2 :]
    turned = jnp.concatenate(
        [first * cosine + second * sine, second * cosine - first * sine], axis=0
    )
    inside = turned * gain
    middle = jnp.mean(inside * unit, axis=0, keepdims=True)
    return scale * (inside - unit * middle), turned * unit


def fold(values):
    lanes = 128
    return sum(values[:, i : i + lanes] for i in range(0, values.shape[1], lanes))


def repeated(table, heads):
    return jnp.concatenate([table] * heads, axis=1)


def masked_scores(key_block, query_columns, start, query_block, slots, length):
    scores = dot_nn(key_block, query_columns)
    key_pos = start + lax.broadcasted_iota(jnp.int32, scores.shape, 0)
    query_pos = query_block * slots + lax.rem(
        lax.broadcasted_iota(jnp.int32, scores.shape, 1), slots
    )
    return jnp.where((key_pos <= query_pos) & (key_pos < length), scores, -1e30)


def chunks_needed(query_block, slots, length, chunk):
    return lax.div(
        jnp.minimum((query_block + 1) * slots, length) + (chunk - 1), jnp.int32(chunk)
    )


def attend_kernel(
    row, blocks, slots, heads, chunk,
    base_ref, len_ref, q_ref, kv_ref, qg_ref, kg_ref, cos_ref, sin_ref,
    *refs,
):
    o_ref, lse_ref, k_all, v_t = refs[-4:]
    query_block = pl.program_id(0)
    base, length = base_ref[0], len_ref[row]

    @pl.when(query_block == 0)
    def _():
        for j in range(blocks):
            at = place_of(base, jnp.int32(j), blocks)
            here = slice(j * slots, (j + 1) * slots)
            both = kv_ref[at, 0].T
            keys = prepare(both[:HEAD_SIZE], kg_ref[...], cos_ref[:, here], sin_ref[:, here])
            k_all[here, :] = keys.T.astype(bf16)
            v_t[:, here] = both[HEAD_SIZE:].astype(bf16)

    count = chunks_needed(query_block, slots, length, chunk)
    here = pl.ds(pl.multiple_of(query_block * slots, slots), slots)
    queries = prepare(
        heads_to_columns(q_ref[0, 0], heads),
        qg_ref[...],
        repeated(cos_ref[:, here], heads),
        repeated(sin_ref[:, here], heads),
    )
    queries = queries.astype(bf16) * FACTOR
    columns = heads * slots

    def step(j, carry):
        top, total, accum = carry
        start = pl.multiple_of(j * chunk, chunk)
        scores = masked_scores(
            k_all[pl.ds(start, chunk), :], queries, start, query_block, slots, length
        )
        new_top = jnp.maximum(top, jnp.max(scores, axis=0, keepdims=True))
        probs = jnp.exp(scores - new_top)
        alpha = jnp.exp(top - new_top)
        total = total * alpha + jnp.sum(probs, axis=0, keepdims=True)
        accum = accum * alpha + dot_nn(v_t[:, pl.ds(start, chunk)], probs.astype(bf16))
        return new_top, total, accum

    top, total, accum = lax.fori_loop(
        0,
        count,
        step,
        (
            jnp.full((1, columns), -1e30, f32),
            jnp.zeros((1, columns), f32),
            jnp.zeros((HEAD_SIZE, columns), f32),
        ),
    )
    o_ref[0, 0] = columns_to_heads(accum / total, heads, slots).astype(bf16)
    lse_ref[0, 0] = top + jnp.log(total)


def attend_back_kernel(
    blocks, slots, heads, chunk,
    base_ref, len_ref, q_ref, kv_ref, qg_ref, kg_ref, cos_ref, sin_ref, o_ref, do_ref, lse_ref,
    dq_ref, dkv_ref, dqg_ref, dkg_ref, k_all, v_all, k_t, dk_all, dv_all,
):
    row, query_block = pl.program_id(0), pl.program_id(1)
    base, length = base_ref[0], len_ref[row]

    @pl.when((row == 0) & (query_block == 0))
    def _():
        dqg_ref[...] = jnp.zeros_like(dqg_ref)
        dkg_ref[...] = jnp.zeros_like(dkg_ref)

    @pl.when(query_block == 0)
    def _():
        for j in range(blocks):
            at = place_of(base, jnp.int32(j), blocks)
            here = slice(j * slots, (j + 1) * slots)
            both = kv_ref[at, 0]
            keys = prepare(both.T[:HEAD_SIZE], kg_ref[...], cos_ref[:, here], sin_ref[:, here])
            k_t[:, here] = keys.astype(bf16)
            k_all[here, :] = keys.T.astype(bf16)
            v_all[here, :] = both[:, HEAD_SIZE:].astype(bf16)
        dk_all[...] = jnp.zeros_like(dk_all)
        dv_all[...] = jnp.zeros_like(dv_all)

    count = chunks_needed(query_block, slots, length, chunk)
    here = pl.ds(pl.multiple_of(query_block * slots, slots), slots)
    cosine, sine = repeated(cos_ref[:, here], heads), repeated(sin_ref[:, here], heads)
    raw = heads_to_columns(q_ref[0, 0], heads)
    queries = prepare(raw, qg_ref[...], cosine, sine).astype(bf16) * FACTOR
    query_rows = columns_to_rows(queries.astype(f32), heads, slots).astype(bf16)
    gradient = heads_to_columns(do_ref[0, 0].astype(f32), heads)
    grad_rows = columns_to_rows(gradient, heads, slots).astype(bf16)
    delta = jnp.sum(
        gradient * heads_to_columns(o_ref[0, 0].astype(f32), heads), axis=0, keepdims=True
    )
    gradient = gradient.astype(bf16)
    log_total = lse_ref[0, 0]

    def step(j, dq_t):
        start = pl.multiple_of(j * chunk, chunk)
        at = pl.ds(start, chunk)
        scores = masked_scores(k_all[at, :], queries, start, query_block, slots, length)
        probs = jnp.exp(scores - log_total)
        grad_probs = dot_nn(v_all[at, :], gradient)
        grad_scores = (probs * (grad_probs - delta)).astype(bf16)
        dv_all[at, :] += dot_nn(probs.astype(bf16), grad_rows)
        dk_all[at, :] += dot_nn(grad_scores, query_rows)
        return dq_t + dot_nn(k_t[:, at], grad_scores)

    dq_t = lax.fori_loop(0, count, step, jnp.zeros((HEAD_SIZE, heads * slots), f32))
    raw_term, gain_term = prepare_back(dq_t * FACTOR, raw, qg_ref[...], cosine, sine)
    dq_ref[0, 0] = columns_to_heads(raw_term, heads, slots).astype(bf16)
    dqg_ref[...] += fold(gain_term)

    @pl.when(query_block == blocks - 1)
    def _():
        for j in range(blocks):
            at = place_of(base, jnp.int32(j), blocks)
            here = slice(j * slots, (j + 1) * slots)
            raw_term, gain_term = prepare_back(
                dk_all[here, :].T,
                kv_ref[at, 0].T[:HEAD_SIZE],
                kg_ref[...],
                cos_ref[:, here],
                sin_ref[:, here],
            )
            dkg_ref[...] += fold(gain_term)
            dkv_ref[at, 0] = jnp.concatenate([raw_term.T, dv_all[here, :]], axis=1).astype(bf16)


def attention_specs(row, blocks, slots, width, total):
    def place(*grid):
        (i, base, _), r = (grid, row) if row is not None else (grid[1:], grid[0])
        return place_of(base[0], i, blocks), r, 0, 0

    row_of = lambda *grid: grid[0] if row is None else row
    constant = lambda *grid: (0, 0)
    both = 2 * HEAD_SIZE
    return (
        pl.BlockSpec((1, 1, slots, width), place),
        pl.BlockSpec((blocks, 1, slots, both), lambda *g: (0, row_of(*g), 0, width // both)),
        pl.BlockSpec((blocks, 1, slots, both), lambda *g: (0, row_of(*g), 0, 0)),
        pl.BlockSpec((HEAD_SIZE, 1), constant),
        pl.BlockSpec((HEAD_SIZE // 2, total), constant),
        pl.BlockSpec((1, 1, 1, width // HEAD_SIZE * slots), place),
        pl.BlockSpec((HEAD_SIZE, 128), constant),
    )


def attend(row, previous, base, lengths, raw, query_gain, key_gain, cosine, sine):
    blocks, rows, slots, columns = raw.shape
    width = columns - 2 * HEAD_SIZE
    heads = width // HEAD_SIZE
    total = blocks * slots
    query_spec, raw_key_spec, _, gain_spec, table_spec, lse_spec, _ = attention_specs(
        row, blocks, slots, width, total
    )
    operands = (base, lengths, raw, raw, query_gain, key_gain, cosine, sine)
    return pl.pallas_call(
        functools.partial(attend_kernel, row, blocks, slots, heads, 2 * slots),
        grid_spec=pltpu.PrefetchScalarGridSpec(
            num_scalar_prefetch=2,
            grid=(blocks,),
            in_specs=[query_spec, raw_key_spec, gain_spec, gain_spec, table_spec, table_spec]
            + [pl.BlockSpec(memory_space=pl.ANY)] * len(previous),
            out_specs=[query_spec, lse_spec],
            scratch_shapes=[
                pltpu.VMEM((total, HEAD_SIZE), bf16),
                pltpu.VMEM((HEAD_SIZE, total), bf16),
            ],
        ),
        out_shape=[
            jax.ShapeDtypeStruct((blocks, rows, slots, width), bf16),
            jax.ShapeDtypeStruct((blocks, rows, 1, heads * slots), f32),
        ],
        input_output_aliases={len(operands) + i: i for i in range(len(previous))},
        compiler_params=pltpu.CompilerParams(vmem_limit_bytes=32 * 2**20),
        cost_estimate=cost(2 * HEAD_SIZE * heads * total * total, 24),
        name="attend",
    )(*operands, *previous)


def attend_back(
    base, lengths, raw, query_gain, key_gain, cosine, sine, attended, gradient, log_total
):
    blocks, rows, slots, columns = raw.shape
    width = columns - 2 * HEAD_SIZE
    heads = width // HEAD_SIZE
    total = blocks * slots
    query_spec, raw_key_spec, key_spec, gain_spec, table_spec, lse_spec, sum_spec = (
        attention_specs(None, blocks, slots, width, total)
    )
    operands = (base, lengths, raw, raw, query_gain, key_gain, cosine, sine)
    operands += (attended, gradient, log_total)
    return pl.pallas_call(
        functools.partial(attend_back_kernel, blocks, slots, heads, 2 * slots),
        grid_spec=pltpu.PrefetchScalarGridSpec(
            num_scalar_prefetch=2,
            grid=(rows, blocks),
            in_specs=[query_spec, raw_key_spec, gain_spec, gain_spec, table_spec, table_spec]
            + [query_spec, query_spec, lse_spec],
            out_specs=[query_spec, key_spec, sum_spec, sum_spec],
            scratch_shapes=[
                pltpu.VMEM((total, HEAD_SIZE), bf16),
                pltpu.VMEM((total, HEAD_SIZE), bf16),
                pltpu.VMEM((HEAD_SIZE, total), bf16),
                pltpu.VMEM((total, HEAD_SIZE), f32),
                pltpu.VMEM((total, HEAD_SIZE), f32),
            ],
        ),
        out_shape=[
            jax.ShapeDtypeStruct((blocks, rows, slots, width), bf16),
            jax.ShapeDtypeStruct((blocks, rows, slots, 2 * HEAD_SIZE), bf16),
            jax.ShapeDtypeStruct((HEAD_SIZE, 128), f32),
            jax.ShapeDtypeStruct((HEAD_SIZE, 128), f32),
        ],
        compiler_params=pltpu.CompilerParams(vmem_limit_bytes=32 * 2**20),
        cost_estimate=cost(5 * HEAD_SIZE * rows * heads * total * total, 16),
        name="attend_back",
    )(*operands)


def feed_kernel(hidden_ref, cotangent_ref, weight_ref, inner_ref, grad_ref):
    units = inner_ref.shape[1]
    hidden = hidden_ref[...]
    gate = dot_nn(hidden, weight_ref[:, :units])
    upward = dot_nn(hidden, weight_ref[:, units : 2 * units])
    grad_inner = dot_nn(cotangent_ref[...], weight_ref[:, 2 * units :])
    sigmoid_gate = jax.nn.sigmoid(gate)
    silu_gate = gate * sigmoid_gate
    inner_ref[...] = (silu_gate * upward).astype(bf16)
    grad_ref[:, :units] = (
        grad_inner * upward * sigmoid_gate * (1.0 + gate * (1.0 - sigmoid_gate))
    ).astype(bf16)
    grad_ref[:, units:] = (grad_inner * silu_gate).astype(bf16)


def feed_forward(share, hidden, cotangents, weights):
    count, width = hidden.shape
    units = weights.shape[1] // 3
    tile = 512
    rows = pl.BlockSpec((tile, width), lambda i: (i, 0))
    return pl.pallas_call(
        feed_kernel,
        grid=(count // tile,),
        in_specs=[rows, rows, pl.BlockSpec(weights.shape, lambda i: (0, 0))],
        out_specs=[
            pl.BlockSpec((tile, units), lambda i: (i, 0)),
            pl.BlockSpec((tile, 2 * units), lambda i: (i, 0)),
        ],
        out_shape=[
            jax.ShapeDtypeStruct((count, units), bf16),
            jax.ShapeDtypeStruct((count, 2 * units), bf16),
        ],
        compiler_params=pltpu.CompilerParams(vmem_limit_bytes=48 * 2**20),
        cost_estimate=cost(6 * count * width * units, share),
        name="feed_forward",
    )(hidden, cotangents, weights)


def feed_gradient_kernel(hidden_ref, cotangent_ref, grad_ref, inner_ref, out_ref):
    split = grad_ref.shape[1]
    out_ref[:, :split] = dot_tn(hidden_ref[...], grad_ref[...]).astype(bf16)
    out_ref[:, split:] = dot_tn(cotangent_ref[...], inner_ref[...]).astype(bf16)


def feed_gradient(share, hidden, cotangents, grad, inner):
    count, width = hidden.shape
    tile = 256
    columns = pl.BlockSpec((count, tile), lambda i: (0, i))
    total = grad.shape[1] + inner.shape[1]
    return pl.pallas_call(
        feed_gradient_kernel,
        grid=(width // tile,),
        in_specs=[columns, columns]
        + [pl.BlockSpec(v.shape, lambda i: (0, 0)) for v in (grad, inner)],
        out_specs=pl.BlockSpec((tile, total), lambda i: (i, 0)),
        out_shape=jax.ShapeDtypeStruct((width, total), bf16),
        compiler_params=pltpu.CompilerParams(vmem_limit_bytes=48 * 2**20),
        cost_estimate=cost(2 * count * width * total, share),
        name="feed_gradient",
    )(hidden, cotangents, grad, inner)


def product_kernel(count, weighed, adds, outs, *refs):
    rows, weights, rest = refs[:count], refs[count : 2 * count], refs[2 * count :]
    out_refs = rest[-outs:]
    total = sum(dot_nt(r[...], w[...]) for r, w in zip(rows, weights))
    if weighed:
        *out_refs, sum_ref = out_refs
        sum_ref[...] = jnp.sum(total * rest[0][...].astype(f32), axis=0, keepdims=True)
    if adds:
        total += rest[weighed][...].astype(f32)
    start = 0
    for out_ref in out_refs:
        out_ref[...] = total[start : start + out_ref.shape[0]].astype(out_ref.dtype)
        start += out_ref.shape[0]


def sum_of_products(
    share, lefts, weights, column, tokens, first, count, splits, add, before, weigh=None
):
    rows = count * tokens
    width = weights[0].shape[0]
    tile = 512
    operands = list(lefts) + list(weights)
    specs = [pl.BlockSpec((rows, v.shape[1]), lambda i: (first // count, 0)) for v in lefts] + [
        pl.BlockSpec((tile, v.shape[1]), lambda i: (i, column)) for v in lefts
    ]
    out_specs = [pl.BlockSpec((r, tile), lambda i: (0, i)) for r, _ in splits]
    out_shape = [jax.ShapeDtypeStruct((r, width), dtype) for r, dtype in splits]
    if weigh is not None:
        operands.append(weigh)
        specs.append(pl.BlockSpec((rows, tile), lambda i: (first // count, i)))
        out_specs.append(pl.BlockSpec((1, tile), lambda i: (0, i)))
        out_shape.append(jax.ShapeDtypeStruct((1, width), f32))
    if add is not None:
        operands.append(add)
        specs.append(pl.BlockSpec((rows, tile), lambda i: (0, i)))
    operands += before
    specs += [pl.BlockSpec(memory_space=pl.ANY)] * len(before)
    return pl.pallas_call(
        functools.partial(
            product_kernel,
            len(lefts),
            int(weigh is not None),
            int(add is not None),
            len(out_shape),
        ),
        grid=(width // tile,),
        in_specs=specs,
        out_specs=out_specs,
        out_shape=out_shape,
        compiler_params=pltpu.CompilerParams(vmem_limit_bytes=48 * 2**20),
        cost_estimate=cost(2 * rows * width * sum(v.shape[1] for v in lefts), share),
        name="sum_of_products",
    )(*operands)


def body(
    inputs,
    lengths,
    attention_gain,
    query_weight,
    key_matrix,
    value_matrix,
    out_weight,
    query_gain,
    key_gain,
    feedforward_gain,
    gate_weight,
    up_weight,
    down_weight,
    cotangent,
):
    rows, slots, width = inputs.shape
    tokens = rows * slots
    parts = lax.axis_size("ctx")
    heads = QUERY_HEADS_TOTAL // parts
    share = parts // KEY_VALUE_HEADS
    query_cols = heads * HEAD_SIZE
    weight_rows = query_weight.shape[0]
    feed = gate_weight.shape[1] // parts
    all_tokens = parts * tokens
    base = lax.axis_index("ctx").astype(jnp.int32)

    qkv_pack = jnp.concatenate(
        [query_weight.reshape(weight_rows, parts, query_cols)]
        + [
            jnp.repeat(w.reshape(weight_rows, KEY_VALUE_HEADS, HEAD_SIZE), share, axis=1)
            for w in (key_matrix, value_matrix)
        ],
        axis=2,
    )
    qkv_block = spread_columns(qkv_pack)
    out_block = spread_columns(out_weight.reshape(weight_rows, parts, query_cols))
    first_units = feed * 4 // 8 // 128 * 128
    feed_packs = [
        jnp.concatenate(
            [
                w.reshape(weight_rows, parts, feed)[:, :, start:stop]
                for w in (gate_weight, up_weight, down_weight)
            ],
            axis=2,
        )
        for start, stop in ((0, first_units), (first_units, feed))
    ]
    flat = inputs.reshape(tokens, width).astype(f32)
    first_scale = rms_scale(flat)
    normed = flat * first_scale
    hidden_pieces, hidden_start = gather_pieces((normed * attention_gain).astype(bf16))
    hidden = stack(hidden_pieces)
    first_block = spread_columns(after(feed_packs[0], out_block, *hidden_start))
    qkv_full = gather_rows(qkv_block)
    out_full = gather_rows(out_block)
    first_full = gather_rows(first_block)

    raw = jnp.concatenate([dot_nn(piece, qkv_full) for piece in hidden_pieces], axis=0)
    cotangent_flat = cotangent.reshape(tokens, width)
    cotangent_pieces, cotangents_start = gather_pieces(after(cotangent_flat, first_block))
    cotangents = stack(cotangent_pieces)
    raw = after(raw, *cotangents_start).reshape(parts, rows, slots, query_cols + 2 * HEAD_SIZE)
    last_block = spread_columns(after(feed_packs[1], *cotangents_start))
    cosine, sine = [
        t.T for t in rotary_tables(jnp.arange(parts * slots, dtype=jnp.int32), HEAD_SIZE)
    ]
    base_array = base.reshape(1)
    gains = [g.astype(f32).reshape(HEAD_SIZE, 1) for g in (query_gain, key_gain)]
    results = ()
    for row in range(rows):
        if row == rows - 1:
            results = fence(results, last_block, cotangent_pieces[-1]) if results else results
        results = attend(row, results, base_array, lengths, raw, *gains, cosine, sine)
    attended, log_total = results
    attended_rows = attended.reshape(all_tokens, query_cols)
    sums = partial_products(
        functools.partial(sum_of_products, 2.4, [attended_rows], [out_full], 0, tokens), tokens
    )
    mixed = flat + near_step(far_step(sums))

    second_scale = rms_scale(mixed)
    normed_again = mixed * second_scale
    pieces, _ = gather_pieces((normed_again * feedforward_gain).astype(bf16), (cotangents,))
    hidden_again = after(stack(pieces), first_full)
    last_full = gather_rows(last_block)
    fulls = [first_full, last_full]
    inners, grads, partials = [], [], []
    for which in range(2):
        if which == 1:
            fulls[1] = after(last_full, partials[0])
        inner, grad = feed_forward(1.7 * which, hidden_again, cotangents, fulls[which])
        inners.append(inner)
        grads.append(grad)
        partials.append(feed_gradient(1.6 * which, hidden_again, cotangents, grad, inner))
    first_gradient = scatter_rows(partials[0])
    last_gradient = scatter_rows(after(partials[1], first_gradient))
    sums = partial_products(
        functools.partial(sum_of_products, 0, grads, fulls, 0, tokens), tokens
    )
    sums = far_step(sums)
    feed_sums = partial_products(
        functools.partial(sum_of_products, 2.4, inners, fulls, 2, tokens), tokens, tuple(sums[1:])
    )
    feed_arrived = far_hops(feed_sums)
    own, *arrived = near_hops(sums)
    if arrived:
        arrived = fence(arrived, feed_sums[0])
    grad_hidden_again = sum(part.astype(f32) for part in (own, *arrived))
    feedforward_gain_local = jnp.sum(grad_hidden_again * normed_again, axis=0)
    scaled_again = grad_hidden_again * feedforward_gain
    grad_mixed = cotangent_flat.astype(f32) + second_scale * (
        scaled_again - normed_again * jnp.mean(scaled_again * normed_again, axis=-1, keepdims=True)
    )

    pieces, _ = gather_pieces(
        after(grad_mixed.astype(bf16), first_gradient, *feed_arrived)
    )
    grad_branch = stack(pieces)
    attended_gradient = jnp.concatenate(
        [dot_nn(piece, out_full).astype(bf16) for piece in pieces], axis=0
    )
    first_collected = collect_columns(after(first_gradient, attended_gradient))
    feed_parts = near_hops(far_add(feed_sums, feed_arrived, (attended_gradient,)))
    feed_out = sum(part.astype(f32) for part in feed_parts)
    outputs = (mixed + feed_out).astype(bf16).reshape(rows, slots, width)
    grad_queries, grad_keys_values, query_gain_sums, key_gain_sums = attend_back(
        base_array,
        lengths,
        raw,
        *gains,
        cosine,
        sine,
        attended,
        attended_gradient.reshape(parts, rows, slots, query_cols),
        log_total,
    )
    query_gain_local, key_gain_local = query_gain_sums.sum(axis=1), key_gain_sums.sum(axis=1)
    grad_raw = jnp.concatenate(
        [
            grad_queries.reshape(all_tokens, query_cols),
            grad_keys_values.reshape(all_tokens, 2 * HEAD_SIZE),
        ],
        axis=1,
    )
    grad_raw = after(grad_raw, *feed_parts[1:], first_collected)
    attention_partial = jnp.concatenate(
        [dot_tn(hidden, grad_raw), dot_tn(grad_branch, after(attended_rows, grad_raw))], axis=1
    ).astype(bf16)
    attention_gradient = scatter_rows(after(attention_partial, last_gradient))
    attention_collected = collect_columns(attention_gradient)
    query_weight_gradient, key_weight_gradient, value_weight_gradient, out_weight_gradient = (
        place_heads(attention_collected, parts, share)
    )
    weighed_sums = []

    def hidden_product(*arguments):
        *sums, weighed = sum_of_products(
            2.4, [grad_raw], [qkv_full], 0, tokens, *arguments, weigh=hidden
        )
        weighed_sums.append(weighed[0])
        return sums

    sums = partial_products(hidden_product, tokens, (attention_partial,))
    last_collected = collect_columns(last_gradient)
    sums = far_step(sums, (feed_out,), (last_collected,))
    grad_hidden = after(near_step(sums), attention_collected)
    gate_weight_gradient, up_weight_gradient, down_weight_gradient = place_units(
        first_collected, last_collected, parts
    )

    attention_gain_local = sum(weighed_sums) / attention_gain.astype(f32)
    scaled_first = grad_hidden * attention_gain
    input_gradient = (
        grad_mixed
        + first_scale
        * (scaled_first - normed * jnp.mean(scaled_first * normed, axis=-1, keepdims=True))
    ).astype(bf16)
    gain_sums = sum_everywhere(
        after(
            jnp.concatenate(
                [attention_gain_local, feedforward_gain_local, query_gain_local, key_gain_local]
            ),
            *sums[1:],
        )
    )
    attention_gain_gradient, feedforward_gain_gradient = gain_sums[:width], gain_sums[width : 2 * width]
    query_gain_gradient = gain_sums[2 * width : 2 * width + HEAD_SIZE]
    key_gain_gradient = gain_sums[2 * width + HEAD_SIZE :]
    return (
        outputs,
        input_gradient.reshape(rows, slots, width),
        attention_gain_gradient,
        query_weight_gradient,
        key_weight_gradient,
        value_weight_gradient,
        out_weight_gradient,
        query_gain_gradient,
        key_gain_gradient,
        feedforward_gain_gradient,
        gate_weight_gradient,
        up_weight_gradient,
        down_weight_gradient,
    )


def solution(mesh):
    weight = P(("dp", "ctx"), None)
    token = P("dp", "ctx", None)
    placed = (
        token, P("dp"), P(), weight, weight, weight, weight, P(), P(), P(), weight, weight, weight, token,
    )
    returned = (
        token, token, P(), weight, weight, weight, weight, P(), P(), P(), weight, weight, weight,
    )
    return jax.shard_map(
        body, mesh=mesh, in_specs=placed, out_specs=returned, check_vma=False
    )
```

```python
import functools

import jax
import jax.numpy as jnp
from jax import lax
from jax.experimental import pallas as pl
from jax.experimental.pallas import tpu as pltpu
from jax.sharding import PartitionSpec as P

QUERY_HEADS_TOTAL = 32
KEY_VALUE_HEADS = 8
HEAD_SIZE = 64
FACTOR = HEAD_SIZE ** (-0.5)

NO_COST = pl.CostEstimate(flops=0, bytes_accessed=0, transcendentals=0)


def cost(flops, share):
    return pl.CostEstimate(flops=int(flops * share), bytes_accessed=0, transcendentals=0)


epsilon = 1e-06
f32 = jnp.float32
bf16 = jnp.bfloat16


def rms_scale(value_rows):
    return lax.rsqrt(jnp.mean(value_rows * value_rows, axis=-1, keepdims=True) + epsilon)


def rotary_tables(positions, width):
    inverse = 10000.0 ** (-(jnp.arange(width // 2, dtype=f32) * 2.0) / width)
    angle_table = positions.astype(f32)[:, None] * inverse[None, :]
    return (jnp.cos(angle_table), jnp.sin(angle_table))


def dot_nn(left, right):
    return jnp.dot(left, right, preferred_element_type=f32)


def dot_tn(left, right):
    return lax.dot_general(left, right, (((0,), (0,)), ((), ())), preferred_element_type=f32)


def dot_nt(left, right):
    return lax.dot_general(left, right, (((1,), (1,)), ((), ())), preferred_element_type=f32)


def fence(values, *earlier):
    count = len(values)
    anywhere = pl.BlockSpec(memory_space=pl.ANY)
    return pl.pallas_call(
        lambda *refs: None,
        in_specs=[anywhere] * (count + len(earlier)),
        out_specs=[anywhere] * count,
        out_shape=[jax.ShapeDtypeStruct(v.shape, v.dtype) for v in values],
        input_output_aliases={i: i for i in range(count)},
        cost_estimate=NO_COST,
        name="fence",
    )(*values, *earlier)


def after(value, *earlier):
    return fence((value,), *earlier)[0]


def stack_kernel(*refs):
    for k, ref in enumerate(refs[:-1]):

        @pl.when(pl.program_id(0) == k)
        def _():
            refs[-1][...] = ref[...]


def stack(pieces):
    if len(pieces) == 1:
        return pieces[0]
    shape = pieces[0].shape
    return pl.pallas_call(
        stack_kernel,
        grid=(len(pieces),),
        in_specs=[pl.BlockSpec(shape, lambda i: (0, 0))] * len(pieces),
        out_specs=pl.BlockSpec(shape, lambda i: (i, 0)),
        out_shape=jax.ShapeDtypeStruct((len(pieces) * shape[0], shape[1]), pieces[0].dtype),
        compiler_params=pltpu.CompilerParams(vmem_limit_bytes=32 * 2**20),
        cost_estimate=NO_COST,
        name="stack",
    )(*pieces)


RELATIVE = (0, 2, 4, 6, 1, 3, 5, 7)


def place_of(own, index, parts):
    if parts != 8:
        return index
    relative = lax.bitwise_xor(own, index)
    return lax.bitwise_or(
        lax.shift_right_logical(relative, 1), lax.shift_left(lax.bitwise_and(relative, 1), 2)
    )


def hop(value, bit):
    return lax.ppermute(value, "ctx", [(i, i ^ bit) for i in range(lax.axis_size("ctx"))])


def halves_kernel(by_x_ref, by_y_ref, *refs):
    refs[-2][...] = by_x_ref[...]
    refs[-1][...] = by_y_ref[...]


def halves(by_x, by_y, before):
    rows, width = by_x.shape
    half = (rows // 2, width)
    return pl.pallas_call(
        halves_kernel,
        grid=(1,),
        in_specs=[pl.BlockSpec(half, lambda i: (0, 0)), pl.BlockSpec(half, lambda i: (1, 0))]
        + [pl.BlockSpec(memory_space=pl.ANY)] * len(before),
        out_specs=[pl.BlockSpec(half, lambda i: (0, 0))] * 2,
        out_shape=[jax.ShapeDtypeStruct(half, by_x.dtype)] * 2,
        cost_estimate=cost(10**9, 1),
        name="halves",
    )(by_x, by_y, *before)


def gather_pieces(value, middle=()):
    if lax.axis_size("ctx") != 8:
        whole = lax.all_gather(value, "ctx", axis=0, tiled=True)
        return (whole,), (whole,)
    by_x, by_y = hop(value, 2), hop(value, 4)
    first, second = halves(by_x, by_y, middle)
    far = stack((hop(first, 4), hop(second, 2)))
    others = [hop(piece, 1) for piece in (value, by_x, by_y)]
    return (value, by_x, by_y, far, *others, hop(far, 1)), (by_x, by_y)


def partial_products(product, tokens, before=()):
    parts = lax.axis_size("ctx")
    if parts != 8:
        return product(0, parts, [(parts * tokens, bf16)], None, before)
    half = (tokens // 2, bf16)
    near_other, far_other = product(4, 4, [(3 * tokens, bf16), (tokens, bf16)], None, before)
    far_other = hop(far_other, 1)
    near_other = after(near_other, far_other)
    far = product(3, 1, [half] * 2, far_other, ())
    own, *near = product(
        0, 3, [(tokens, f32)] + [(tokens, bf16)] * 2, hop(near_other, 1), (far[0],)
    )
    return (own, *near, *far)


def far_hops(sums, far_after=()):
    if lax.axis_size("ctx") != 8:
        return ()
    far_first, far_last = sums[3:]
    if far_after:
        far_first, far_last = fence((far_first, far_last), *far_after)
    return hop(far_first, 2), hop(far_last, 4)


def far_add(sums, arrived, near_after=()):
    if lax.axis_size("ctx") != 8:
        return fence(sums, *near_after) if near_after else sums
    own, by_x, by_y = sums[:3]
    if near_after:
        by_x, by_y = fence((by_x, by_y), *near_after)
    from_x, from_y = arrived
    rows = by_x.shape[0] // 2
    by_x = by_x + jnp.pad(from_y, ((rows, 0), (0, 0)))
    by_y = by_y + jnp.pad(from_x, ((0, rows), (0, 0)))
    return own, by_x, by_y


def far_step(sums, far_after=(), near_after=()):
    return far_add(sums, far_hops(sums, far_after), near_after)


def near_hops(sums):
    if lax.axis_size("ctx") != 8:
        (whole,) = sums
        return (lax.psum_scatter(whole, "ctx", scatter_dimension=0, tiled=True),)
    own, by_x, by_y = sums
    return own, hop(by_x, 2), hop(by_y, 4)


def near_step(sums):
    return sum(part.astype(f32) for part in near_hops(sums))


def sum_everywhere(value):
    if lax.axis_size("ctx") != 8 or lax.axis_size("dp") != 4:
        return lax.psum(value, ("dp", "ctx"))
    value = value + hop(value, 1)
    value = value + (hop(value, 2) + hop(value, 4) + hop(value, 6))
    shifted = [
        lax.ppermute(value, "dp", [(i, i ^ bits) for i in range(4)]) for bits in (1, 2, 3)
    ]
    return (value + shifted[0]) + (shifted[1] + shifted[2])


def spread_columns(packed):
    rows, parts, columns = packed.shape
    return lax.all_to_all(
        packed.reshape(rows, parts * columns), "ctx", split_axis=1, concat_axis=0, tiled=True
    )


def gather_rows(block):
    return lax.all_gather(block, "dp", axis=0, tiled=True)


def scatter_rows(gradient):
    return lax.psum_scatter(gradient, "dp", scatter_dimension=0, tiled=True)


def collect_columns(block):
    return lax.all_to_all(block, "ctx", split_axis=0, concat_axis=0, tiled=True)


def place_units_kernel(first_ref, last_ref, *out_refs):
    for which, out_ref in enumerate(out_refs):
        start = 0
        for ref in (first_ref, last_ref):
            units = ref.shape[1] // 3
            out_ref[:, start : start + units] = ref[
                :, which * units : (which + 1) * units
            ].astype(f32)
            start += units


def place_units(first, last, parts):
    rows = first.shape[0] // parts
    units = (first.shape[1] + last.shape[1]) // 3
    return pl.pallas_call(
        place_units_kernel,
        grid=(parts,),
        in_specs=[pl.BlockSpec((rows, v.shape[1]), lambda i: (i, 0)) for v in (first, last)],
        out_specs=[pl.BlockSpec((rows, units), lambda i: (0, i))] * 3,
        out_shape=[jax.ShapeDtypeStruct((rows, units * parts), f32)] * 3,
        compiler_params=pltpu.CompilerParams(vmem_limit_bytes=16 * 2**20),
        cost_estimate=cost(10**7, 800),
        name="place_units",
    )(first, last)


def place_heads_kernel(parts, share, block_ref, query_ref, key_ref, value_ref, out_ref):
    rows = query_ref.shape[0]
    width = query_ref.shape[1] // parts
    for part in range(parts):
        block = block_ref[part * rows : (part + 1) * rows, :].astype(f32)
        here = slice(part * width, (part + 1) * width)
        query_ref[:, here] = block[:, :width]
        out_ref[:, here] = block[:, width + 2 * HEAD_SIZE :]
        head = part // share
        for ref, start in ((key_ref, width), (value_ref, width + HEAD_SIZE)):
            columns = slice(head * HEAD_SIZE, (head + 1) * HEAD_SIZE)
            piece = block[:, start : start + HEAD_SIZE]
            ref[:, columns] = piece if part % share == 0 else ref[:, columns] + piece


def place_heads(block, parts, share):
    rows = block.shape[0] // parts
    width = (block.shape[1] - 2 * HEAD_SIZE) // 2 * parts
    whole = pl.BlockSpec(memory_space=pltpu.VMEM)
    shapes = [(rows, width), (rows, parts // share * HEAD_SIZE)]
    shapes += [shapes[1], shapes[0]]
    return pl.pallas_call(
        functools.partial(place_heads_kernel, parts, share),
        in_specs=[whole],
        out_specs=[whole] * 4,
        out_shape=[jax.ShapeDtypeStruct(shape, f32) for shape in shapes],
        compiler_params=pltpu.CompilerParams(vmem_limit_bytes=16 * 2**20),
        cost_estimate=cost(10**7, 400),
        name="place_heads",
    )(block)


def heads_to_columns(block, heads):
    return jnp.concatenate(
        [block[:, h * HEAD_SIZE : (h + 1) * HEAD_SIZE].T for h in range(heads)], axis=1
    )


def columns_to_heads(columns, heads, slots):
    return jnp.concatenate(
        [columns[:, h * slots : (h + 1) * slots].T for h in range(heads)], axis=1
    )


def columns_to_rows(columns, heads, slots):
    return jnp.concatenate(
        [columns[:, h * slots : (h + 1) * slots].T for h in range(heads)], axis=0
    )


def head_scale(raw):
    return lax.rsqrt(jnp.mean(raw * raw, axis=0, keepdims=True) + epsilon)


def prepare(raw, gain, cosine, sine):
    value = raw * head_scale(raw) * gain
    first, second = value[: HEAD_SIZE // 2], value[HEAD_SIZE // 2 :]
    return jnp.concatenate(
        [first * cosine - second * sine, second * cosine + first * sine], axis=0
    )


def prepare_back(gradient, raw, gain, cosine, sine):
    scale = head_scale(raw)
    unit = raw * scale
    first, second = gradient[: HEAD_SIZE // 2], gradient[HEAD_SIZE // 2 :]
    turned = jnp.concatenate(
        [first * cosine + second * sine, second * cosine - first * sine], axis=0
    )
    inside = turned * gain
    middle = jnp.mean(inside * unit, axis=0, keepdims=True)
    return scale * (inside - unit * middle), turned * unit


def fold(values):
    lanes = 128
    return sum(values[:, i : i + lanes] for i in range(0, values.shape[1], lanes))


def repeated(table, heads):
    return jnp.concatenate([table] * heads, axis=1)


def masked_scores(key_block, query_columns, start, query_block, slots, length):
    scores = dot_nn(key_block, query_columns)
    key_pos = start + lax.broadcasted_iota(jnp.int32, scores.shape, 0)
    query_pos = query_block * slots + lax.rem(
        lax.broadcasted_iota(jnp.int32, scores.shape, 1), slots
    )
    return jnp.where((key_pos <= query_pos) & (key_pos < length), scores, -1e30)


def chunks_needed(query_block, slots, length, chunk):
    return lax.div(
        jnp.minimum((query_block + 1) * slots, length) + (chunk - 1), jnp.int32(chunk)
    )


def attend_kernel(
    row, blocks, slots, heads, chunk,
    base_ref, len_ref, q_ref, kv_ref, qg_ref, kg_ref, cos_ref, sin_ref,
    *refs,
):
    o_ref, lse_ref, k_all, v_t = refs[-4:]
    query_block = pl.program_id(0)
    base, length = base_ref[0], len_ref[row]

    @pl.when(query_block == 0)
    def _():
        for j in range(blocks):
            at = place_of(base, jnp.int32(j), blocks)
            here = slice(j * slots, (j + 1) * slots)
            both = kv_ref[at, 0].T
            keys = prepare(both[:HEAD_SIZE], kg_ref[...], cos_ref[:, here], sin_ref[:, here])
            k_all[here, :] = keys.T.astype(bf16)
            v_t[:, here] = both[HEAD_SIZE:].astype(bf16)

    count = chunks_needed(query_block, slots, length, chunk)
    here = pl.ds(pl.multiple_of(query_block * slots, slots), slots)
    queries = prepare(
        heads_to_columns(q_ref[0, 0], heads),
        qg_ref[...],
        repeated(cos_ref[:, here], heads),
        repeated(sin_ref[:, here], heads),
    )
    queries = queries.astype(bf16) * FACTOR
    columns = heads * slots

    def step(j, carry):
        top, total, accum = carry
        start = pl.multiple_of(j * chunk, chunk)
        scores = masked_scores(
            k_all[pl.ds(start, chunk), :], queries, start, query_block, slots, length
        )
        new_top = jnp.maximum(top, jnp.max(scores, axis=0, keepdims=True))
        probs = jnp.exp(scores - new_top)
        alpha = jnp.exp(top - new_top)
        total = total * alpha + jnp.sum(probs, axis=0, keepdims=True)
        accum = accum * alpha + dot_nn(v_t[:, pl.ds(start, chunk)], probs.astype(bf16))
        return new_top, total, accum

    top, total, accum = lax.fori_loop(
        0,
        count,
        step,
        (
            jnp.full((1, columns), -1e30, f32),
            jnp.zeros((1, columns), f32),
            jnp.zeros((HEAD_SIZE, columns), f32),
        ),
    )
    o_ref[0, 0] = columns_to_heads(accum / total, heads, slots).astype(bf16)
    lse_ref[0, 0] = top + jnp.log(total)


def attend_back_kernel(
    blocks, slots, heads, chunk,
    base_ref, len_ref, q_ref, kv_ref, qg_ref, kg_ref, cos_ref, sin_ref, o_ref, do_ref, lse_ref,
    dq_ref, dkv_ref, dqg_ref, dkg_ref, k_all, v_all, k_t, dk_all, dv_all,
):
    row, query_block = pl.program_id(0), pl.program_id(1)
    base, length = base_ref[0], len_ref[row]

    @pl.when((row == 0) & (query_block == 0))
    def _():
        dqg_ref[...] = jnp.zeros_like(dqg_ref)
        dkg_ref[...] = jnp.zeros_like(dkg_ref)

    @pl.when(query_block == 0)
    def _():
        for j in range(blocks):
            at = place_of(base, jnp.int32(j), blocks)
            here = slice(j * slots, (j + 1) * slots)
            both = kv_ref[at, 0]
            keys = prepare(both.T[:HEAD_SIZE], kg_ref[...], cos_ref[:, here], sin_ref[:, here])
            k_t[:, here] = keys.astype(bf16)
            k_all[here, :] = keys.T.astype(bf16)
            v_all[here, :] = both[:, HEAD_SIZE:].astype(bf16)
        dk_all[...] = jnp.zeros_like(dk_all)
        dv_all[...] = jnp.zeros_like(dv_all)

    count = chunks_needed(query_block, slots, length, chunk)
    here = pl.ds(pl.multiple_of(query_block * slots, slots), slots)
    cosine, sine = repeated(cos_ref[:, here], heads), repeated(sin_ref[:, here], heads)
    raw = heads_to_columns(q_ref[0, 0], heads)
    queries = prepare(raw, qg_ref[...], cosine, sine).astype(bf16) * FACTOR
    query_rows = columns_to_rows(queries.astype(f32), heads, slots).astype(bf16)
    gradient = heads_to_columns(do_ref[0, 0].astype(f32), heads)
    grad_rows = columns_to_rows(gradient, heads, slots).astype(bf16)
    delta = jnp.sum(
        gradient * heads_to_columns(o_ref[0, 0].astype(f32), heads), axis=0, keepdims=True
    )
    gradient = gradient.astype(bf16)
    log_total = lse_ref[0, 0]

    def step(j, dq_t):
        start = pl.multiple_of(j * chunk, chunk)
        at = pl.ds(start, chunk)
        scores = masked_scores(k_all[at, :], queries, start, query_block, slots, length)
        probs = jnp.exp(scores - log_total)
        grad_probs = dot_nn(v_all[at, :], gradient)
        grad_scores = (probs * (grad_probs - delta)).astype(bf16)
        dv_all[at, :] += dot_nn(probs.astype(bf16), grad_rows)
        dk_all[at, :] += dot_nn(grad_scores, query_rows)
        return dq_t + dot_nn(k_t[:, at], grad_scores)

    dq_t = lax.fori_loop(0, count, step, jnp.zeros((HEAD_SIZE, heads * slots), f32))
    raw_term, gain_term = prepare_back(dq_t * FACTOR, raw, qg_ref[...], cosine, sine)
    dq_ref[0, 0] = columns_to_heads(raw_term, heads, slots).astype(bf16)
    dqg_ref[...] += fold(gain_term)

    @pl.when(query_block == blocks - 1)
    def _():
        for j in range(blocks):
            at = place_of(base, jnp.int32(j), blocks)
            here = slice(j * slots, (j + 1) * slots)
            raw_term, gain_term = prepare_back(
                dk_all[here, :].T,
                kv_ref[at, 0].T[:HEAD_SIZE],
                kg_ref[...],
                cos_ref[:, here],
                sin_ref[:, here],
            )
            dkg_ref[...] += fold(gain_term)
            dkv_ref[at, 0] = jnp.concatenate([raw_term.T, dv_all[here, :]], axis=1).astype(bf16)


def attention_specs(row, blocks, slots, width, total):
    def place(*grid):
        (i, base, _), r = (grid, row) if row is not None else (grid[1:], grid[0])
        return place_of(base[0], i, blocks), r, 0, 0

    row_of = lambda *grid: grid[0] if row is None else row
    constant = lambda *grid: (0, 0)
    both = 2 * HEAD_SIZE
    return (
        pl.BlockSpec((1, 1, slots, width), place),
        pl.BlockSpec((blocks, 1, slots, both), lambda *g: (0, row_of(*g), 0, width // both)),
        pl.BlockSpec((blocks, 1, slots, both), lambda *g: (0, row_of(*g), 0, 0)),
        pl.BlockSpec((HEAD_SIZE, 1), constant),
        pl.BlockSpec((HEAD_SIZE // 2, total), constant),
        pl.BlockSpec((1, 1, 1, width // HEAD_SIZE * slots), place),
        pl.BlockSpec((HEAD_SIZE, 128), constant),
    )


def attend(row, previous, base, lengths, raw, query_gain, key_gain, cosine, sine):
    blocks, rows, slots, columns = raw.shape
    width = columns - 2 * HEAD_SIZE
    heads = width // HEAD_SIZE
    total = blocks * slots
    query_spec, raw_key_spec, _, gain_spec, table_spec, lse_spec, _ = attention_specs(
        row, blocks, slots, width, total
    )
    operands = (base, lengths, raw, raw, query_gain, key_gain, cosine, sine)
    return pl.pallas_call(
        functools.partial(attend_kernel, row, blocks, slots, heads, 2 * slots),
        grid_spec=pltpu.PrefetchScalarGridSpec(
            num_scalar_prefetch=2,
            grid=(blocks,),
            in_specs=[query_spec, raw_key_spec, gain_spec, gain_spec, table_spec, table_spec]
            + [pl.BlockSpec(memory_space=pl.ANY)] * len(previous),
            out_specs=[query_spec, lse_spec],
            scratch_shapes=[
                pltpu.VMEM((total, HEAD_SIZE), bf16),
                pltpu.VMEM((HEAD_SIZE, total), bf16),
            ],
        ),
        out_shape=[
            jax.ShapeDtypeStruct((blocks, rows, slots, width), bf16),
            jax.ShapeDtypeStruct((blocks, rows, 1, heads * slots), f32),
        ],
        input_output_aliases={len(operands) + i: i for i in range(len(previous))},
        compiler_params=pltpu.CompilerParams(vmem_limit_bytes=32 * 2**20),
        cost_estimate=cost(2 * HEAD_SIZE * heads * total * total, 24),
        name="attend",
    )(*operands, *previous)


def attend_back(
    base, lengths, raw, query_gain, key_gain, cosine, sine, attended, gradient, log_total
):
    blocks, rows, slots, columns = raw.shape
    width = columns - 2 * HEAD_SIZE
    heads = width // HEAD_SIZE
    total = blocks * slots
    query_spec, raw_key_spec, key_spec, gain_spec, table_spec, lse_spec, sum_spec = (
        attention_specs(None, blocks, slots, width, total)
    )
    operands = (base, lengths, raw, raw, query_gain, key_gain, cosine, sine)
    operands += (attended, gradient, log_total)
    return pl.pallas_call(
        functools.partial(attend_back_kernel, blocks, slots, heads, 2 * slots),
        grid_spec=pltpu.PrefetchScalarGridSpec(
            num_scalar_prefetch=2,
            grid=(rows, blocks),
            in_specs=[query_spec, raw_key_spec, gain_spec, gain_spec, table_spec, table_spec]
            + [query_spec, query_spec, lse_spec],
            out_specs=[query_spec, key_spec, sum_spec, sum_spec],
            scratch_shapes=[
                pltpu.VMEM((total, HEAD_SIZE), bf16),
                pltpu.VMEM((total, HEAD_SIZE), bf16),
                pltpu.VMEM((HEAD_SIZE, total), bf16),
                pltpu.VMEM((total, HEAD_SIZE), f32),
                pltpu.VMEM((total, HEAD_SIZE), f32),
            ],
        ),
        out_shape=[
            jax.ShapeDtypeStruct((blocks, rows, slots, width), bf16),
            jax.ShapeDtypeStruct((blocks, rows, slots, 2 * HEAD_SIZE), bf16),
            jax.ShapeDtypeStruct((HEAD_SIZE, 128), f32),
            jax.ShapeDtypeStruct((HEAD_SIZE, 128), f32),
        ],
        compiler_params=pltpu.CompilerParams(vmem_limit_bytes=32 * 2**20),
        cost_estimate=cost(5 * HEAD_SIZE * rows * heads * total * total, 16),
        name="attend_back",
    )(*operands)


def feed_kernel(hidden_ref, cotangent_ref, weight_ref, inner_ref, grad_ref):
    units = inner_ref.shape[1]
    hidden = hidden_ref[...]
    gate = dot_nn(hidden, weight_ref[:, :units])
    upward = dot_nn(hidden, weight_ref[:, units : 2 * units])
    grad_inner = dot_nn(cotangent_ref[...], weight_ref[:, 2 * units :])
    sigmoid_gate = jax.nn.sigmoid(gate)
    silu_gate = gate * sigmoid_gate
    inner_ref[...] = (silu_gate * upward).astype(bf16)
    grad_ref[:, :units] = (
        grad_inner * upward * sigmoid_gate * (1.0 + gate * (1.0 - sigmoid_gate))
    ).astype(bf16)
    grad_ref[:, units:] = (grad_inner * silu_gate).astype(bf16)


def feed_forward(share, hidden, cotangents, weights):
    count, width = hidden.shape
    units = weights.shape[1] // 3
    tile = 512
    rows = pl.BlockSpec((tile, width), lambda i: (i, 0))
    return pl.pallas_call(
        feed_kernel,
        grid=(count // tile,),
        in_specs=[rows, rows, pl.BlockSpec(weights.shape, lambda i: (0, 0))],
        out_specs=[
            pl.BlockSpec((tile, units), lambda i: (i, 0)),
            pl.BlockSpec((tile, 2 * units), lambda i: (i, 0)),
        ],
        out_shape=[
            jax.ShapeDtypeStruct((count, units), bf16),
            jax.ShapeDtypeStruct((count, 2 * units), bf16),
        ],
        compiler_params=pltpu.CompilerParams(vmem_limit_bytes=48 * 2**20),
        cost_estimate=cost(6 * count * width * units, share),
        name="feed_forward",
    )(hidden, cotangents, weights)


def feed_gradient_kernel(hidden_ref, cotangent_ref, grad_ref, inner_ref, out_ref):
    split = grad_ref.shape[1]
    out_ref[:, :split] = dot_tn(hidden_ref[...], grad_ref[...]).astype(bf16)
    out_ref[:, split:] = dot_tn(cotangent_ref[...], inner_ref[...]).astype(bf16)


def feed_gradient(share, hidden, cotangents, grad, inner):
    count, width = hidden.shape
    tile = 512
    columns = pl.BlockSpec((count, tile), lambda i: (0, i))
    total = grad.shape[1] + inner.shape[1]
    return pl.pallas_call(
        feed_gradient_kernel,
        grid=(width // tile,),
        in_specs=[columns, columns]
        + [pl.BlockSpec(v.shape, lambda i: (0, 0)) for v in (grad, inner)],
        out_specs=pl.BlockSpec((tile, total), lambda i: (i, 0)),
        out_shape=jax.ShapeDtypeStruct((width, total), bf16),
        compiler_params=pltpu.CompilerParams(vmem_limit_bytes=48 * 2**20),
        cost_estimate=cost(2 * count * width * total, share),
        name="feed_gradient",
    )(hidden, cotangents, grad, inner)


def product_kernel(count, weighed, adds, outs, *refs):
    rows, weights, rest = refs[:count], refs[count : 2 * count], refs[2 * count :]
    out_refs = rest[-outs:]
    total = sum(dot_nt(r[...], w[...]) for r, w in zip(rows, weights))
    if weighed:
        *out_refs, sum_ref = out_refs
        sum_ref[...] = jnp.sum(total * rest[0][...].astype(f32), axis=0, keepdims=True)
    if adds:
        total += rest[weighed][...].astype(f32)
    start = 0
    for out_ref in out_refs:
        out_ref[...] = total[start : start + out_ref.shape[0]].astype(out_ref.dtype)
        start += out_ref.shape[0]


def sum_of_products(
    share, lefts, weights, column, tokens, first, count, splits, add, before, weigh=None
):
    rows = count * tokens
    width = weights[0].shape[0]
    tile = 512
    operands = list(lefts) + list(weights)
    specs = [pl.BlockSpec((rows, v.shape[1]), lambda i: (first // count, 0)) for v in lefts] + [
        pl.BlockSpec((tile, v.shape[1]), lambda i: (i, column)) for v in lefts
    ]
    out_specs = [pl.BlockSpec((r, tile), lambda i: (0, i)) for r, _ in splits]
    out_shape = [jax.ShapeDtypeStruct((r, width), dtype) for r, dtype in splits]
    if weigh is not None:
        operands.append(weigh)
        specs.append(pl.BlockSpec((rows, tile), lambda i: (first // count, i)))
        out_specs.append(pl.BlockSpec((1, tile), lambda i: (0, i)))
        out_shape.append(jax.ShapeDtypeStruct((1, width), f32))
    if add is not None:
        operands.append(add)
        specs.append(pl.BlockSpec((rows, tile), lambda i: (0, i)))
    operands += before
    specs += [pl.BlockSpec(memory_space=pl.ANY)] * len(before)
    return pl.pallas_call(
        functools.partial(
            product_kernel,
            len(lefts),
            int(weigh is not None),
            int(add is not None),
            len(out_shape),
        ),
        grid=(width // tile,),
        in_specs=specs,
        out_specs=out_specs,
        out_shape=out_shape,
        compiler_params=pltpu.CompilerParams(vmem_limit_bytes=48 * 2**20),
        cost_estimate=cost(2 * rows * width * sum(v.shape[1] for v in lefts), share),
        name="sum_of_products",
    )(*operands)


def body(
    inputs,
    lengths,
    attention_gain,
    query_weight,
    key_matrix,
    value_matrix,
    out_weight,
    query_gain,
    key_gain,
    feedforward_gain,
    gate_weight,
    up_weight,
    down_weight,
    cotangent,
):
    rows, slots, width = inputs.shape
    tokens = rows * slots
    parts = lax.axis_size("ctx")
    heads = QUERY_HEADS_TOTAL // parts
    share = parts // KEY_VALUE_HEADS
    query_cols = heads * HEAD_SIZE
    weight_rows = query_weight.shape[0]
    feed = gate_weight.shape[1] // parts
    all_tokens = parts * tokens
    base = lax.axis_index("ctx").astype(jnp.int32)

    qkv_pack = jnp.concatenate(
        [query_weight.reshape(weight_rows, parts, query_cols)]
        + [
            jnp.repeat(w.reshape(weight_rows, KEY_VALUE_HEADS, HEAD_SIZE), share, axis=1)
            for w in (key_matrix, value_matrix)
        ],
        axis=2,
    )
    qkv_block = spread_columns(qkv_pack)
    out_block = spread_columns(out_weight.reshape(weight_rows, parts, query_cols))
    first_units = feed * 4 // 8 // 128 * 128
    feed_packs = [
        jnp.concatenate(
            [
                w.reshape(weight_rows, parts, feed)[:, :, start:stop]
                for w in (gate_weight, up_weight, down_weight)
            ],
            axis=2,
        )
        for start, stop in ((0, first_units), (first_units, feed))
    ]
    flat = inputs.reshape(tokens, width).astype(f32)
    first_scale = rms_scale(flat)
    normed = flat * first_scale
    hidden_pieces, hidden_start = gather_pieces((normed * attention_gain).astype(bf16))
    hidden = stack(hidden_pieces)
    first_block = spread_columns(after(feed_packs[0], out_block, *hidden_start))
    qkv_full = gather_rows(qkv_block)
    out_full = gather_rows(out_block)
    first_full = gather_rows(first_block)

    raw = jnp.concatenate([dot_nn(piece, qkv_full) for piece in hidden_pieces], axis=0)
    cotangent_flat = cotangent.reshape(tokens, width)
    cotangent_pieces, cotangents_start = gather_pieces(after(cotangent_flat, first_block))
    cotangents = stack(cotangent_pieces)
    raw = after(raw, *cotangents_start).reshape(parts, rows, slots, query_cols + 2 * HEAD_SIZE)
    last_block = spread_columns(after(feed_packs[1], *cotangents_start))
    cosine, sine = [
        t.T for t in rotary_tables(jnp.arange(parts * slots, dtype=jnp.int32), HEAD_SIZE)
    ]
    base_array = base.reshape(1)
    gains = [g.astype(f32).reshape(HEAD_SIZE, 1) for g in (query_gain, key_gain)]
    results = ()
    for row in range(rows):
        if row == rows - 1:
            results = fence(results, last_block, cotangent_pieces[-1]) if results else results
        results = attend(row, results, base_array, lengths, raw, *gains, cosine, sine)
    attended, log_total = results
    attended_rows = attended.reshape(all_tokens, query_cols)
    sums = partial_products(
        functools.partial(sum_of_products, 2.4, [attended_rows], [out_full], 0, tokens), tokens
    )
    mixed = flat + near_step(far_step(sums))

    second_scale = rms_scale(mixed)
    normed_again = mixed * second_scale
    pieces, _ = gather_pieces((normed_again * feedforward_gain).astype(bf16), (cotangents,))
    hidden_again = after(stack(pieces), first_full)
    last_full = gather_rows(last_block)
    fulls = [first_full, last_full]
    inners, grads, partials = [], [], []
    for which in range(2):
        if which == 1:
            fulls[1] = after(last_full, partials[0])
        inner, grad = feed_forward(1.7 * which, hidden_again, cotangents, fulls[which])
        inners.append(inner)
        grads.append(grad)
        partials.append(feed_gradient(1.6 * which, hidden_again, cotangents, grad, inner))
    first_gradient = scatter_rows(partials[0])
    last_gradient = scatter_rows(after(partials[1], first_gradient))
    sums = partial_products(
        functools.partial(sum_of_products, 0, grads, fulls, 0, tokens), tokens
    )
    sums = far_step(sums)
    feed_sums = partial_products(
        functools.partial(sum_of_products, 1.2, inners, fulls, 2, tokens), tokens, tuple(sums[1:])
    )
    feed_arrived = far_hops(feed_sums)
    own, *arrived = near_hops(sums)
    if arrived:
        arrived = fence(arrived, feed_sums[0])
    grad_hidden_again = sum(part.astype(f32) for part in (own, *arrived))
    feedforward_gain_local = jnp.sum(grad_hidden_again * normed_again, axis=0)
    scaled_again = grad_hidden_again * feedforward_gain
    grad_mixed = cotangent_flat.astype(f32) + second_scale * (
        scaled_again - normed_again * jnp.mean(scaled_again * normed_again, axis=-1, keepdims=True)
    )

    pieces, _ = gather_pieces(
        after(grad_mixed.astype(bf16), first_gradient, *feed_arrived)
    )
    grad_branch = stack(pieces)
    attended_gradient = jnp.concatenate(
        [dot_nn(piece, out_full).astype(bf16) for piece in pieces], axis=0
    )
    first_collected = collect_columns(after(first_gradient, attended_gradient))
    feed_parts = near_hops(far_add(feed_sums, feed_arrived, (attended_gradient,)))
    feed_out = sum(part.astype(f32) for part in feed_parts)
    outputs = (mixed + feed_out).astype(bf16).reshape(rows, slots, width)
    grad_queries, grad_keys_values, query_gain_sums, key_gain_sums = attend_back(
        base_array,
        lengths,
        raw,
        *gains,
        cosine,
        sine,
        attended,
        attended_gradient.reshape(parts, rows, slots, query_cols),
        log_total,
    )
    query_gain_local, key_gain_local = query_gain_sums.sum(axis=1), key_gain_sums.sum(axis=1)
    grad_raw = jnp.concatenate(
        [
            grad_queries.reshape(all_tokens, query_cols),
            grad_keys_values.reshape(all_tokens, 2 * HEAD_SIZE),
        ],
        axis=1,
    )
    grad_raw = after(grad_raw, *feed_parts[1:], first_collected)
    attention_partial = jnp.concatenate(
        [dot_tn(hidden, grad_raw), dot_tn(grad_branch, after(attended_rows, grad_raw))], axis=1
    ).astype(bf16)
    attention_gradient = scatter_rows(after(attention_partial, last_gradient))
    attention_collected = collect_columns(attention_gradient)
    query_weight_gradient, key_weight_gradient, value_weight_gradient, out_weight_gradient = (
        place_heads(attention_collected, parts, share)
    )
    weighed_sums = []

    def hidden_product(*arguments):
        *sums, weighed = sum_of_products(
            2.4, [grad_raw], [qkv_full], 0, tokens, *arguments, weigh=hidden
        )
        weighed_sums.append(weighed[0])
        return sums

    sums = partial_products(hidden_product, tokens, (attention_partial,))
    last_collected = collect_columns(last_gradient)
    sums = far_step(sums, (feed_out,), (last_collected,))
    grad_hidden = after(near_step(sums), attention_collected)
    gate_weight_gradient, up_weight_gradient, down_weight_gradient = place_units(
        first_collected, last_collected, parts
    )

    attention_gain_local = sum(weighed_sums) / attention_gain.astype(f32)
    scaled_first = grad_hidden * attention_gain
    input_gradient = (
        grad_mixed
        + first_scale
        * (scaled_first - normed * jnp.mean(scaled_first * normed, axis=-1, keepdims=True))
    ).astype(bf16)
    gain_sums = sum_everywhere(
        after(
            jnp.concatenate(
                [attention_gain_local, feedforward_gain_local, query_gain_local, key_gain_local]
            ),
            *sums[1:],
        )
    )
    attention_gain_gradient, feedforward_gain_gradient = gain_sums[:width], gain_sums[width : 2 * width]
    query_gain_gradient = gain_sums[2 * width : 2 * width + HEAD_SIZE]
    key_gain_gradient = gain_sums[2 * width + HEAD_SIZE :]
    return (
        outputs,
        input_gradient.reshape(rows, slots, width),
        attention_gain_gradient,
        query_weight_gradient,
        key_weight_gradient,
        value_weight_gradient,
        out_weight_gradient,
        query_gain_gradient,
        key_gain_gradient,
        feedforward_gain_gradient,
        gate_weight_gradient,
        up_weight_gradient,
        down_weight_gradient,
    )


def solution(mesh):
    weight = P(("dp", "ctx"), None)
    token = P("dp", "ctx", None)
    placed = (
        token, P("dp"), P(), weight, weight, weight, weight, P(), P(), P(), weight, weight, weight, token,
    )
    returned = (
        token, token, P(), weight, weight, weight, weight, P(), P(), P(), weight, weight, weight,
    )
    return jax.shard_map(
        body, mesh=mesh, in_specs=placed, out_specs=returned, check_vma=False
    )
```
